128 devices in a mesh: tm: 4 (over y_lo, core), tile: 32 (over y_hi, z, x).
Axes of the slice: x: 4, y: 4 (y_hi: 2, y_lo: 2; y = y_hi * 2 + y_lo), z: 4, core: 2. Of those that a mesh axis runs over, the one named last changes fastest.
Arguments:
- latent_grad: bfloat16 [32, 160, 4096], P(None, 'tile', 'tm'), may hold values from -6 to 6
- section_input: bfloat16 [32, 160, 256, 512], P('tm', None, 'tile'), may hold values from -6 to 6
- kernel: bfloat16 [512, 432], replicated, may hold values from -0.3125 to 0.3125
Outputs:
- input_grad: bfloat16 [32, 160, 256, 512], P('tm', None, 'tile')
- kernel_grad: float32 [512, 432], P('tile')
The draws below stay inside these ranges and needn't reach their ends.
All inputs are finite; a program needn't handle non-finite values.
Results may differ from the reference program's by a relative error of at most 0.0029.
Values may be sent and summed in bfloat16 or wider, within the bound.
A program may use at most 128 MiB of HBM per device.

```python
import math
import jax
import jax.numpy as jnp
from jax import lax

CIN = 512
COUT = 16
TL = 32
H = 160
W = 256


def block_scale(own_key, extent, split, least, top_value):
    loudness, own = 1.0, jax.random.fold_in(own_key, 6)
    for position, parts in split:
        steps = jnp.exp(jax.random.uniform(jax.random.fold_in(own, position), (parts,), jnp.float32, least / len(split), top_value / len(split)))
        loudness = loudness * jnp.repeat(steps, extent[position] // parts).reshape([-1 if axis == position else 1 for axis in range(len(extent))])
    return loudness


def noise(stream_key, shape, deviation, limit, split=(), kind=jnp.bfloat16):
    result = deviation * jax.random.normal(stream_key, shape, jnp.float32)
    if split:
        result = result * block_scale(stream_key, shape, split, -0.22, 0.18)
    return jnp.clip(result, -limit, limit).astype(kind)


def setup_inputs(seed: int = 0) -> dict:
    keys = jax.random.split(jax.random.key(seed), 4)
    return {
        "latent_grad": noise(keys[0], (TL, H, W * COUT), 1.0, 6.0, ((1, 32), (2, 4))),
        "section_input": noise(keys[1], (TL, H, W, CIN), 1.5, 6.0, ((0, 4), (2, 32))),
        "kernel": noise(keys[2], (CIN, 27 * COUT), (27 * COUT) ** -0.5, 0.3125),
    }


def silu_slope(values):
    sigmoid_value = jax.nn.sigmoid(values)
    return sigmoid_value * (1.0 + values * (1.0 - sigmoid_value))

def reference(latent_grad, section_input, kernel):
    grad_field = latent_grad.reshape(TL, H, W, COUT)
    padded = jnp.pad(grad_field, ((0, 2), (1, 1), (1, 1), (0, 0)))
    zero_index = jnp.zeros((), jnp.int32)

    def frame_step(running_sum, frame_index):
        frame_index = frame_index.astype(jnp.int32)
        tap_list = []
        for step_time in range(3):
            for step_row in range(3):
                for step_col in range(3):
                    starts = ((frame_index + step_time).astype(jnp.int32), (zero_index + (2 - step_row)).astype(jnp.int32), (zero_index + (2 - step_col)).astype(jnp.int32), zero_index)
                    window = lax.dynamic_slice(padded, starts, (1, H, W, COUT))
                    tap_list.append(window[0])
        columns = jnp.stack(tap_list, axis=2).reshape(H * W, 27 * COUT)
        frame_input = lax.dynamic_index_in_dim(section_input, frame_index, 0, keepdims=False)
        frame_input = frame_input.reshape(H * W, CIN).astype(jnp.float32)
        activation = jax.nn.silu(frame_input).astype(jnp.bfloat16)
        input_part = lax.dot_general(columns, kernel, (((1,), (1,)), ((), ())), preferred_element_type=jnp.float32)
        frame_grad = (input_part * silu_slope(frame_input)).astype(jnp.bfloat16).reshape(H, W, CIN)
        running_sum = running_sum + lax.dot_general(activation, columns, (((0,), (0,)), ((), ())), preferred_element_type=jnp.float32)
        return (running_sum, frame_grad)
    running_sum, input_grad = lax.scan(frame_step, jnp.zeros((CIN, 27 * COUT), jnp.float32), jnp.arange(TL, dtype=jnp.int32))
    kernel_grad = running_sum * (1.0 / math.sqrt(TL * H * W))
    return (input_grad, kernel_grad)
```

```python
import functools
import math

import jax
import jax.numpy as jnp
from jax import lax
from jax.experimental import pallas as pl
from jax.experimental.pallas import tpu as pltpu
from jax.sharding import PartitionSpec as P

MESH = pl.DeviceIdType.MESH
F32, BF16 = jnp.float32, jnp.bfloat16
LANES = 128
OUT = 16
STRIP = 8
FRAMES = 8
ROWS = 5
SLOTS = 16


def lane_of(shape, axis):
    return lax.broadcasted_iota(jnp.int32, shape, axis)


def frames_aside(rows, shift):
    turned = rows.reshape(ROWS * FRAMES, LANES)
    if shift:
        turned = pltpu.roll(turned, shift, 1)
    turned = pltpu.roll(turned, 0, 1, stride=OUT, stride_axis=0).reshape(ROWS, FRAMES, LANES)
    return jnp.sum(turned, axis=1, keepdims=True)


def halo_pack(left, right, left_after, right_after):
    return [
        frames_aside(left, 0),
        frames_aside(right, OUT),
        frames_aside(left_after, 0) + frames_aside(right_after, 3 * OUT),
    ]


def exchange(n_tm, n_tile, grad_ref, recv_ref, edge_ref, msg, emsg, sems):
    tm, tile = lax.axis_index("tm"), lax.axis_index("tile")
    strips = n_tile // n_tm
    block = tile // strips
    place = lax.rem(tile, strips)
    from_left = jnp.logical_and(place == 0, block > 0)
    from_right = jnp.logical_and(place == strips - 1, block < n_tm - 1)
    has_edge = jnp.logical_or(from_left, from_right)
    edge_block = jnp.where(place == 0, block - 1, block + 1)
    count = n_tm * strips
    send_main, send_edge, recv_main, recv_edge = (sems.at[i] for i in range(4))

    def is_me(target_tm, target_tile):
        return jnp.logical_and(target_tm == tm, target_tile == tile)

    barrier = pltpu.get_barrier_semaphore()

    def greet(band, _):
        @pl.when(jnp.logical_not(is_me(block, band)))
        def _():
            pl.semaphore_signal(barrier, inc=1, device_id=(block, band), device_id_type=MESH)

        @pl.when(jnp.logical_and(has_edge, jnp.logical_not(is_me(edge_block, band))))
        def _():
            pl.semaphore_signal(barrier, inc=1, device_id=(edge_block, band), device_id_type=MESH)

        return 0

    lax.fori_loop(0, n_tile, greet, 0)

    def backwards():
        r, c = lane_of((LANES, LANES), 0), lane_of((LANES, LANES), 1)
        same = jnp.logical_and(r // OUT + c // OUT == STRIP - 1, lax.rem(r, OUT) == lax.rem(c, OUT))
        return jnp.where(same, 1.0, 0.0).astype(BF16)

    flip = backwards()
    lane = lane_of((1, 1, LANES), 2)
    row = lane_of((1, FRAMES, 1), 1)
    left_lanes, right_lanes = lane < OUT, lane >= LANES - OUT
    emsg[...] = jnp.zeros(emsg.shape, BF16)
    nothing = jnp.zeros((ROWS, FRAMES, LANES), F32)
    flipped = []
    for t in range(n_tm):
        rows = grad_ref[:, t].astype(F32).reshape(ROWS * FRAMES, strips * LANES).astype(BF16)
        flipped.append([
            jnp.dot(rows[:, s * LANES : (s + 1) * LANES], flip, preferred_element_type=F32)
            .reshape(ROWS, FRAMES, LANES)
            for s in range(strips)
        ])
    for t in range(n_tm):
        here = flipped[t]
        after = [jnp.where(row < 2, v, 0.0) for v in flipped[t + 1]] if t + 1 < n_tm else [nothing] * strips
        for s in range(strips):
            halo = []
            for part in (here, after):
                halo.append(jnp.where(left_lanes, part[s - 1], 0.0) if s > 0 else nothing)
                halo.append(jnp.where(right_lanes, part[s + 1], 0.0) if s + 1 < strips else nothing)
            tail = [after[s][:, 0:2]] + halo_pack(*halo) + [jnp.zeros((ROWS, 3, LANES), F32)]
            msg[t, s] = jnp.concatenate([here[s]] + tail, axis=1).astype(BF16)
        for side in range(2):
            if side == 0:
                halo = [jnp.where(left_lanes, part[strips - 1], 0.0) for part in (here, after)]
                packed = halo_pack(halo[0], nothing, halo[1], nothing)
            else:
                halo = [jnp.where(right_lanes, part[0], 0.0) for part in (here, after)]
                packed = halo_pack(nothing, halo[0], nothing, halo[1])
            packed = jnp.concatenate(packed, axis=1)
            pieces = [packed[i] for i in range(ROWS)] + [jnp.zeros((SLOTS - 3 * ROWS, LANES), F32)]
            emsg[side, t] = jnp.concatenate(pieces, axis=0).astype(BF16)

    self_main = (block == tm).astype(jnp.int32)
    to_right, to_left = tm < n_tm - 1, tm > 0
    right_tile, left_tile = (tm + 1) * strips, tm * strips - 1
    self_edge = (
        jnp.logical_and(to_right, tile == right_tile).astype(jnp.int32)
        + jnp.logical_and(to_left, tile == left_tile).astype(jnp.int32)
    )
    edges_out = n_tm * (to_right.astype(jnp.int32) + to_left.astype(jnp.int32))
    pl.semaphore_wait(barrier, count - self_main + edges_out - self_edge)

    def send(source, target, send_sem, recv_sem, target_tm, target_tile):
        own = is_me(target_tm, target_tile)

        @pl.when(jnp.logical_not(own))
        def _():
            pltpu.make_async_remote_copy(
                src_ref=source, dst_ref=target, send_sem=send_sem, recv_sem=recv_sem,
                device_id=(target_tm, target_tile), device_id_type=MESH,
            ).start()

        @pl.when(own)
        def _():
            pltpu.make_async_copy(source, target, recv_sem).start()

    def send_one(k, _):
        turn = lax.rem(k + tile, count)
        t, s = turn // strips, lax.rem(turn, strips)
        send(msg.at[t, s], recv_ref.at[tile], send_main, recv_main, t, tm * strips + s)
        return 0

    def send_edges(t, _):
        @pl.when(to_right)
        def _():
            send(emsg.at[0, t], edge_ref.at[tile], send_edge, recv_edge, t, right_tile)

        @pl.when(to_left)
        def _():
            send(emsg.at[1, t], edge_ref.at[tile], send_edge, recv_edge, t, left_tile)

        return 0

    lax.fori_loop(0, n_tm, send_edges, 0)
    lax.fori_loop(0, count, send_one, 0)

    @pl.when(jnp.logical_not(has_edge))
    def _():
        edge_ref[...] = jnp.zeros(edge_ref.shape, BF16)

    @pl.when(has_edge)
    def _():
        pltpu.make_async_copy(edge_ref, edge_ref, recv_edge).wait()

    pltpu.make_async_copy(recv_ref, recv_ref, recv_main).wait()

    def drain(k, _):
        pltpu.make_async_copy(msg.at[0, 0], msg.at[0, 0], send_main).wait()
        return 0

    lax.fori_loop(0, count - self_main, drain, 0)

    def drain_edge(k, _):
        pltpu.make_async_copy(emsg.at[0, 0], emsg.at[0, 0], send_edge).wait()
        return 0

    lax.fori_loop(0, edges_out - self_edge, drain_edge, 0)


def compute(
    recv_ref, edge_ref, x_ref, kernel_ref, out_ref, part_ref,
    xbuf, act, slope, field, packed, halo, vee, cols, cols_t, last, last_t, weights, acc, total,
    in_sem, out_sem,
):
    ring, height, width, cin = xbuf.shape
    frames = act.shape[0]
    wide = frames + 2
    count = height * width
    bands = recv_ref.shape[0]

    def fetch(t):
        slot = lax.rem(t, ring)
        return pltpu.make_async_copy(x_ref.at[t], xbuf.at[slot], in_sem.at[slot])

    for t in range(ring):
        fetch(t).start()

    weights[...] = jnp.zeros(weights.shape, BF16)
    for kt in range(3):
        taps = kernel_ref[9 * kt * OUT : 9 * (kt + 1) * OUT, :]
        taps = (0.5 * taps.astype(F32)).astype(BF16)
        weights[kt * LANES : (kt + 1) * LANES, :] = taps[:LANES]
        weights[3 * LANES + kt * OUT : 3 * LANES + (kt + 1) * OUT, :] = taps[LANES:]

    step = 8

    def silu_frame(t, _):
        fetch(t).wait()
        slot = lax.rem(t, ring)

        def silu_rows(r, _):
            half = 0.5 * xbuf[slot, pl.ds(r * step, step)].astype(F32).reshape(step * width, cin)
            u = jnp.tanh(half)
            turned = half * u
            place = pl.ds(pl.multiple_of(r * step * width, step * width), step * width)
            act[t, place, :] = (half + turned).astype(BF16)
            slope[t, place, :] = (1.0 + u) * ((1.0 + half) - turned)
            return 0

        lax.fori_loop(0, height // step, silu_rows, 0)

        @pl.when(t + ring < frames)
        def _():
            fetch(t + ring).start()

        return 0

    lax.fori_loop(0, frames, silu_frame, 0)

    def unpack(b, _):
        rows = recv_ref[b].astype(F32)
        edge = edge_ref[b].astype(F32)
        field[pl.ds(b * ROWS, ROWS)] = rows
        for i in range(ROWS):
            for k in range(3):
                packed[k, pl.ds(b * ROWS + i, 1), :] = rows[i, 10 + k : 11 + k, :] + edge[3 * i + k : 3 * i + k + 1, :]
        return 0

    lax.fori_loop(0, bands, unpack, 0)
    r, c = lane_of((3 * LANES, LANES), 0), lane_of((3 * LANES, LANES), 1)
    side, block, channel = r // LANES, lax.rem(r, LANES) // OUT, lax.rem(r, OUT)
    left = jnp.concatenate([packed[k] for k in range(3)], axis=1).astype(BF16)
    for t in range(wide):
        if t < frames:
            from_left = jnp.logical_and(side == 0, block == t)
            from_right = jnp.logical_and(side == 1, block == t)
        else:
            from_left = jnp.logical_and(side == 2, block == t - frames)
            from_right = jnp.logical_and(side == 2, block == t - frames + 2)
        spread = jnp.logical_or(
            jnp.logical_and(from_left, c == channel),
            jnp.logical_and(from_right, c == channel + LANES - OUT),
        )
        halo[t] = jnp.dot(left, jnp.where(spread, 1.0, 0.0).astype(BF16), preferred_element_type=F32)

    lane3, col3 = lane_of((1, width, LANES), 2), lane_of((1, width, LANES), 1)
    outside = jnp.logical_or(
        jnp.logical_and(col3 == 0, lane3 < OUT),
        jnp.logical_and(col3 == width - 1, lane3 >= LANES - OUT),
    )
    edge_rows = jnp.zeros((width, LANES), F32)
    group = 16
    for t in range(wide):
        vee[t, 0:width, :] = edge_rows
        vee[t, (height + 1) * width : (height + 2) * width, :] = edge_rows

        def spread(g, _, t=t):
            rows = pl.ds(g * group, group)
            main = jnp.broadcast_to(field[rows, t : t + 1, :], (group, width, LANES))
            side = jnp.broadcast_to(halo[t, rows][:, None, :], (group, width, LANES))
            place = pl.ds(pl.multiple_of((g * group + 1) * width, width), group * width)
            rows = jnp.where(outside, side, main).reshape(group * width, LANES)
            vee[t, place, :] = pltpu.roll(rows, 0, 1, stride=OUT, stride_axis=0)
            return 0

        lax.fori_loop(0, height // group, spread, 0)

    lane2 = lane_of((1, LANES), 1)

    def turn(t, g, shift_rows, shift):
        place = pl.ds(pl.multiple_of((g * group + shift_rows) * width, width), group * width)
        return pltpu.roll(vee[t, place, :], shift, 1) if shift else vee[t, place, :]

    def fill(t, _):
        def fill_rows(g, _):
            place = pl.ds(pl.multiple_of(g * group * width, group * width), group * width)
            s0 = turn(t, g, 2, 2 * OUT)
            s1 = turn(t, g, 1, 5 * OUT)
            s2 = turn(t, g, 0, 0)
            block = jnp.where(lane2 < 3 * OUT, s0, jnp.where(lane2 < 6 * OUT, s1, s2)).astype(BF16)
            cols[t, place, :] = block
            return 0

        lax.fori_loop(0, height // group, fill_rows, 0)
        cols_t[pl.ds(pl.multiple_of(t * LANES, LANES), LANES), :] = jnp.transpose(cols[t])
        return 0

    lax.fori_loop(0, wide, fill, 0)

    def fill_last(t, _):
        def fill_rows(g, _):
            place = pl.ds(pl.multiple_of(g * group * width, group * width), group * width)
            taps = [turn(t + kt, g, 0, kt * OUT) for kt in range(3)]
            block = jnp.where(
                lane2 < OUT, taps[0],
                jnp.where(lane2 < 2 * OUT, taps[1], jnp.where(lane2 < 3 * OUT, taps[2], 0.0)),
            )
            last[t, place, :] = block.astype(BF16)
            return 0

        lax.fori_loop(0, height // group, fill_rows, 0)
        last_t[t] = jnp.transpose(last[t])[0 : 3 * OUT]
        return 0

    lax.fori_loop(0, frames, fill_last, 0)

    acc[...] = jnp.zeros(acc.shape, F32)

    def add_frame(t, _):
        left = jnp.concatenate(
            [cols_t[pl.ds(pl.multiple_of(t * LANES, LANES), 3 * LANES), :], last_t[t]], axis=0
        )
        acc[...] += jnp.dot(left, act[t], preferred_element_type=F32)
        return 0

    lax.fori_loop(0, frames, add_frame, 0)
    total[27 * OUT :, :] = jnp.zeros((total.shape[0] - 27 * OUT, cin), F32)
    for kt in range(3):
        total[9 * kt * OUT : 9 * kt * OUT + LANES, :] = acc[kt * LANES : (kt + 1) * LANES, :]
        total[9 * kt * OUT + LANES : 9 * (kt + 1) * OUT, :] = acc[3 * LANES + kt * OUT : 3 * LANES + (kt + 1) * OUT, :]
    part_ref[...] = jnp.transpose(total[...])[:, : 27 * OUT]

    chunk = 40

    def put(t):
        slot = lax.rem(t, ring)
        return pltpu.make_async_copy(xbuf.at[slot], out_ref.at[t], out_sem.at[slot])

    def grad_frame(t, _):
        slot = lax.rem(t, ring)

        @pl.when(t >= ring)
        def _():
            put(t - ring).wait()

        def grad_rows(r, _):
            place = pl.ds(pl.multiple_of(r * chunk * width, chunk * width), chunk * width)
            left = jnp.concatenate([cols[t + kt, place, :] for kt in range(3)] + [last[t, place, :]], axis=1)
            grad = jnp.dot(left, weights[...], preferred_element_type=F32) * slope[t, place, :]
            xbuf[slot, pl.ds(r * chunk, chunk)] = grad.reshape(chunk, width, cin).astype(BF16)
            return 0

        lax.fori_loop(0, height // chunk, grad_rows, 0)
        put(t).start()
        return 0

    lax.fori_loop(0, frames, grad_frame, 0)
    for t in range(frames - ring, frames):
        put(t).wait()


def reduce_kernel(
    n_tm, n_tile, scale, part_ref, out_ref, half, mine, pieces, sums, quads, sems, recv_sems
):
    tm, tile = lax.axis_index("tm"), lax.axis_index("tile")
    cores = 2
    core, y_lo = lax.rem(tm, cores), tm // cores
    groups = n_tile // cores
    y_hi, spot = tile // groups, lax.rem(tile, groups)
    rows = mine.shape[0]
    share = rows // groups

    barrier = pltpu.get_barrier_semaphore()
    partner = (tm - core) + (1 - core)
    pl.semaphore_signal(barrier, inc=1, device_id=(partner, tile), device_id_type=MESH)
    source_tm = y_lo * cores + y_hi

    def greet(k, _):
        source_tile = core * groups + k

        @pl.when(jnp.logical_not(jnp.logical_and(source_tm == tm, source_tile == tile)))
        def _():
            pl.semaphore_signal(
                barrier, inc=1, device_id=(source_tm, source_tile), device_id_type=MESH
            )

        return 0

    lax.fori_loop(0, groups, greet, 0)
    for k in range(1, n_tm):
        pl.semaphore_signal(
            barrier, inc=1, device_id=(lax.rem(tm + k, n_tm), tile), device_id_type=MESH
        )
    self_one = (core == y_hi).astype(jnp.int32)
    pl.semaphore_wait(barrier, 1 + groups - self_one + n_tm - 1)

    swap = pltpu.make_async_remote_copy(
        src_ref=part_ref.at[pl.ds(pl.multiple_of((1 - core) * rows, rows), rows)], dst_ref=half,
        send_sem=sems.at[0], recv_sem=sems.at[1],
        device_id=(partner, tile), device_id_type=MESH,
    )
    swap.start()
    swap.wait()
    own = part_ref[pl.ds(pl.multiple_of(core * rows, rows), rows), :] + half[...]
    mine[...] = own

    dest_tm = y_lo * cores + y_hi

    def piece(k):
        return mine.at[pl.ds(pl.multiple_of(k * share, share), share)]

    def send_piece(k, _):
        g = lax.rem(k + spot, groups)
        dest_tile = core * groups + g
        own_one = jnp.logical_and(dest_tm == tm, dest_tile == tile)

        @pl.when(jnp.logical_not(own_one))
        def _():
            pltpu.make_async_remote_copy(
                src_ref=piece(g), dst_ref=pieces.at[spot], send_sem=sems.at[2], recv_sem=recv_sems.at[0],
                device_id=(dest_tm, dest_tile), device_id_type=MESH,
            ).start()

        @pl.when(own_one)
        def _():
            pltpu.make_async_copy(piece(g), pieces.at[spot], recv_sems.at[0]).start()

        return 0

    lax.fori_loop(0, groups, send_piece, 0)
    pltpu.make_async_copy(pieces, pieces, recv_sems.at[0]).wait()

    def drain(k, _):
        pltpu.make_async_copy(pieces.at[0], pieces.at[0], sems.at[2]).wait()
        return 0

    lax.fori_loop(0, groups - self_one, drain, 0)
    sums[...] = jnp.sum(pieces[...], axis=0)

    copies = []
    for k in range(1, n_tm):
        copies.append(
            pltpu.make_async_remote_copy(
                src_ref=sums, dst_ref=quads.at[tm], send_sem=sems.at[3 + k], recv_sem=recv_sems.at[k],
                device_id=(lax.rem(tm + k, n_tm), tile), device_id_type=MESH,
            )
        )
        copies[-1].start()
    quads[tm] = sums[...]
    for copy in copies:
        copy.wait()
    whole = quads[0]
    for k in range(1, n_tm):
        whole = whole + quads[k]
    out_ref[...] = whole * scale


def on_device(n_tm, n_tile, scale, latent_grad, section_input, kernel):
    frames, height, width, cin = section_input.shape
    taps = kernel.shape[1]
    strips = n_tile // n_tm
    banded = jnp.transpose(latent_grad, (1, 0, 2)).reshape(ROWS, n_tm, FRAMES, strips * LANES)
    vmem = pl.BlockSpec(memory_space=pltpu.VMEM)
    anywhere = pl.BlockSpec(memory_space=pl.ANY)
    recv, edge = pl.pallas_call(
        functools.partial(exchange, n_tm, n_tile),
        out_shape=(
            jax.ShapeDtypeStruct((n_tile, ROWS, SLOTS, LANES), BF16),
            jax.ShapeDtypeStruct((n_tile, SLOTS, LANES), BF16),
        ),
        in_specs=[vmem],
        out_specs=(vmem, vmem),
        scratch_shapes=[
            pltpu.VMEM((n_tm, strips, ROWS, SLOTS, LANES), BF16),
            pltpu.VMEM((2, n_tm, SLOTS, LANES), BF16),
            pltpu.SemaphoreType.DMA((4,)),
        ],
        compiler_params=pltpu.CompilerParams(collective_id=0, has_side_effects=True),
    )(banded)
    wide, count = frames + 2, height * width
    kernel_t = jnp.transpose(kernel)
    input_grad, part = pl.pallas_call(
        compute,
        out_shape=(
            jax.ShapeDtypeStruct((frames, height, width, cin), BF16),
            jax.ShapeDtypeStruct((cin, taps), F32),
        ),
        in_specs=[vmem, vmem, anywhere, vmem],
        out_specs=(anywhere, vmem),
        scratch_shapes=[
            pltpu.VMEM((frames // 2, height, width, cin), BF16),
            pltpu.VMEM((frames, count, cin), BF16),
            pltpu.VMEM((frames, count, cin), F32),
            pltpu.VMEM((height, SLOTS, LANES), F32),
            pltpu.VMEM((3, height, LANES), F32),
            pltpu.VMEM((wide, height, LANES), F32),
            pltpu.VMEM((wide, (height + 2) * width, LANES), F32),
            pltpu.VMEM((wide, count, LANES), BF16),
            pltpu.VMEM((wide * LANES, count), BF16),
            pltpu.VMEM((frames, count, LANES), BF16),
            pltpu.VMEM((frames, 3 * OUT, count), BF16),
            pltpu.VMEM((4 * LANES, cin), BF16),
            pltpu.VMEM((27 * OUT, cin), F32),
            pltpu.VMEM((4 * LANES, cin), F32),
            pltpu.SemaphoreType.DMA((frames // 2,)),
            pltpu.SemaphoreType.DMA((frames // 2,)),
        ],
        compiler_params=pltpu.CompilerParams(vmem_limit_bytes=62 << 20),
    )(recv, edge, section_input, kernel_t)
    cores = 2
    rows = cin // cores
    share = cin // n_tile
    kernel_grad = pl.pallas_call(
        functools.partial(reduce_kernel, n_tm, n_tile, scale),
        out_shape=jax.ShapeDtypeStruct((share, taps), F32),
        in_specs=[vmem],
        out_specs=vmem,
        scratch_shapes=[
            pltpu.VMEM((rows, taps), F32),
            pltpu.VMEM((rows, taps), F32),
            pltpu.VMEM((n_tile // cores, share, taps), F32),
            pltpu.VMEM((share, taps), F32),
            pltpu.VMEM((n_tm, share, taps), F32),
            pltpu.SemaphoreType.DMA((3 + n_tm,)),
            pltpu.SemaphoreType.DMA((n_tm,)),
        ],
        compiler_params=pltpu.CompilerParams(collective_id=1, has_side_effects=True),
    )(part)
    return input_grad, kernel_grad


def solution(mesh):
    n_tm, n_tile = mesh.shape["tm"], mesh.shape["tile"]
    positions = n_tm * FRAMES * n_tile * ROWS * n_tile * STRIP
    return jax.shard_map(
        functools.partial(on_device, n_tm, n_tile, 1.0 / math.sqrt(positions)),
        mesh=mesh,
        in_specs=(P(None, "tile", "tm"), P("tm", None, "tile", None), P()),
        out_specs=(P("tm", None, "tile", None), P("tile", None)),
        check_vma=False,
    )
```

```python
import functools
import math

import jax
import jax.numpy as jnp
from jax import lax
from jax.experimental import pallas as pl
from jax.experimental.pallas import tpu as pltpu
from jax.sharding import PartitionSpec as P

MESH = pl.DeviceIdType.MESH
F32, BF16 = jnp.float32, jnp.bfloat16
LANES = 128
OUT = 16
STRIP = 8
FRAMES = 8
ROWS = 5
SLOTS = 16


def lane_of(shape, axis):
    return lax.broadcasted_iota(jnp.int32, shape, axis)


def frames_aside(rows, shift):
    turned = rows.reshape(ROWS * FRAMES, LANES)
    if shift:
        turned = pltpu.roll(turned, shift, 1)
    turned = pltpu.roll(turned, 0, 1, stride=OUT, stride_axis=0).reshape(ROWS, FRAMES, LANES)
    return jnp.sum(turned, axis=1, keepdims=True)


def halo_pack(left, right, left_after, right_after):
    return [
        frames_aside(left, 0),
        frames_aside(right, OUT),
        frames_aside(left_after, 0) + frames_aside(right_after, 3 * OUT),
    ]


def exchange(n_tm, n_tile, grad_ref, recv_ref, edge_ref, msg, emsg, sems):
    tm, tile = lax.axis_index("tm"), lax.axis_index("tile")
    strips = n_tile // n_tm
    block = tile // strips
    place = lax.rem(tile, strips)
    from_left = jnp.logical_and(place == 0, block > 0)
    from_right = jnp.logical_and(place == strips - 1, block < n_tm - 1)
    has_edge = jnp.logical_or(from_left, from_right)
    edge_block = jnp.where(place == 0, block - 1, block + 1)
    count = n_tm * strips
    send_main, send_edge, recv_main, recv_edge = (sems.at[i] for i in range(4))

    def is_me(target_tm, target_tile):
        return jnp.logical_and(target_tm == tm, target_tile == tile)

    barrier = pltpu.get_barrier_semaphore()

    def greet(band, _):
        @pl.when(jnp.logical_not(is_me(block, band)))
        def _():
            pl.semaphore_signal(barrier, inc=1, device_id=(block, band), device_id_type=MESH)

        @pl.when(jnp.logical_and(has_edge, jnp.logical_not(is_me(edge_block, band))))
        def _():
            pl.semaphore_signal(barrier, inc=1, device_id=(edge_block, band), device_id_type=MESH)

        return 0

    lax.fori_loop(0, n_tile, greet, 0)

    def backwards():
        r, c = lane_of((LANES, LANES), 0), lane_of((LANES, LANES), 1)
        same = jnp.logical_and(r // OUT + c // OUT == STRIP - 1, lax.rem(r, OUT) == lax.rem(c, OUT))
        return jnp.where(same, 1.0, 0.0).astype(BF16)

    flip = backwards()
    lane = lane_of((1, 1, LANES), 2)
    row = lane_of((1, FRAMES, 1), 1)
    left_lanes, right_lanes = lane < OUT, lane >= LANES - OUT
    emsg[...] = jnp.zeros(emsg.shape, BF16)
    nothing = jnp.zeros((ROWS, FRAMES, LANES), F32)
    flipped = []
    for t in range(n_tm):
        rows = grad_ref[:, t].astype(F32).reshape(ROWS * FRAMES, strips * LANES).astype(BF16)
        flipped.append([
            jnp.dot(rows[:, s * LANES : (s + 1) * LANES], flip, preferred_element_type=F32)
            .reshape(ROWS, FRAMES, LANES)
            for s in range(strips)
        ])
    for t in range(n_tm):
        here = flipped[t]
        after = [jnp.where(row < 2, v, 0.0) for v in flipped[t + 1]] if t + 1 < n_tm else [nothing] * strips
        for s in range(strips):
            halo = []
            for part in (here, after):
                halo.append(jnp.where(left_lanes, part[s - 1], 0.0) if s > 0 else nothing)
                halo.append(jnp.where(right_lanes, part[s + 1], 0.0) if s + 1 < strips else nothing)
            tail = [after[s][:, 0:2]] + halo_pack(*halo) + [jnp.zeros((ROWS, 3, LANES), F32)]
            msg[t, s] = jnp.concatenate([here[s]] + tail, axis=1).astype(BF16)
        for side in range(2):
            if side == 0:
                halo = [jnp.where(left_lanes, part[strips - 1], 0.0) for part in (here, after)]
                packed = halo_pack(halo[0], nothing, halo[1], nothing)
            else:
                halo = [jnp.where(right_lanes, part[0], 0.0) for part in (here, after)]
                packed = halo_pack(nothing, halo[0], nothing, halo[1])
            packed = jnp.concatenate(packed, axis=1)
            pieces = [packed[i] for i in range(ROWS)] + [jnp.zeros((SLOTS - 3 * ROWS, LANES), F32)]
            emsg[side, t] = jnp.concatenate(pieces, axis=0).astype(BF16)

    self_main = (block == tm).astype(jnp.int32)
    to_right, to_left = tm < n_tm - 1, tm > 0
    right_tile, left_tile = (tm + 1) * strips, tm * strips - 1
    self_edge = (
        jnp.logical_and(to_right, tile == right_tile).astype(jnp.int32)
        + jnp.logical_and(to_left, tile == left_tile).astype(jnp.int32)
    )
    edges_out = n_tm * (to_right.astype(jnp.int32) + to_left.astype(jnp.int32))
    pl.semaphore_wait(barrier, count - self_main + edges_out - self_edge)

    def send(source, target, send_sem, recv_sem, target_tm, target_tile):
        own = is_me(target_tm, target_tile)

        @pl.when(jnp.logical_not(own))
        def _():
            pltpu.make_async_remote_copy(
                src_ref=source, dst_ref=target, send_sem=send_sem, recv_sem=recv_sem,
                device_id=(target_tm, target_tile), device_id_type=MESH,
            ).start()

        @pl.when(own)
        def _():
            pltpu.make_async_copy(source, target, recv_sem).start()

    def send_one(k, _):
        turn = lax.rem(k + tile, count)
        t, s = turn // strips, lax.rem(turn, strips)
        send(msg.at[t, s], recv_ref.at[tile], send_main, recv_main, t, tm * strips + s)
        return 0

    def send_edges(t, _):
        @pl.when(to_right)
        def _():
            send(emsg.at[0, t], edge_ref.at[tile], send_edge, recv_edge, t, right_tile)

        @pl.when(to_left)
        def _():
            send(emsg.at[1, t], edge_ref.at[tile], send_edge, recv_edge, t, left_tile)

        return 0

    lax.fori_loop(0, n_tm, send_edges, 0)
    lax.fori_loop(0, count, send_one, 0)

    @pl.when(jnp.logical_not(has_edge))
    def _():
        edge_ref[...] = jnp.zeros(edge_ref.shape, BF16)

    @pl.when(has_edge)
    def _():
        pltpu.make_async_copy(edge_ref, edge_ref, recv_edge).wait()

    pltpu.make_async_copy(recv_ref, recv_ref, recv_main).wait()

    def drain(k, _):
        pltpu.make_async_copy(msg.at[0, 0], msg.at[0, 0], send_main).wait()
        return 0

    lax.fori_loop(0, count - self_main, drain, 0)

    def drain_edge(k, _):
        pltpu.make_async_copy(emsg.at[0, 0], emsg.at[0, 0], send_edge).wait()
        return 0

    lax.fori_loop(0, edges_out - self_edge, drain_edge, 0)


def compute(
    recv_ref, edge_ref, x_ref, kernel_ref, out_ref, part_ref,
    xbuf, act, slope, field, packed, halo, vee, cols, cols_t, last, last_t, weights, acc, total,
    in_sem, out_sem,
):
    ring, height, width, cin = xbuf.shape
    frames = act.shape[0]
    wide = frames + 2
    count = height * width
    bands = recv_ref.shape[0]

    def fetch(t):
        slot = lax.rem(t, ring)
        return pltpu.make_async_copy(x_ref.at[t], xbuf.at[slot], in_sem.at[slot])

    for t in range(ring):
        fetch(t).start()

    weights[...] = jnp.zeros(weights.shape, BF16)
    for kt in range(3):
        taps = kernel_ref[9 * kt * OUT : 9 * (kt + 1) * OUT, :]
        taps = (0.5 * taps.astype(F32)).astype(BF16)
        weights[kt * LANES : (kt + 1) * LANES, :] = taps[:LANES]
        weights[3 * LANES + kt * OUT : 3 * LANES + (kt + 1) * OUT, :] = taps[LANES:]

    step = 8

    def silu_frame(t, _):
        fetch(t).wait()
        slot = lax.rem(t, ring)

        def silu_rows(r, _):
            half = 0.5 * xbuf[slot, pl.ds(r * step, step)].astype(F32).reshape(step * width, cin)
            u = jnp.tanh(half)
            turned = half * u
            place = pl.ds(pl.multiple_of(r * step * width, step * width), step * width)
            act[t, place, :] = (half + turned).astype(BF16)
            slope[t, place, :] = (1.0 + u) * ((1.0 + half) - turned)
            return 0

        lax.fori_loop(0, height // step, silu_rows, 0, unroll=4)

        @pl.when(t + ring < frames)
        def _():
            fetch(t + ring).start()

        return 0

    lax.fori_loop(0, frames, silu_frame, 0)

    def unpack(b, _):
        rows = recv_ref[b].astype(F32)
        edge = edge_ref[b].astype(F32)
        field[pl.ds(b * ROWS, ROWS)] = rows
        for i in range(ROWS):
            for k in range(3):
                packed[k, pl.ds(b * ROWS + i, 1), :] = rows[i, 10 + k : 11 + k, :] + edge[3 * i + k : 3 * i + k + 1, :]
        return 0

    lax.fori_loop(0, bands, unpack, 0, unroll=4)
    r, c = lane_of((3 * LANES, LANES), 0), lane_of((3 * LANES, LANES), 1)
    side, block, channel = r // LANES, lax.rem(r, LANES) // OUT, lax.rem(r, OUT)
    left = jnp.concatenate([packed[k] for k in range(3)], axis=1).astype(BF16)
    for t in range(wide):
        if t < frames:
            from_left = jnp.logical_and(side == 0, block == t)
            from_right = jnp.logical_and(side == 1, block == t)
        else:
            from_left = jnp.logical_and(side == 2, block == t - frames)
            from_right = jnp.logical_and(side == 2, block == t - frames + 2)
        spread = jnp.logical_or(
            jnp.logical_and(from_left, c == channel),
            jnp.logical_and(from_right, c == channel + LANES - OUT),
        )
        halo[t] = jnp.dot(left, jnp.where(spread, 1.0, 0.0).astype(BF16), preferred_element_type=F32)

    lane3, col3 = lane_of((1, width, LANES), 2), lane_of((1, width, LANES), 1)
    outside = jnp.logical_or(
        jnp.logical_and(col3 == 0, lane3 < OUT),
        jnp.logical_and(col3 == width - 1, lane3 >= LANES - OUT),
    )
    edge_rows = jnp.zeros((width, LANES), F32)
    group = 16
    for t in range(wide):
        vee[t, 0:width, :] = edge_rows
        vee[t, (height + 1) * width : (height + 2) * width, :] = edge_rows

        def spread(g, _, t=t):
            rows = pl.ds(g * group, group)
            main = jnp.broadcast_to(field[rows, t : t + 1, :], (group, width, LANES))
            side = jnp.broadcast_to(halo[t, rows][:, None, :], (group, width, LANES))
            place = pl.ds(pl.multiple_of((g * group + 1) * width, width), group * width)
            rows = jnp.where(outside, side, main).reshape(group * width, LANES)
            vee[t, place, :] = pltpu.roll(rows, 0, 1, stride=OUT, stride_axis=0)
            return 0

        lax.fori_loop(0, height // group, spread, 0, unroll=True)

    lane2 = lane_of((1, LANES), 1)

    def turn(t, g, shift_rows, shift):
        place = pl.ds(pl.multiple_of((g * group + shift_rows) * width, width), group * width)
        rows = vee[t, place, :].astype(BF16)
        return pltpu.roll(rows, shift, 1) if shift else rows

    def fill(t, _):
        def fill_rows(g, _):
            place = pl.ds(pl.multiple_of(g * group * width, group * width), group * width)
            s0 = turn(t, g, 2, 2 * OUT)
            s1 = turn(t, g, 1, 5 * OUT)
            s2 = turn(t, g, 0, 0)
            block = jnp.where(lane2 < 3 * OUT, s0, jnp.where(lane2 < 6 * OUT, s1, s2))
            cols[t, place, :] = block
            return 0

        lax.fori_loop(0, height // group, fill_rows, 0, unroll=True)
        cols_t[pl.ds(pl.multiple_of(t * LANES, LANES), LANES), :] = jnp.transpose(cols[t])
        return 0

    lax.fori_loop(0, wide, fill, 0)

    def fill_last(t, _):
        def fill_rows(g, _):
            place = pl.ds(pl.multiple_of(g * group * width, group * width), group * width)
            taps = [turn(t + kt, g, 0, kt * OUT) for kt in range(3)]
            block = jnp.where(
                lane2 < OUT, taps[0],
                jnp.where(lane2 < 2 * OUT, taps[1], jnp.where(lane2 < 3 * OUT, taps[2], jnp.zeros_like(taps[2]))),
            )
            last[t, place, :] = block
            return 0

        lax.fori_loop(0, height // group, fill_rows, 0, unroll=True)
        last_t[t] = jnp.transpose(last[t])[0 : 3 * OUT]
        return 0

    lax.fori_loop(0, frames, fill_last, 0)

    acc[...] = jnp.zeros(acc.shape, F32)

    def add_frame(t, _):
        left = jnp.concatenate(
            [cols_t[pl.ds(pl.multiple_of(t * LANES, LANES), 3 * LANES), :], last_t[t]], axis=0
        )
        acc[...] += jnp.dot(left, act[t], preferred_element_type=F32)
        return 0

    lax.fori_loop(0, frames, add_frame, 0)
    total[27 * OUT :, :] = jnp.zeros((total.shape[0] - 27 * OUT, cin), F32)
    for kt in range(3):
        total[9 * kt * OUT : 9 * kt * OUT + LANES, :] = acc[kt * LANES : (kt + 1) * LANES, :]
        total[9 * kt * OUT + LANES : 9 * (kt + 1) * OUT, :] = acc[3 * LANES + kt * OUT : 3 * LANES + (kt + 1) * OUT, :]
    part_ref[...] = jnp.transpose(total[...])[:, : 27 * OUT]

    chunk = 80

    def put(t):
        slot = lax.rem(t, ring)
        return pltpu.make_async_copy(xbuf.at[slot], out_ref.at[t], out_sem.at[slot])

    def grad_frame(t, _):
        slot = lax.rem(t, ring)

        @pl.when(t >= ring)
        def _():
            put(t - ring).wait()

        def grad_rows(r, _):
            place = pl.ds(pl.multiple_of(r * chunk * width, chunk * width), chunk * width)
            left = jnp.concatenate([cols[t + kt, place, :] for kt in range(3)] + [last[t, place, :]], axis=1)
            grad = jnp.dot(left, weights[...], preferred_element_type=F32) * slope[t, place, :]
            xbuf[slot, pl.ds(r * chunk, chunk)] = grad.reshape(chunk, width, cin).astype(BF16)
            return 0

        lax.fori_loop(0, height // chunk, grad_rows, 0, unroll=True)
        put(t).start()
        return 0

    lax.fori_loop(0, frames, grad_frame, 0)
    for t in range(frames - ring, frames):
        put(t).wait()


def reduce_kernel(
    n_tm, n_tile, scale, part_ref, out_ref, half, mine, pieces, sums, quads, sems, recv_sems
):
    tm, tile = lax.axis_index("tm"), lax.axis_index("tile")
    cores = 2
    core, y_lo = lax.rem(tm, cores), tm // cores
    groups = n_tile // cores
    y_hi, spot = tile // groups, lax.rem(tile, groups)
    rows = mine.shape[0]
    share = rows // groups

    barrier = pltpu.get_barrier_semaphore()
    partner = (tm - core) + (1 - core)
    pl.semaphore_signal(barrier, inc=1, device_id=(partner, tile), device_id_type=MESH)
    source_tm = y_lo * cores + y_hi

    def greet(k, _):
        source_tile = core * groups + k

        @pl.when(jnp.logical_not(jnp.logical_and(source_tm == tm, source_tile == tile)))
        def _():
            pl.semaphore_signal(
                barrier, inc=1, device_id=(source_tm, source_tile), device_id_type=MESH
            )

        return 0

    lax.fori_loop(0, groups, greet, 0)
    for k in range(1, n_tm):
        pl.semaphore_signal(
            barrier, inc=1, device_id=(lax.rem(tm + k, n_tm), tile), device_id_type=MESH
        )
    self_one = (core == y_hi).astype(jnp.int32)
    pl.semaphore_wait(barrier, 1 + groups - self_one + n_tm - 1)

    swap = pltpu.make_async_remote_copy(
        src_ref=part_ref.at[pl.ds(pl.multiple_of((1 - core) * rows, rows), rows)], dst_ref=half,
        send_sem=sems.at[0], recv_sem=sems.at[1],
        device_id=(partner, tile), device_id_type=MESH,
    )
    swap.start()
    swap.wait()
    own = part_ref[pl.ds(pl.multiple_of(core * rows, rows), rows), :] + half[...]
    mine[...] = own

    dest_tm = y_lo * cores + y_hi

    def piece(k):
        return mine.at[pl.ds(pl.multiple_of(k * share, share), share)]

    def send_piece(k, _):
        g = lax.rem(k + spot, groups)
        dest_tile = core * groups + g
        own_one = jnp.logical_and(dest_tm == tm, dest_tile == tile)

        @pl.when(jnp.logical_not(own_one))
        def _():
            pltpu.make_async_remote_copy(
                src_ref=piece(g), dst_ref=pieces.at[spot], send_sem=sems.at[2], recv_sem=recv_sems.at[0],
                device_id=(dest_tm, dest_tile), device_id_type=MESH,
            ).start()

        @pl.when(own_one)
        def _():
            pltpu.make_async_copy(piece(g), pieces.at[spot], recv_sems.at[0]).start()

        return 0

    lax.fori_loop(0, groups, send_piece, 0)
    pltpu.make_async_copy(pieces, pieces, recv_sems.at[0]).wait()

    def drain(k, _):
        pltpu.make_async_copy(pieces.at[0], pieces.at[0], sems.at[2]).wait()
        return 0

    lax.fori_loop(0, groups - self_one, drain, 0)
    sums[...] = jnp.sum(pieces[...], axis=0)

    copies = []
    for k in range(1, n_tm):
        copies.append(
            pltpu.make_async_remote_copy(
                src_ref=sums, dst_ref=quads.at[tm], send_sem=sems.at[3 + k], recv_sem=recv_sems.at[k],
                device_id=(lax.rem(tm + k, n_tm), tile), device_id_type=MESH,
            )
        )
        copies[-1].start()
    quads[tm] = sums[...]
    for copy in copies:
        copy.wait()
    whole = quads[0]
    for k in range(1, n_tm):
        whole = whole + quads[k]
    out_ref[...] = whole * scale


def on_device(n_tm, n_tile, scale, latent_grad, section_input, kernel):
    frames, height, width, cin = section_input.shape
    taps = kernel.shape[1]
    strips = n_tile // n_tm
    banded = jnp.transpose(latent_grad, (1, 0, 2)).reshape(ROWS, n_tm, FRAMES, strips * LANES)
    vmem = pl.BlockSpec(memory_space=pltpu.VMEM)
    anywhere = pl.BlockSpec(memory_space=pl.ANY)
    recv, edge = pl.pallas_call(
        functools.partial(exchange, n_tm, n_tile),
        out_shape=(
            jax.ShapeDtypeStruct((n_tile, ROWS, SLOTS, LANES), BF16),
            jax.ShapeDtypeStruct((n_tile, SLOTS, LANES), BF16),
        ),
        in_specs=[vmem],
        out_specs=(vmem, vmem),
        scratch_shapes=[
            pltpu.VMEM((n_tm, strips, ROWS, SLOTS, LANES), BF16),
            pltpu.VMEM((2, n_tm, SLOTS, LANES), BF16),
            pltpu.SemaphoreType.DMA((4,)),
        ],
        compiler_params=pltpu.CompilerParams(collective_id=0, has_side_effects=True),
    )(banded)
    wide, count = frames + 2, height * width
    kernel_t = jnp.transpose(kernel)
    input_grad, part = pl.pallas_call(
        compute,
        out_shape=(
            jax.ShapeDtypeStruct((frames, height, width, cin), BF16),
            jax.ShapeDtypeStruct((cin, taps), F32),
        ),
        in_specs=[vmem, vmem, anywhere, vmem],
        out_specs=(anywhere, vmem),
        scratch_shapes=[
            pltpu.VMEM((frames // 2, height, width, cin), BF16),
            pltpu.VMEM((frames, count, cin), BF16),
            pltpu.VMEM((frames, count, cin), F32),
            pltpu.VMEM((height, SLOTS, LANES), F32),
            pltpu.VMEM((3, height, LANES), F32),
            pltpu.VMEM((wide, height, LANES), F32),
            pltpu.VMEM((wide, (height + 2) * width, LANES), F32),
            pltpu.VMEM((wide, count, LANES), BF16),
            pltpu.VMEM((wide * LANES, count), BF16),
            pltpu.VMEM((frames, count, LANES), BF16),
            pltpu.VMEM((frames, 3 * OUT, count), BF16),
            pltpu.VMEM((4 * LANES, cin), BF16),
            pltpu.VMEM((27 * OUT, cin), F32),
            pltpu.VMEM((4 * LANES, cin), F32),
            pltpu.SemaphoreType.DMA((frames // 2,)),
            pltpu.SemaphoreType.DMA((frames // 2,)),
        ],
        compiler_params=pltpu.CompilerParams(vmem_limit_bytes=62 << 20),
    )(recv, edge, section_input, kernel_t)
    cores = 2
    rows = cin // cores
    share = cin // n_tile
    kernel_grad = pl.pallas_call(
        functools.partial(reduce_kernel, n_tm, n_tile, scale),
        out_shape=jax.ShapeDtypeStruct((share, taps), F32),
        in_specs=[vmem],
        out_specs=vmem,
        scratch_shapes=[
            pltpu.VMEM((rows, taps), F32),
            pltpu.VMEM((rows, taps), F32),
            pltpu.VMEM((n_tile // cores, share, taps), F32),
            pltpu.VMEM((share, taps), F32),
            pltpu.VMEM((n_tm, share, taps), F32),
            pltpu.SemaphoreType.DMA((3 + n_tm,)),
            pltpu.SemaphoreType.DMA((n_tm,)),
        ],
        compiler_params=pltpu.CompilerParams(collective_id=1, has_side_effects=True),
    )(part)
    return input_grad, kernel_grad


def solution(mesh):
    n_tm, n_tile = mesh.shape["tm"], mesh.shape["tile"]
    positions = n_tm * FRAMES * n_tile * ROWS * n_tile * STRIP
    return jax.shard_map(
        functools.partial(on_device, n_tm, n_tile, 1.0 / math.sqrt(positions)),
        mesh=mesh,
        in_specs=(P(None, "tile", "tm"), P("tm", None, "tile", None), P()),
        out_specs=(P("tm", None, "tile", None), P("tile", None)),
        check_vma=False,
    )
```

```python
import functools
import math

import jax
import jax.numpy as jnp
from jax import lax
from jax.experimental import pallas as pl
from jax.experimental.pallas import tpu as pltpu
from jax.sharding import PartitionSpec as P

MESH = pl.DeviceIdType.MESH
F32, BF16 = jnp.float32, jnp.bfloat16
LANES = 128
OUT = 16
STRIP = 8
FRAMES = 8
ROWS = 5
TILES = ROWS + 4
CORES = 2
WINDOW = 3


def lane_of(shape, axis):
    return lax.broadcasted_iota(jnp.int32, shape, axis)


def aligned(index, size):
    return pl.ds(pl.multiple_of(index * size, size), size)


def turned(value, shift, axis):
    shift %= value.shape[axis]
    return pltpu.roll(value, shift, axis) if shift else value


def strip_halo(left, right):
    lane = lane_of((1, LANES), 1)
    rows = []
    for i in range(ROWS):
        value = jnp.zeros((FRAMES, LANES), F32)
        if right is not None:
            value = jnp.where(lane >= LANES - OUT, right[i], value)
        if left is not None:
            value = jnp.where(lane < OUT, left[i], value)
        rows.append(turned(value, OUT + 2 * OUT * i, 1))
    return rows[0] + rows[1] + rows[2] + rows[3], rows[4]


def later_halo(first, second):
    row = lane_of((FRAMES, 1), 0)
    value = jnp.where(row < 6, turned(second, 4, 0), 0.0)
    return jnp.where(row < 2, 0.0, jnp.where(row < 4, turned(first, 2, 0), value))


def whole(
    n_tm, n_tile, scale, grad_ref, x_ref, kernel_ref, out_ref, kgrad_ref,
    msg, emsg, recv, edge, act, slope, field, halo, vee, cols, cols_t, last, last_t,
    weights, acc, part, mine, pieces, sums, quads, in_sem, sems,
):
    frames, height, width, cin = out_ref.shape
    wide, count = frames + 2, height * width
    tm, tile = lax.axis_index("tm"), lax.axis_index("tile")
    strips = n_tile // n_tm
    block = tile // strips
    place_in_block = lax.rem(tile, strips)
    from_left = jnp.logical_and(place_in_block == 0, block > 0)
    from_right = jnp.logical_and(place_in_block == strips - 1, block < n_tm - 1)
    has_edge = jnp.logical_or(from_left, from_right)
    edge_block = jnp.where(place_in_block == 0, block - 1, block + 1)
    messages = n_tm * strips
    send_main, send_edge, recv_main, recv_edge = (sems.at[i] for i in range(4))
    swap_send, swap_recv, piece_send, piece_recv = (sems.at[i] for i in range(4, 8))
    core, y_lo = lax.rem(tm, CORES), tm // CORES
    groups = n_tile // CORES
    y_hi, spot = tile // groups, lax.rem(tile, groups)
    partner = tm + 1 - 2 * core
    owner_tm = y_lo * CORES + y_hi

    def is_me(target_tm, target_tile):
        return jnp.logical_and(target_tm == tm, target_tile == tile)

    barrier = pltpu.get_barrier_semaphore()

    def hail(target_tm, target_tile):
        pl.semaphore_signal(barrier, inc=1, device_id=(target_tm, target_tile), device_id_type=MESH)

    def hail_bands(band, _):
        @pl.when(jnp.logical_not(is_me(block, band)))
        def _():
            hail(block, band)

        @pl.when(jnp.logical_and(has_edge, jnp.logical_not(is_me(edge_block, band))))
        def _():
            hail(edge_block, band)

        return 0

    lax.fori_loop(0, n_tile, hail_bands, 0)
    hail(partner, tile)

    def hail_groups(k, _):
        @pl.when(jnp.logical_not(is_me(owner_tm, core * groups + k)))
        def _():
            hail(owner_tm, core * groups + k)

        return 0

    lax.fori_loop(0, groups, hail_groups, 0)
    for k in range(1, n_tm):
        hail(lax.rem(tm + k, n_tm), tile)

    def fetch(t):
        return pltpu.make_async_copy(x_ref.at[t], out_ref.at[t], in_sem.at[t])

    for t in range(frames):
        fetch(t).start()

    r, c = lane_of((LANES, LANES), 0), lane_of((LANES, LANES), 1)
    same = jnp.logical_and(r // OUT + c // OUT == STRIP - 1, lax.rem(r, OUT) == lax.rem(c, OUT))
    flip = jnp.where(same, 1.0, 0.0).astype(BF16)
    row = lane_of((FRAMES, 1), 0)
    nothing = jnp.zeros((FRAMES, LANES), F32)
    flipped, halos = [], []
    for t in range(n_tm):
        rows = grad_ref[:, t].astype(F32).reshape(ROWS * FRAMES, strips * LANES).astype(BF16)
        here = [
            jnp.dot(rows[:, s * LANES : (s + 1) * LANES], flip, preferred_element_type=F32)
            .reshape(ROWS, FRAMES, LANES)
            for s in range(strips)
        ]
        flipped.append(here)
        padded = [None, None] + here + [None, None]
        halos.append([strip_halo(padded[s], padded[s + 2]) for s in range(strips + 2)])
    for t in range(n_tm):
        ends = t + 1 == n_tm
        for s in range(-1, strips + 1):
            first, second = halos[t][s + 1]
            later = nothing if ends else later_halo(*halos[t + 1][s + 1])
            if s < 0 or s == strips:
                side = 0 if s == strips else 1
                emsg[side, t, 0], emsg[side, t, 1], emsg[side, t, 2] = (
                    v.astype(BF16) for v in (first, second, later)
                )
                continue
            if ends:
                late = nothing
            else:
                nxt = flipped[t + 1][s]
                late = jnp.where(row < 6, turned(nxt[2], 4, 0), turned(nxt[3], 6, 0))
                late = jnp.where(row < 2, nxt[0], jnp.where(row < 4, turned(nxt[1], 2, 0), late))
                later = jnp.where(row < 2, nxt[4], later)
            tiles = [flipped[t][s][i] for i in range(ROWS)] + [first, second, late, later]
            for i, value in enumerate(tiles):
                msg[t, s, i] = value.astype(BF16)

    self_main = (block == tm).astype(jnp.int32)
    to_right, to_left = tm < n_tm - 1, tm > 0
    right_tile, left_tile = (tm + 1) * strips, tm * strips - 1
    self_edge = (
        jnp.logical_and(to_right, tile == right_tile).astype(jnp.int32)
        + jnp.logical_and(to_left, tile == left_tile).astype(jnp.int32)
    )
    edges_out = n_tm * (to_right.astype(jnp.int32) + to_left.astype(jnp.int32))
    self_piece = (core == y_hi).astype(jnp.int32)
    exchange_out = messages - self_main + edges_out - self_edge
    pl.semaphore_wait(barrier, exchange_out + 1 + groups - self_piece + n_tm - 1)

    def send(source, target, send_sem, recv_sem, target_tm, target_tile):
        own = is_me(target_tm, target_tile)

        @pl.when(jnp.logical_not(own))
        def _():
            pltpu.make_async_remote_copy(
                src_ref=source, dst_ref=target, send_sem=send_sem, recv_sem=recv_sem,
                device_id=(target_tm, target_tile), device_id_type=MESH,
            ).start()

        @pl.when(own)
        def _():
            pltpu.make_async_copy(source, target, recv_sem).start()

    def send_edges(t, _):
        @pl.when(to_right)
        def _():
            send(emsg.at[0, t], edge.at[tile], send_edge, recv_edge, t, right_tile)

        @pl.when(to_left)
        def _():
            send(emsg.at[1, t], edge.at[tile], send_edge, recv_edge, t, left_tile)

        return 0

    def send_one(k, _):
        turn = lax.rem(k + tile, messages)
        t, s = turn // strips, lax.rem(turn, strips)
        send(msg.at[t, s], recv.at[tile], send_main, recv_main, t, tm * strips + s)
        return 0

    lax.fori_loop(0, n_tm, send_edges, 0)
    lax.fori_loop(0, messages, send_one, 0)

    weights[...] = jnp.zeros(weights.shape, BF16)
    for kt in range(3):
        taps = kernel_ref[9 * kt * OUT : 9 * (kt + 1) * OUT, :]
        taps = (0.5 * taps.astype(F32)).astype(BF16)
        weights[kt * LANES : (kt + 1) * LANES, :] = taps[:LANES]
        weights[3 * LANES + kt * OUT : 3 * LANES + (kt + 1) * OUT, :] = taps[LANES:]

    step = 8

    def silu_frame(t, _):
        fetch(t).wait()

        def silu_rows(r, _):
            half_x = 0.5 * out_ref[t, pl.ds(r * step, step)].astype(F32).reshape(step * width, cin)
            u = jnp.tanh(half_x)
            product = half_x * u
            rows = aligned(r, step * width)
            act[t, rows, :] = (half_x + product).astype(BF16)
            slope[t, rows, :] = (1.0 + u) * ((1.0 + half_x) - product)
            return 0

        lax.fori_loop(0, height // step, silu_rows, 0, unroll=4)
        return 0

    lax.fori_loop(0, frames, silu_frame, 0)

    @pl.when(jnp.logical_not(has_edge))
    def _():
        edge[...] = jnp.zeros(edge.shape, BF16)

    @pl.when(has_edge)
    def _():
        pltpu.make_async_copy(edge, edge, recv_edge).wait()

    pltpu.make_async_copy(recv, recv, recv_main).wait()

    def unpack(b, _):
        tiles = [recv[b, i].astype(F32) for i in range(TILES)]
        beside = tiles[5] + edge[b, 0].astype(F32)
        beside_4 = tiles[6] + edge[b, 1].astype(F32)
        later = tiles[8] + edge[b, 2].astype(F32)
        for i in range(ROWS):
            at = b * ROWS + i
            field[at, 0:FRAMES] = tiles[i]
            field[at, FRAMES:] = turned(tiles[7], -2 * i, 0) if i < 4 else later
            halo[at, 0:FRAMES] = turned(beside if i < 4 else beside_4, -OUT - 2 * OUT * i, 1)
            halo[at, FRAMES:] = turned(turned(later, -2 if i < 4 else -4, 0), -OUT - 2 * OUT * i, 1)
        return 0

    lax.fori_loop(0, n_tile, unpack, 0, unroll=4)

    lane3, col3 = lane_of((1, width, LANES), 2), lane_of((1, width, LANES), 1)
    outside = jnp.logical_or(
        jnp.logical_and(col3 == 0, lane3 < OUT),
        jnp.logical_and(col3 == width - 1, lane3 >= LANES - OUT),
    )
    edge_rows = jnp.zeros((width, LANES), F32)
    group = 16
    for t in range(WINDOW):
        vee[t, 0:width, :] = edge_rows
        vee[t, (height + 1) * width : (height + 2) * width, :] = edge_rows

    lane2 = lane_of((1, LANES), 1)

    def tap(t, g, shift_rows, shift):
        at = pl.ds(pl.multiple_of((g * group + shift_rows) * width, width), group * width)
        return turned(vee[t % WINDOW, at, :].astype(BF16), shift, 1)

    for t in range(wide):
        def spread(g, _, t=t):
            rows = pl.ds(g * group, group)
            main = jnp.broadcast_to(field[rows, t : t + 1, :], (group, width, LANES))
            side = jnp.broadcast_to(halo[rows, t : t + 1, :], (group, width, LANES))
            at = pl.ds(pl.multiple_of((g * group + 1) * width, width), group * width)
            values = jnp.where(outside, side, main).reshape(group * width, LANES)
            vee[t % WINDOW, at, :] = pltpu.roll(values, 0, 1, stride=OUT, stride_axis=0)
            return 0

        def fill(g, _, t=t):
            rows = aligned(g, group * width)
            s0, s1, s2 = tap(t, g, 2, 2 * OUT), tap(t, g, 1, 5 * OUT), tap(t, g, 0, 0)
            cols[t, rows, :] = jnp.where(lane2 < 3 * OUT, s0, jnp.where(lane2 < 6 * OUT, s1, s2))
            return 0

        def fill_last(g, _, t=t):
            rows = aligned(g, group * width)
            taps = [tap(t - 2 + kt, g, 0, kt * OUT) for kt in range(3)]
            value = jnp.where(lane2 < 3 * OUT, taps[2], jnp.zeros_like(taps[2]))
            last[t - 2, rows, :] = jnp.where(lane2 < OUT, taps[0], jnp.where(lane2 < 2 * OUT, taps[1], value))
            return 0

        lax.fori_loop(0, height // group, spread, 0, unroll=True)
        lax.fori_loop(0, height // group, fill, 0, unroll=True)
        cols_t[t * LANES : (t + 1) * LANES, :] = jnp.transpose(cols[t])
        if t >= 2:
            lax.fori_loop(0, height // group, fill_last, 0, unroll=True)
            last_t[t - 2] = jnp.transpose(last[t - 2])[0 : 3 * OUT]

    acc[...] = jnp.zeros(acc.shape, F32)

    def add_frame(t, _):
        left = jnp.concatenate(
            [cols_t[pl.ds(pl.multiple_of(t * LANES, LANES), 3 * LANES), :], last_t[t]], axis=0
        )
        acc[...] += jnp.dot(left, act[t], preferred_element_type=F32)
        return 0

    lax.fori_loop(0, frames, add_frame, 0)
    pieces_of_total = []
    for kt in range(3):
        pieces_of_total.append(acc[kt * LANES : (kt + 1) * LANES, :])
        pieces_of_total.append(acc[3 * LANES + kt * OUT : 3 * LANES + (kt + 1) * OUT, :])
    pieces_of_total.append(jnp.zeros((part.shape[1] - 27 * OUT, cin), F32))
    part[...] = jnp.transpose(jnp.concatenate(pieces_of_total, axis=0))

    chunk = 80

    def grad_frame(t, _):
        def grad_rows(r, _):
            rows = aligned(r, chunk * width)
            left = jnp.concatenate([cols[t + kt, rows, :] for kt in range(3)] + [last[t, rows, :]], axis=1)
            grad = jnp.dot(left, weights[...], preferred_element_type=F32) * slope[t, rows, :]
            out_ref[t, pl.ds(r * chunk, chunk)] = grad.reshape(chunk, width, cin).astype(BF16)
            return 0

        lax.fori_loop(0, height // chunk, grad_rows, 0, unroll=True)
        return 0

    rows = mine.shape[0]
    share = rows // groups
    swap = pltpu.make_async_remote_copy(
        src_ref=part.at[aligned(1 - core, rows)], dst_ref=mine,
        send_sem=swap_send, recv_sem=swap_recv,
        device_id=(partner, tile), device_id_type=MESH,
    )
    swap.start()
    lax.fori_loop(0, SPLIT[0], grad_frame, 0)
    swap.wait()
    mine[...] += part[aligned(core, rows), :]

    def send_piece(k, _):
        g = lax.rem(k + spot, groups)
        send(mine.at[aligned(g, share)], pieces.at[spot], piece_send, piece_recv, owner_tm, core * groups + g)
        return 0

    lax.fori_loop(0, groups, send_piece, 0)
    lax.fori_loop(SPLIT[0], SPLIT[1], grad_frame, 0)
    pltpu.make_async_copy(pieces, pieces, piece_recv).wait()
    sums[...] = jnp.sum(pieces[...], axis=0)

    copies = []
    for k in range(1, n_tm):
        copies.append(
            pltpu.make_async_remote_copy(
                src_ref=sums, dst_ref=quads.at[tm], send_sem=sems.at[8 + 2 * k], recv_sem=sems.at[9 + 2 * k],
                device_id=(lax.rem(tm + k, n_tm), tile), device_id_type=MESH,
            )
        )
        copies[-1].start()
    quads[tm] = sums[...]
    lax.fori_loop(SPLIT[1], frames, grad_frame, 0)

    def drain(source, sem, times):
        def one(k, _):
            pltpu.make_async_copy(source, source, sem).wait()
            return 0

        lax.fori_loop(0, times, one, 0)

    drain(msg.at[0, 0], send_main, messages - self_main)
    drain(emsg.at[0, 0], send_edge, edges_out - self_edge)
    drain(pieces.at[0], piece_send, groups - self_piece)
    for copy in copies:
        copy.wait()
    result = quads[0]
    for k in range(1, n_tm):
        result = result + quads[k]
    kgrad_ref[...] = (result * scale)[:, : kgrad_ref.shape[1]]


SPLIT = (2, 6)


def on_device(n_tm, n_tile, scale, latent_grad, section_input, kernel):
    frames, height, width, cin = section_input.shape
    taps = kernel.shape[1]
    strips = n_tile // n_tm
    banded = jnp.transpose(latent_grad, (1, 0, 2)).reshape(ROWS, n_tm, FRAMES, strips * LANES)
    wide, count = frames + 2, height * width
    rows, share, padded = cin // CORES, cin // n_tile, 4 * LANES
    vmem = pl.BlockSpec(memory_space=pltpu.VMEM)
    return pl.pallas_call(
        functools.partial(whole, n_tm, n_tile, scale),
        out_shape=(
            pltpu.VMEM((frames, height, width, cin), BF16),
            jax.ShapeDtypeStruct((share, taps), F32),
        ),
        in_specs=[vmem, pl.BlockSpec(memory_space=pl.ANY), vmem],
        out_specs=(vmem, vmem),
        scratch_shapes=[
            pltpu.VMEM((n_tm, strips, TILES, FRAMES, LANES), BF16),
            pltpu.VMEM((2, n_tm, 3, FRAMES, LANES), BF16),
            pltpu.VMEM((n_tile, TILES, FRAMES, LANES), BF16),
            pltpu.VMEM((n_tile, 3, FRAMES, LANES), BF16),
            pltpu.VMEM((frames, count, cin), BF16),
            pltpu.VMEM((frames, count, cin), F32),
            pltpu.VMEM((height, 2 * FRAMES, LANES), F32),
            pltpu.VMEM((height, 2 * FRAMES, LANES), F32),
            pltpu.VMEM((WINDOW, (height + 2) * width, LANES), F32),
            pltpu.VMEM((wide, count, LANES), BF16),
            pltpu.VMEM((wide * LANES, count), BF16),
            pltpu.VMEM((frames, count, LANES), BF16),
            pltpu.VMEM((frames, 3 * OUT, count), BF16),
            pltpu.VMEM((padded, cin), BF16),
            pltpu.VMEM((27 * OUT, cin), F32),
            pltpu.VMEM((cin, padded), F32),
            pltpu.VMEM((rows, padded), F32),
            pltpu.VMEM((n_tile // CORES, share, padded), F32),
            pltpu.VMEM((share, padded), F32),
            pltpu.VMEM((n_tm, share, padded), F32),
            pltpu.SemaphoreType.DMA((frames,)),
            pltpu.SemaphoreType.DMA((16,)),
        ],
        compiler_params=pltpu.CompilerParams(
            collective_id=0, has_side_effects=True, vmem_limit_bytes=VMEM_LIMIT
        ),
    )(banded, section_input, jnp.transpose(kernel))


VMEM_LIMIT = 53 << 20


def solution(mesh):
    n_tm, n_tile = mesh.shape["tm"], mesh.shape["tile"]
    positions = n_tm * FRAMES * n_tile * ROWS * n_tile * STRIP
    return jax.shard_map(
        functools.partial(on_device, n_tm, n_tile, 1.0 / math.sqrt(positions)),
        mesh=mesh,
        in_specs=(P(None, "tile", "tm"), P("tm", None, "tile", None), P()),
        out_specs=(P("tm", None, "tile", None), P("tile", None)),
        check_vma=False,
    )
```

```python
import functools
import math

import jax
import jax.numpy as jnp
from jax import lax
from jax.experimental import pallas as pl
from jax.experimental.pallas import tpu as pltpu
from jax.sharding import PartitionSpec as P

MESH = pl.DeviceIdType.MESH
F32, BF16 = jnp.float32, jnp.bfloat16
LANES = 128
OUT = 16
STRIP = 8
FRAMES = 8
ROWS = 5
TILES = ROWS + 4
CORES = 2
WINDOW = 3


def lane_of(shape, axis):
    return lax.broadcasted_iota(jnp.int32, shape, axis)


def aligned(index, size):
    return pl.ds(pl.multiple_of(index * size, size), size)


def turned(value, shift, axis):
    shift %= value.shape[axis]
    return pltpu.roll(value, shift, axis) if shift else value


def strip_halo(left, right):
    lane = lane_of((1, LANES), 1)
    rows = []
    for i in range(ROWS):
        value = jnp.zeros((FRAMES, LANES), F32)
        if right is not None:
            value = jnp.where(lane >= LANES - OUT, right[i], value)
        if left is not None:
            value = jnp.where(lane < OUT, left[i], value)
        rows.append(turned(value, OUT + 2 * OUT * i, 1))
    return rows[0] + rows[1] + rows[2] + rows[3], rows[4]


def later_halo(first, second):
    row = lane_of((FRAMES, 1), 0)
    value = jnp.where(row < 6, turned(second, 4, 0), 0.0)
    return jnp.where(row < 2, 0.0, jnp.where(row < 4, turned(first, 2, 0), value))


def whole(
    n_tm, n_tile, scale, grad_hbm, x_ref, kernel_hbm, out_ref, kgrad_ref,
    grad_ref, kernel_ref, msg, emsg, recv, edge, act, slope, field, halo, vee, cols, cols_t, last, last_t,
    weights, acc, part, mine, pieces, sums, quads, in_sem, sems,
):
    frames, height, width, cin = out_ref.shape
    wide, count = frames + 2, height * width
    tm, tile = lax.axis_index("tm"), lax.axis_index("tile")
    strips = n_tile // n_tm
    block = tile // strips
    place_in_block = lax.rem(tile, strips)
    from_left = jnp.logical_and(place_in_block == 0, block > 0)
    from_right = jnp.logical_and(place_in_block == strips - 1, block < n_tm - 1)
    has_edge = jnp.logical_or(from_left, from_right)
    edge_block = jnp.where(place_in_block == 0, block - 1, block + 1)
    messages = n_tm * strips
    send_main, send_edge, recv_main, recv_edge = (sems.at[i] for i in range(4))
    swap_send, swap_recv, piece_send, piece_recv = (sems.at[i] for i in range(4, 8))
    core, y_lo = lax.rem(tm, CORES), tm // CORES
    groups = n_tile // CORES
    y_hi, spot = tile // groups, lax.rem(tile, groups)
    partner = tm + 1 - 2 * core
    owner_tm = y_lo * CORES + y_hi

    def is_me(target_tm, target_tile):
        return jnp.logical_and(target_tm == tm, target_tile == tile)

    grad_copy = pltpu.make_async_copy(grad_hbm, grad_ref, sems.at[8])
    kernel_copy = pltpu.make_async_copy(kernel_hbm, kernel_ref, sems.at[9])
    grad_copy.start()
    kernel_copy.start()

    def fetch(t):
        return pltpu.make_async_copy(x_ref.at[t], out_ref.at[t], in_sem.at[t])

    for t in range(frames):
        fetch(t).start()

    barrier = pltpu.get_barrier_semaphore()

    def hail(target_tm, target_tile):
        pl.semaphore_signal(barrier, inc=1, device_id=(target_tm, target_tile), device_id_type=MESH)

    def hail_bands(band, _):
        @pl.when(jnp.logical_not(is_me(block, band)))
        def _():
            hail(block, band)

        @pl.when(jnp.logical_and(has_edge, jnp.logical_not(is_me(edge_block, band))))
        def _():
            hail(edge_block, band)

        return 0

    lax.fori_loop(0, n_tile, hail_bands, 0)
    hail(partner, tile)

    def hail_groups(k, _):
        @pl.when(jnp.logical_not(is_me(owner_tm, core * groups + k)))
        def _():
            hail(owner_tm, core * groups + k)

        return 0

    lax.fori_loop(0, groups, hail_groups, 0)
    for k in range(1, n_tm):
        hail(lax.rem(tm + k, n_tm), tile)

    r, c = lane_of((LANES, LANES), 0), lane_of((LANES, LANES), 1)
    same = jnp.logical_and(r // OUT + c // OUT == STRIP - 1, lax.rem(r, OUT) == lax.rem(c, OUT))
    flip = jnp.where(same, 1.0, 0.0).astype(BF16)
    row = lane_of((FRAMES, 1), 0)
    nothing = jnp.zeros((FRAMES, LANES), F32)
    grad_copy.wait()
    flipped, halos = [], []
    for t in range(n_tm):
        rows = grad_ref[:, t].astype(F32).reshape(ROWS * FRAMES, strips * LANES).astype(BF16)
        here = [
            jnp.dot(rows[:, s * LANES : (s + 1) * LANES], flip, preferred_element_type=F32)
            .reshape(ROWS, FRAMES, LANES)
            for s in range(strips)
        ]
        flipped.append(here)
        padded = [None, None] + here + [None, None]
        halos.append([strip_halo(padded[s], padded[s + 2]) for s in range(strips + 2)])
    for t in range(n_tm):
        ends = t + 1 == n_tm
        for s in range(-1, strips + 1):
            first, second = halos[t][s + 1]
            later = nothing if ends else later_halo(*halos[t + 1][s + 1])
            if s < 0 or s == strips:
                side = 0 if s == strips else 1
                emsg[side, t, 0], emsg[side, t, 1], emsg[side, t, 2] = (
                    v.astype(BF16) for v in (first, second, later)
                )
                continue
            if ends:
                late = nothing
            else:
                nxt = flipped[t + 1][s]
                late = jnp.where(row < 6, turned(nxt[2], 4, 0), turned(nxt[3], 6, 0))
                late = jnp.where(row < 2, nxt[0], jnp.where(row < 4, turned(nxt[1], 2, 0), late))
                later = jnp.where(row < 2, nxt[4], later)
            tiles = [flipped[t][s][i] for i in range(ROWS)] + [first, second, late, later]
            for i, value in enumerate(tiles):
                msg[t, s, i] = value.astype(BF16)

    self_main = (block == tm).astype(jnp.int32)
    to_right, to_left = tm < n_tm - 1, tm > 0
    right_tile, left_tile = (tm + 1) * strips, tm * strips - 1
    self_edge = (
        jnp.logical_and(to_right, tile == right_tile).astype(jnp.int32)
        + jnp.logical_and(to_left, tile == left_tile).astype(jnp.int32)
    )
    edges_out = n_tm * (to_right.astype(jnp.int32) + to_left.astype(jnp.int32))
    self_piece = (core == y_hi).astype(jnp.int32)
    exchange_out = messages - self_main + edges_out - self_edge
    pl.semaphore_wait(barrier, exchange_out + 1 + groups - self_piece + n_tm - 1)

    def send(source, target, send_sem, recv_sem, target_tm, target_tile):
        own = is_me(target_tm, target_tile)

        @pl.when(jnp.logical_not(own))
        def _():
            pltpu.make_async_remote_copy(
                src_ref=source, dst_ref=target, send_sem=send_sem, recv_sem=recv_sem,
                device_id=(target_tm, target_tile), device_id_type=MESH,
            ).start()

        @pl.when(own)
        def _():
            pltpu.make_async_copy(source, target, recv_sem).start()

    def send_edges(t, _):
        @pl.when(to_right)
        def _():
            send(emsg.at[0, t], edge.at[tile], send_edge, recv_edge, t, right_tile)

        @pl.when(to_left)
        def _():
            send(emsg.at[1, t], edge.at[tile], send_edge, recv_edge, t, left_tile)

        return 0

    def send_one(k, _):
        turn = lax.rem(k + tile, messages)
        t, s = turn // strips, lax.rem(turn, strips)
        send(msg.at[t, s], recv.at[tile], send_main, recv_main, t, tm * strips + s)
        return 0

    lax.fori_loop(0, n_tm, send_edges, 0)
    lax.fori_loop(0, messages, send_one, 0)

    kernel_copy.wait()
    weights[...] = jnp.zeros(weights.shape, BF16)
    for kt in range(3):
        taps = kernel_ref[9 * kt * OUT : 9 * (kt + 1) * OUT, :]
        taps = (0.5 * taps.astype(F32)).astype(BF16)
        weights[kt * LANES : (kt + 1) * LANES, :] = taps[:LANES]
        weights[3 * LANES + kt * OUT : 3 * LANES + (kt + 1) * OUT, :] = taps[LANES:]

    step = 8

    def silu_frame(t, _):
        fetch(t).wait()

        def silu_rows(r, _):
            half_x = 0.5 * out_ref[t, pl.ds(r * step, step)].astype(F32).reshape(step * width, cin)
            u = jnp.tanh(half_x)
            product = half_x * u
            rows = aligned(r, step * width)
            act[t, rows, :] = (half_x + product).astype(BF16)
            slope[t, rows, :] = (1.0 + u) * ((1.0 + half_x) - product)
            return 0

        lax.fori_loop(0, height // step, silu_rows, 0, unroll=4)
        return 0

    lax.fori_loop(0, frames, silu_frame, 0)

    @pl.when(jnp.logical_not(has_edge))
    def _():
        edge[...] = jnp.zeros(edge.shape, BF16)

    @pl.when(has_edge)
    def _():
        pltpu.make_async_copy(edge, edge, recv_edge).wait()

    pltpu.make_async_copy(recv, recv, recv_main).wait()

    def unpack(b, _):
        tiles = [recv[b, i].astype(F32) for i in range(TILES)]
        beside = tiles[5] + edge[b, 0].astype(F32)
        beside_4 = tiles[6] + edge[b, 1].astype(F32)
        later = tiles[8] + edge[b, 2].astype(F32)
        for i in range(ROWS):
            at = b * ROWS + i
            field[at, 0:FRAMES] = tiles[i]
            field[at, FRAMES:] = turned(tiles[7], -2 * i, 0) if i < 4 else later
            halo[at, 0:FRAMES] = turned(beside if i < 4 else beside_4, -OUT - 2 * OUT * i, 1)
            halo[at, FRAMES:] = turned(turned(later, -2 if i < 4 else -4, 0), -OUT - 2 * OUT * i, 1)
        return 0

    lax.fori_loop(0, n_tile, unpack, 0, unroll=4)

    lane3, col3 = lane_of((1, width, LANES), 2), lane_of((1, width, LANES), 1)
    outside = jnp.logical_or(
        jnp.logical_and(col3 == 0, lane3 < OUT),
        jnp.logical_and(col3 == width - 1, lane3 >= LANES - OUT),
    )
    edge_rows = jnp.zeros((width, LANES), F32)
    group = 16
    for t in range(WINDOW):
        vee[t, 0:width, :] = edge_rows
        vee[t, (height + 1) * width : (height + 2) * width, :] = edge_rows

    lane2 = lane_of((1, LANES), 1)

    def tap(t, g, shift_rows, shift):
        at = pl.ds(pl.multiple_of((g * group + shift_rows) * width, width), group * width)
        return turned(vee[t % WINDOW, at, :].astype(BF16), shift, 1)

    acc[...] = jnp.zeros(acc.shape, F32)

    def add_frame(t):
        left = jnp.concatenate([cols_t[t * LANES : (t + 3) * LANES, :], last_t[t]], axis=0)
        acc[...] += jnp.dot(left, act[t], preferred_element_type=F32)

    for t in range(wide):
        def spread(g, _, t=t):
            rows = pl.ds(g * group, group)
            main = jnp.broadcast_to(field[rows, t : t + 1, :], (group, width, LANES))
            side = jnp.broadcast_to(halo[rows, t : t + 1, :], (group, width, LANES))
            at = pl.ds(pl.multiple_of((g * group + 1) * width, width), group * width)
            values = jnp.where(outside, side, main).reshape(group * width, LANES)
            vee[t % WINDOW, at, :] = pltpu.roll(values, 0, 1, stride=OUT, stride_axis=0)
            return 0

        def fill(g, _, t=t):
            rows = aligned(g, group * width)
            s0, s1, s2 = tap(t, g, 2, 2 * OUT), tap(t, g, 1, 5 * OUT), tap(t, g, 0, 0)
            cols[t, rows, :] = jnp.where(lane2 < 3 * OUT, s0, jnp.where(lane2 < 6 * OUT, s1, s2))
            return 0

        def fill_last(g, _, t=t):
            rows = aligned(g, group * width)
            taps = [tap(t - 2 + kt, g, 0, kt * OUT) for kt in range(3)]
            value = jnp.where(lane2 < 3 * OUT, taps[2], jnp.zeros_like(taps[2]))
            last[t - 2, rows, :] = jnp.where(lane2 < OUT, taps[0], jnp.where(lane2 < 2 * OUT, taps[1], value))
            return 0

        lax.fori_loop(0, height // group, spread, 0, unroll=True)
        lax.fori_loop(0, height // group, fill, 0, unroll=True)
        cols_t[t * LANES : (t + 1) * LANES, :] = jnp.transpose(cols[t])
        if t >= 2:
            lax.fori_loop(0, height // group, fill_last, 0, unroll=True)
            last_t[t - 2] = jnp.transpose(last[t - 2])[0 : 3 * OUT]
        if t >= 3:
            add_frame(t - 3)
    add_frame(frames - 1)

    pieces_of_total = []
    for kt in range(3):
        pieces_of_total.append(acc[kt * LANES : (kt + 1) * LANES, :])
        pieces_of_total.append(acc[3 * LANES + kt * OUT : 3 * LANES + (kt + 1) * OUT, :])
    pieces_of_total.append(jnp.zeros((part.shape[1] - 27 * OUT, cin), F32))
    part[...] = jnp.transpose(jnp.concatenate(pieces_of_total, axis=0))

    chunk = 40

    def grad_frame(t, _):
        def grad_rows(r, _):
            rows = aligned(r, chunk * width)
            left = jnp.concatenate([cols[t + kt, rows, :] for kt in range(3)] + [last[t, rows, :]], axis=1)
            grad = jnp.dot(left, weights[...], preferred_element_type=F32) * slope[t, rows, :]
            out_ref[t, pl.ds(r * chunk, chunk)] = grad.reshape(chunk, width, cin).astype(BF16)
            return 0

        lax.fori_loop(0, height // chunk, grad_rows, 0, unroll=True)
        return 0

    rows = mine.shape[0]
    share = rows // groups
    swap = pltpu.make_async_remote_copy(
        src_ref=part.at[aligned(1 - core, rows)], dst_ref=mine,
        send_sem=swap_send, recv_sem=swap_recv,
        device_id=(partner, tile), device_id_type=MESH,
    )
    swap.start()
    lax.fori_loop(0, SPLIT[0], grad_frame, 0)
    swap.wait()
    mine[...] += part[aligned(core, rows), :]

    def send_piece(k, _):
        g = lax.rem(k + spot, groups)
        send(mine.at[aligned(g, share)], pieces.at[spot], piece_send, piece_recv, owner_tm, core * groups + g)
        return 0

    lax.fori_loop(0, groups, send_piece, 0)
    lax.fori_loop(SPLIT[0], SPLIT[1], grad_frame, 0)
    pltpu.make_async_copy(pieces, pieces, piece_recv).wait()
    sums[...] = jnp.sum(pieces[...], axis=0)

    copies = []
    for k in range(1, n_tm):
        copies.append(
            pltpu.make_async_remote_copy(
                src_ref=sums, dst_ref=quads.at[tm], send_sem=sems.at[8 + 2 * k], recv_sem=sems.at[9 + 2 * k],
                device_id=(lax.rem(tm + k, n_tm), tile), device_id_type=MESH,
            )
        )
        copies[-1].start()
    quads[tm] = sums[...]
    lax.fori_loop(SPLIT[1], frames, grad_frame, 0)

    def drain(source, sem, times):
        def one(k, _):
            pltpu.make_async_copy(source, source, sem).wait()
            return 0

        lax.fori_loop(0, times, one, 0)

    drain(msg.at[0, 0], send_main, messages - self_main)
    drain(emsg.at[0, 0], send_edge, edges_out - self_edge)
    drain(pieces.at[0], piece_send, groups - self_piece)
    for copy in copies:
        copy.wait()
    result = quads[0]
    for k in range(1, n_tm):
        result = result + quads[k]
    kgrad_ref[...] = (result * scale)[:, : kgrad_ref.shape[1]]


SPLIT = (1, 7)


def on_device(n_tm, n_tile, scale, latent_grad, section_input, kernel):
    frames, height, width, cin = section_input.shape
    taps = kernel.shape[1]
    strips = n_tile // n_tm
    banded = jnp.transpose(latent_grad, (1, 0, 2)).reshape(ROWS, n_tm, FRAMES, strips * LANES)
    wide, count = frames + 2, height * width
    rows, share, padded = cin // CORES, cin // n_tile, 4 * LANES
    vmem = pl.BlockSpec(memory_space=pltpu.VMEM)
    return pl.pallas_call(
        functools.partial(whole, n_tm, n_tile, scale),
        out_shape=(
            pltpu.VMEM((frames, height, width, cin), BF16),
            jax.ShapeDtypeStruct((share, taps), F32),
        ),
        in_specs=[pl.BlockSpec(memory_space=pl.ANY)] * 3,
        out_specs=(vmem, vmem),
        scratch_shapes=[
            pltpu.VMEM((ROWS, n_tm, FRAMES, strips * LANES), BF16),
            pltpu.VMEM((taps, cin), BF16),
            pltpu.VMEM((n_tm, strips, TILES, FRAMES, LANES), BF16),
            pltpu.VMEM((2, n_tm, 3, FRAMES, LANES), BF16),
            pltpu.VMEM((n_tile, TILES, FRAMES, LANES), BF16),
            pltpu.VMEM((n_tile, 3, FRAMES, LANES), BF16),
            pltpu.VMEM((frames, count, cin), BF16),
            pltpu.VMEM((frames, count, cin), F32),
            pltpu.VMEM((height, 2 * FRAMES, LANES), F32),
            pltpu.VMEM((height, 2 * FRAMES, LANES), F32),
            pltpu.VMEM((WINDOW, (height + 2) * width, LANES), F32),
            pltpu.VMEM((wide, count, LANES), BF16),
            pltpu.VMEM((wide * LANES, count), BF16),
            pltpu.VMEM((frames, count, LANES), BF16),
            pltpu.VMEM((frames, 3 * OUT, count), BF16),
            pltpu.VMEM((padded, cin), BF16),
            pltpu.VMEM((27 * OUT, cin), F32),
            pltpu.VMEM((cin, padded), F32),
            pltpu.VMEM((rows, padded), F32),
            pltpu.VMEM((n_tile // CORES, share, padded), F32),
            pltpu.VMEM((share, padded), F32),
            pltpu.VMEM((n_tm, share, padded), F32),
            pltpu.SemaphoreType.DMA((frames,)),
            pltpu.SemaphoreType.DMA((16,)),
        ],
        compiler_params=pltpu.CompilerParams(
            collective_id=0, has_side_effects=True, vmem_limit_bytes=VMEM_LIMIT
        ),
    )(banded, section_input, jnp.transpose(kernel))


VMEM_LIMIT = 53 << 20


def solution(mesh):
    n_tm, n_tile = mesh.shape["tm"], mesh.shape["tile"]
    positions = n_tm * FRAMES * n_tile * ROWS * n_tile * STRIP
    return jax.shard_map(
        functools.partial(on_device, n_tm, n_tile, 1.0 / math.sqrt(positions)),
        mesh=mesh,
        in_specs=(P(None, "tile", "tm"), P("tm", None, "tile", None), P()),
        out_specs=(P("tm", None, "tile", None), P("tile", None)),
        check_vma=False,
    )
```

```python
import functools
import math

import jax
import jax.numpy as jnp
from jax import lax
from jax.experimental import pallas as pl
from jax.experimental.pallas import tpu as pltpu
from jax.sharding import PartitionSpec as P

MESH = pl.DeviceIdType.MESH
F32, BF16 = jnp.float32, jnp.bfloat16
LANES = 128
OUT = 16
STRIP = 8
FRAMES = 8
ROWS = 5
FIRST = 5
SECOND = 4
EARLY = 4
CORES = 2
WINDOW = 3


def lane_of(shape, axis):
    return lax.broadcasted_iota(jnp.int32, shape, axis)


def aligned(index, size):
    return pl.ds(pl.multiple_of(index * size, size), size)


def turned(value, shift, axis):
    shift %= value.shape[axis]
    return pltpu.roll(value, shift, axis) if shift else value


def strip_halo(left, right):
    lane = lane_of((1, LANES), 1)
    rows = []
    for i in range(ROWS):
        value = jnp.zeros((FRAMES, LANES), F32)
        if right is not None:
            value = jnp.where(lane >= LANES - OUT, right[i], value)
        if left is not None:
            value = jnp.where(lane < OUT, left[i], value)
        rows.append(turned(value, OUT + 2 * OUT * i, 1))
    return rows[0] + rows[1] + rows[2] + rows[3], rows[4]


def later_halo(first, second):
    row = lane_of((FRAMES, 1), 0)
    value = jnp.where(row < 6, turned(second, 4, 0), 0.0)
    return jnp.where(row < 2, 0.0, jnp.where(row < 4, turned(first, 2, 0), value))


def whole(
    n_tm, n_tile, scale, grad_hbm, x_ref, kernel_hbm, out_ref, kgrad_ref,
    grad_ref, kernel_ref, msg, msg_2, emsg, recv, recv_2, edge, act, slope, field, halo, vee, cols, cols_t, last, last_t,
    weights, acc, part, mine, mine_half, pieces, sums, quads, in_sem, sems,
):
    frames, height, width, cin = out_ref.shape
    wide, count = frames + 2, height * width
    tm, tile = lax.axis_index("tm"), lax.axis_index("tile")
    strips = n_tile // n_tm
    block = tile // strips
    place_in_block = lax.rem(tile, strips)
    from_left = jnp.logical_and(place_in_block == 0, block > 0)
    from_right = jnp.logical_and(place_in_block == strips - 1, block < n_tm - 1)
    has_edge = jnp.logical_or(from_left, from_right)
    edge_block = jnp.where(place_in_block == 0, block - 1, block + 1)
    messages = n_tm * strips
    send_main, send_edge, recv_main, recv_edge = (sems.at[i] for i in range(4))
    swap_send, swap_recv, piece_send, piece_recv = (sems.at[i] for i in range(4, 8))
    send_2, recv_main_2 = sems.at[10], sems.at[11]
    row_send, row_recv = sems.at[12], sems.at[13]
    core, y_lo = lax.rem(tm, CORES), tm // CORES
    groups = n_tile // CORES
    y_hi, spot = tile // groups, lax.rem(tile, groups)
    partner = tm + 1 - 2 * core
    level = y_hi * CORES + y_lo
    owner_tile = core * groups + spot

    def is_me(target_tm, target_tile):
        return jnp.logical_and(target_tm == tm, target_tile == tile)

    grad_copy = pltpu.make_async_copy(grad_hbm, grad_ref, sems.at[8])
    kernel_copy = pltpu.make_async_copy(kernel_hbm, kernel_ref, sems.at[9])
    grad_copy.start()
    kernel_copy.start()

    def fetch(t):
        return pltpu.make_async_copy(x_ref.at[t], out_ref.at[t], in_sem.at[t])

    for t in range(frames):
        fetch(t).start()

    barrier = pltpu.get_barrier_semaphore()

    def hail(target_tm, target_tile):
        pl.semaphore_signal(barrier, inc=1, device_id=(target_tm, target_tile), device_id_type=MESH)

    def hail_bands(band, _):
        @pl.when(jnp.logical_not(is_me(block, band)))
        def _():
            hail(block, band)

        @pl.when(jnp.logical_and(has_edge, jnp.logical_not(is_me(edge_block, band))))
        def _():
            hail(edge_block, band)

        return 0

    lax.fori_loop(0, n_tile, hail_bands, 0)
    hail(partner, tile)

    def hail_plane(k, _):
        hail(tm, y_hi * groups + lax.rem(spot + k, groups))
        return 0

    lax.fori_loop(1, groups, hail_plane, 0)
    for k in range(n_tm):
        source = (k % CORES) * CORES + y_hi, (k // CORES) * groups + spot

        @pl.when(jnp.logical_not(is_me(*source)))
        def _():
            hail(*source)

    r, c = lane_of((LANES, LANES), 0), lane_of((LANES, LANES), 1)
    same = jnp.logical_and(r // OUT + c // OUT == STRIP - 1, lax.rem(r, OUT) == lax.rem(c, OUT))
    flip = jnp.where(same, 1.0, 0.0).astype(BF16)
    row = lane_of((FRAMES, 1), 0)
    nothing = jnp.zeros((FRAMES, LANES), F32)
    grad_copy.wait()
    flipped, halos = [], []
    for t in range(n_tm):
        rows = grad_ref[:, t].astype(F32).reshape(ROWS * FRAMES, strips * LANES).astype(BF16)
        here = [
            jnp.dot(rows[:, s * LANES : (s + 1) * LANES], flip, preferred_element_type=F32)
            .reshape(ROWS, FRAMES, LANES)
            for s in range(strips)
        ]
        flipped.append(here)
        padded = [None, None] + here + [None, None]
        halos.append([strip_halo(padded[s], padded[s + 2]) for s in range(strips + 2)])
    later = []
    for t in range(n_tm):
        later.append([
            nothing if t + 1 == n_tm else later_halo(*halos[t + 1][s]) for s in range(strips + 2)
        ])
        for s in range(strips):
            here = flipped[t][s]
            tiles = [
                jnp.where(row < EARLY, here[0], turned(here[1], EARLY, 0)),
                jnp.where(row < EARLY, here[2], turned(here[3], EARLY, 0)),
                here[4], *halos[t][s + 1],
            ]
            for i, value in enumerate(tiles):
                msg[t, s, i] = value.astype(BF16)
        for side, s in ((0, strips + 1), (1, 0)):
            for i, value in enumerate([*halos[t][s], later[t][s]]):
                emsg[side, t, i] = value.astype(BF16)

    self_main = (block == tm).astype(jnp.int32)
    to_right, to_left = tm < n_tm - 1, tm > 0
    right_tile, left_tile = (tm + 1) * strips, tm * strips - 1
    self_edge = (
        jnp.logical_and(to_right, tile == right_tile).astype(jnp.int32)
        + jnp.logical_and(to_left, tile == left_tile).astype(jnp.int32)
    )
    edges_out = n_tm * (to_right.astype(jnp.int32) + to_left.astype(jnp.int32))
    self_owner = (core == y_hi).astype(jnp.int32)
    exchange_out = messages - self_main + edges_out - self_edge
    pl.semaphore_wait(barrier, exchange_out + 1 + groups - 1 + n_tm - self_owner)

    def send(source, target, send_sem, recv_sem, target_tm, target_tile):
        own = is_me(target_tm, target_tile)

        @pl.when(jnp.logical_not(own))
        def _():
            pltpu.make_async_remote_copy(
                src_ref=source, dst_ref=target, send_sem=send_sem, recv_sem=recv_sem,
                device_id=(target_tm, target_tile), device_id_type=MESH,
            ).start()

        @pl.when(own)
        def _():
            pltpu.make_async_copy(source, target, recv_sem).start()

    def send_edges(t, _):
        @pl.when(to_right)
        def _():
            send(emsg.at[0, t], edge.at[tile], send_edge, recv_edge, t, right_tile)

        @pl.when(to_left)
        def _():
            send(emsg.at[1, t], edge.at[tile], send_edge, recv_edge, t, left_tile)

        return 0

    def send_all(source, target, send_sem, recv_sem):
        def send_one(k, _):
            turn = lax.rem(k + tile, messages)
            t, s = turn // strips, lax.rem(turn, strips)
            send(source.at[t, s], target.at[tile], send_sem, recv_sem, t, tm * strips + s)
            return 0

        lax.fori_loop(0, messages, send_one, 0)

    lax.fori_loop(0, n_tm, send_edges, 0)
    send_all(msg, recv, send_main, recv_main)

    for t in range(n_tm):
        for s in range(strips):
            here, rest = flipped[t][s], later[t][s + 1]
            if t + 1 < n_tm:
                nxt = flipped[t + 1][s]
                late = jnp.where(row < 6, turned(nxt[2], 4, 0), turned(nxt[3], 6, 0))
                late = jnp.where(row < 2, nxt[0], jnp.where(row < 4, turned(nxt[1], 2, 0), late))
                rest = jnp.where(row < 2, nxt[4], rest)
            else:
                late = nothing
            tiles = [
                jnp.where(row < EARLY, turned(here[0], EARLY, 0), here[1]),
                jnp.where(row < EARLY, turned(here[2], EARLY, 0), here[3]),
                late, rest,
            ]
            for i, value in enumerate(tiles):
                msg_2[t, s, i] = value.astype(BF16)

    kernel_copy.wait()
    weights[...] = jnp.zeros(weights.shape, BF16)
    for kt in range(3):
        taps = kernel_ref[9 * kt * OUT : 9 * (kt + 1) * OUT, :]
        taps = (0.5 * taps.astype(F32)).astype(BF16)
        weights[kt * LANES : (kt + 1) * LANES, :] = taps[:LANES]
        weights[3 * LANES + kt * OUT : 3 * LANES + (kt + 1) * OUT, :] = taps[LANES:]

    step = 8

    def silu_frame(t, _):
        fetch(t).wait()

        def silu_rows(r, _):
            half_x = 0.5 * out_ref[t, pl.ds(r * step, step)].astype(F32).reshape(step * width, cin)
            u = jnp.tanh(half_x)
            product = half_x * u
            rows = aligned(r, step * width)
            act[t, rows, :] = (half_x + product).astype(BF16)
            slope[t, rows, :] = (1.0 + u) * ((1.0 + half_x) - product)
            return 0

        lax.fori_loop(0, height // step, silu_rows, 0, unroll=4)
        return 0

    lax.fori_loop(0, EARLY, silu_frame, 0)
    send_all(msg_2, recv_2, send_2, recv_main_2)
    lax.fori_loop(EARLY, frames, silu_frame, 0)

    @pl.when(jnp.logical_not(has_edge))
    def _():
        edge[...] = jnp.zeros(edge.shape, BF16)

    @pl.when(has_edge)
    def _():
        pltpu.make_async_copy(edge, edge, recv_edge).wait()

    pltpu.make_async_copy(recv, recv, recv_main).wait()

    def unpack(b, _):
        tiles = [recv[b, i].astype(F32) for i in range(FIRST)]
        beside = tiles[3] + edge[b, 0].astype(F32)
        beside_4 = tiles[4] + edge[b, 1].astype(F32)
        for i in range(ROWS):
            at = b * ROWS + i
            field[at, 0:FRAMES] = turned(tiles[i // 2], EARLY * (i % 2), 0)
            halo[at, 0:FRAMES] = turned(beside if i < 4 else beside_4, -OUT - 2 * OUT * i, 1)
        return 0

    def unpack_2(b, _):
        tiles = [recv_2[b, i].astype(F32) for i in range(SECOND)]
        late = tiles[3] + edge[b, 2].astype(F32)
        for i in range(ROWS):
            at = b * ROWS + i
            if i < 4:
                field[at, EARLY:FRAMES] = turned(tiles[i // 2], EARLY * (1 - i % 2), 0)[EARLY:]
            field[at, FRAMES:] = turned(tiles[2], -2 * i, 0) if i < 4 else late
            halo[at, FRAMES:] = turned(turned(late, -2 if i < 4 else -4, 0), -OUT - 2 * OUT * i, 1)
        return 0

    lax.fori_loop(0, n_tile, unpack, 0, unroll=4)

    lane3, col3 = lane_of((1, width, LANES), 2), lane_of((1, width, LANES), 1)
    outside = jnp.logical_or(
        jnp.logical_and(col3 == 0, lane3 < OUT),
        jnp.logical_and(col3 == width - 1, lane3 >= LANES - OUT),
    )
    edge_rows = jnp.zeros((width, LANES), F32)
    group = 16
    for t in range(WINDOW):
        vee[t, 0:width, :] = edge_rows
        vee[t, (height + 1) * width : (height + 2) * width, :] = edge_rows

    lane2 = lane_of((1, LANES), 1)

    def tap(t, g, shift_rows, shift):
        at = pl.ds(pl.multiple_of((g * group + shift_rows) * width, width), group * width)
        return turned(vee[t % WINDOW, at, :].astype(BF16), shift, 1)

    acc[...] = jnp.zeros(acc.shape, F32)

    def add_frame(t):
        left = jnp.concatenate([cols_t[t * LANES : (t + 3) * LANES, :], last_t[t]], axis=0)
        acc[...] += jnp.dot(left, act[t], preferred_element_type=F32)

    for t in range(wide):
        if t == EARLY:
            pltpu.make_async_copy(recv_2, recv_2, recv_main_2).wait()
            lax.fori_loop(0, n_tile, unpack_2, 0, unroll=4)

        def spread(g, _, t=t):
            rows = pl.ds(g * group, group)
            main = jnp.broadcast_to(field[rows, t : t + 1, :], (group, width, LANES))
            side = jnp.broadcast_to(halo[rows, t : t + 1, :], (group, width, LANES))
            at = pl.ds(pl.multiple_of((g * group + 1) * width, width), group * width)
            values = jnp.where(outside, side, main).reshape(group * width, LANES)
            vee[t % WINDOW, at, :] = pltpu.roll(values, 0, 1, stride=OUT, stride_axis=0)
            return 0

        def fill(g, _, t=t):
            rows = aligned(g, group * width)
            s0, s1, s2 = tap(t, g, 2, 2 * OUT), tap(t, g, 1, 5 * OUT), tap(t, g, 0, 0)
            cols[t, rows, :] = jnp.where(lane2 < 3 * OUT, s0, jnp.where(lane2 < 6 * OUT, s1, s2))
            return 0

        def fill_last(g, _, t=t):
            rows = aligned(g, group * width)
            taps = [tap(t - 2 + kt, g, 0, kt * OUT) for kt in range(3)]
            value = jnp.where(lane2 < 3 * OUT, taps[2], jnp.zeros_like(taps[2]))
            last[t - 2, rows, :] = jnp.where(lane2 < OUT, taps[0], jnp.where(lane2 < 2 * OUT, taps[1], value))
            return 0

        lax.fori_loop(0, height // group, spread, 0, unroll=True)
        lax.fori_loop(0, height // group, fill, 0, unroll=True)
        cols_t[t * LANES : (t + 1) * LANES, :] = jnp.transpose(cols[t])
        if t >= 2:
            lax.fori_loop(0, height // group, fill_last, 0, unroll=True)
            last_t[t - 2] = jnp.transpose(last[t - 2])[0 : 3 * OUT]
        if t >= 3:
            add_frame(t - 3)
    add_frame(frames - 1)

    pieces_of_total = []
    for kt in range(3):
        pieces_of_total.append(acc[kt * LANES : (kt + 1) * LANES, :])
        pieces_of_total.append(acc[3 * LANES + kt * OUT : 3 * LANES + (kt + 1) * OUT, :])
    pieces_of_total.append(jnp.zeros((part.shape[1] - 27 * OUT, cin), F32))
    part[...] = jnp.transpose(jnp.concatenate(pieces_of_total, axis=0))

    chunk = 40

    def grad_frame(t, _):
        def grad_rows(r, _):
            rows = aligned(r, chunk * width)
            left = jnp.concatenate([cols[t + kt, rows, :] for kt in range(3)] + [last[t, rows, :]], axis=1)
            grad = jnp.dot(left, weights[...], preferred_element_type=F32) * slope[t, rows, :]
            out_ref[t, pl.ds(r * chunk, chunk)] = grad.reshape(chunk, width, cin).astype(BF16)
            return 0

        lax.fori_loop(0, height // chunk, grad_rows, 0, unroll=True)
        return 0

    rows = mine.shape[0]
    share = rows // groups
    swap = pltpu.make_async_remote_copy(
        src_ref=part.at[aligned(1 - core, rows)], dst_ref=mine,
        send_sem=swap_send, recv_sem=swap_recv,
        device_id=(partner, tile), device_id_type=MESH,
    )
    swap.start()
    lax.fori_loop(0, SPLIT[0], grad_frame, 0)
    swap.wait()
    mine[...] += part[aligned(core, rows), :]

    mine_half[...] = mine[...].astype(BF16)

    def send_piece(k, _):
        g = lax.rem(spot + k, groups)
        pltpu.make_async_remote_copy(
            src_ref=mine_half.at[aligned(g, share)], dst_ref=pieces.at[spot],
            send_sem=piece_send, recv_sem=piece_recv,
            device_id=(tm, y_hi * groups + g), device_id_type=MESH,
        ).start()
        return 0

    lax.fori_loop(1, groups, send_piece, 0)
    pieces[spot] = mine_half[aligned(spot, share), :]
    lax.fori_loop(SPLIT[0], SPLIT[1], grad_frame, 0)
    others = pieces.at[pl.ds(0, groups - 1)]
    pltpu.make_async_copy(others, others, piece_recv).wait()
    sums[...] = jnp.sum(pieces[...].astype(F32), axis=0)

    for k in range(n_tm):
        send(sums, quads.at[level], row_send, row_recv, k, owner_tile)
    lax.fori_loop(SPLIT[1], frames, grad_frame, 0)
    pltpu.make_async_copy(quads, quads, row_recv).wait()

    def drain(source, sem, times):
        def one(k, _):
            pltpu.make_async_copy(source, source, sem).wait()
            return 0

        lax.fori_loop(0, times, one, 0)

    drain(msg.at[0, 0], send_main, messages - self_main)
    drain(emsg.at[0, 0], send_edge, edges_out - self_edge)
    drain(msg_2.at[0, 0], send_2, messages - self_main)
    drain(pieces.at[0], piece_send, groups - 1)
    drain(sums, row_send, n_tm - self_owner)
    result = quads[0]
    for k in range(1, n_tm):
        result = result + quads[k]
    kgrad_ref[...] = (result * scale)[:, : kgrad_ref.shape[1]]


SPLIT = (1, 7)


def on_device(n_tm, n_tile, scale, latent_grad, section_input, kernel):
    frames, height, width, cin = section_input.shape
    taps = kernel.shape[1]
    strips = n_tile // n_tm
    banded = jnp.transpose(latent_grad, (1, 0, 2)).reshape(ROWS, n_tm, FRAMES, strips * LANES)
    wide, count = frames + 2, height * width
    rows, share, padded = cin // CORES, cin // n_tile, 4 * LANES
    vmem = pl.BlockSpec(memory_space=pltpu.VMEM)
    return pl.pallas_call(
        functools.partial(whole, n_tm, n_tile, scale),
        out_shape=(
            pltpu.VMEM((frames, height, width, cin), BF16),
            jax.ShapeDtypeStruct((share, taps), F32),
        ),
        in_specs=[pl.BlockSpec(memory_space=pl.ANY)] * 3,
        out_specs=(vmem, vmem),
        scratch_shapes=[
            pltpu.VMEM((ROWS, n_tm, FRAMES, strips * LANES), BF16),
            pltpu.VMEM((taps, cin), BF16),
            pltpu.VMEM((n_tm, strips, FIRST, FRAMES, LANES), BF16),
            pltpu.VMEM((n_tm, strips, SECOND, FRAMES, LANES), BF16),
            pltpu.VMEM((2, n_tm, 3, FRAMES, LANES), BF16),
            pltpu.VMEM((n_tile, FIRST, FRAMES, LANES), BF16),
            pltpu.VMEM((n_tile, SECOND, FRAMES, LANES), BF16),
            pltpu.VMEM((n_tile, 3, FRAMES, LANES), BF16),
            pltpu.VMEM((frames, count, cin), BF16),
            pltpu.VMEM((frames, count, cin), F32),
            pltpu.VMEM((height, 2 * FRAMES, LANES), F32),
            pltpu.VMEM((height, 2 * FRAMES, LANES), F32),
            pltpu.VMEM((WINDOW, (height + 2) * width, LANES), F32),
            pltpu.VMEM((wide, count, LANES), BF16),
            pltpu.VMEM((wide * LANES, count), BF16),
            pltpu.VMEM((frames, count, LANES), BF16),
            pltpu.VMEM((frames, 3 * OUT, count), BF16),
            pltpu.VMEM((padded, cin), BF16),
            pltpu.VMEM((27 * OUT, cin), F32),
            pltpu.VMEM((cin, padded), F32),
            pltpu.VMEM((rows, padded), F32),
            pltpu.VMEM((rows, padded), BF16),
            pltpu.VMEM((n_tile // CORES, share, padded), BF16),
            pltpu.VMEM((share, padded), F32),
            pltpu.VMEM((n_tm, share, padded), F32),
            pltpu.SemaphoreType.DMA((frames,)),
            pltpu.SemaphoreType.DMA((16,)),
        ],
        compiler_params=pltpu.CompilerParams(
            collective_id=0, has_side_effects=True, vmem_limit_bytes=VMEM_LIMIT
        ),
    )(banded, section_input, jnp.transpose(kernel))


VMEM_LIMIT = 53 << 20


def solution(mesh):
    n_tm, n_tile = mesh.shape["tm"], mesh.shape["tile"]
    positions = n_tm * FRAMES * n_tile * ROWS * n_tile * STRIP
    return jax.shard_map(
        functools.partial(on_device, n_tm, n_tile, 1.0 / math.sqrt(positions)),
        mesh=mesh,
        in_specs=(P(None, "tile", "tm"), P("tm", None, "tile", None), P()),
        out_specs=(P("tm", None, "tile", None), P("tile", None)),
        check_vma=False,
    )
```

```python
import functools
import math

import jax
import jax.numpy as jnp
from jax import lax
from jax.experimental import pallas as pl
from jax.experimental.pallas import tpu as pltpu
from jax.sharding import PartitionSpec as P

MESH = pl.DeviceIdType.MESH
F32, BF16 = jnp.float32, jnp.bfloat16
LANES = 128
OUT = 16
STRIP = 8
FRAMES = 8
ROWS = 5
FIRST = 5
SECOND = 4
EARLY = 4
CORES = 2
WINDOW = 3


def lane_of(shape, axis):
    return lax.broadcasted_iota(jnp.int32, shape, axis)


def aligned(index, size):
    return pl.ds(pl.multiple_of(index * size, size), size)


def turned(value, shift, axis):
    shift %= value.shape[axis]
    return pltpu.roll(value, shift, axis) if shift else value


def wrapped(index, size):
    return jnp.where(index >= size, index - size, index)


def strip_halo(left, right):
    lane = lane_of((1, LANES), 1)
    rows = []
    for i in range(ROWS):
        value = jnp.zeros((FRAMES, LANES), F32)
        if right is not None:
            value = jnp.where(lane >= LANES - OUT, right[i], value)
        if left is not None:
            value = jnp.where(lane < OUT, left[i], value)
        rows.append(turned(value, OUT + 2 * OUT * i, 1))
    return rows[0] + rows[1] + rows[2] + rows[3], rows[4]


def later_halo(first, second):
    row = lane_of((FRAMES, 1), 0)
    value = jnp.where(row < 6, turned(second, 4, 0), 0.0)
    return jnp.where(row < 2, 0.0, jnp.where(row < 4, turned(first, 2, 0), value))


def whole(
    n_tm, n_tile, scale, grad_hbm, x_ref, kernel_hbm, out_ref, kgrad_ref,
    grad_ref, kernel_ref, msg, msg_2, emsg, recv, recv_2, edge, act, slope, field, halo, vee, cols, cols_t, last, last_t,
    weights, acc, part, mine, mine_half, pieces, sums, quads, in_sem, sems,
):
    frames, height, width, cin = out_ref.shape
    wide, count = frames + 2, height * width
    tm, tile = lax.axis_index("tm"), lax.axis_index("tile")
    strips = n_tile // n_tm
    block = tile // strips
    place_in_block = lax.rem(tile, strips)
    from_left = jnp.logical_and(place_in_block == 0, block > 0)
    from_right = jnp.logical_and(place_in_block == strips - 1, block < n_tm - 1)
    has_edge = jnp.logical_or(from_left, from_right)
    edge_block = jnp.where(place_in_block == 0, block - 1, block + 1)
    messages = n_tm * strips
    send_main, send_edge, recv_main, recv_edge = (sems.at[i] for i in range(4))
    swap_send, swap_recv, piece_send, piece_recv = (sems.at[i] for i in range(4, 8))
    send_2, recv_main_2 = sems.at[10], sems.at[11]
    row_send, row_recv = sems.at[12], sems.at[13]
    core, y_lo = lax.rem(tm, CORES), tm // CORES
    groups = n_tile // CORES
    y_hi, spot = tile // groups, lax.rem(tile, groups)
    partner = tm + 1 - 2 * core
    level = y_hi * CORES + y_lo
    owner_tile = core * groups + spot

    def is_me(target_tm, target_tile):
        return jnp.logical_and(target_tm == tm, target_tile == tile)

    grad_copy = pltpu.make_async_copy(grad_hbm, grad_ref, sems.at[8])
    kernel_copy = pltpu.make_async_copy(kernel_hbm, kernel_ref, sems.at[9])
    grad_copy.start()
    kernel_copy.start()

    def fetch(t):
        return pltpu.make_async_copy(x_ref.at[t], out_ref.at[t], in_sem.at[t])

    for t in range(frames):
        fetch(t).start()

    barrier = pltpu.get_barrier_semaphore()

    def hail(target_tm, target_tile):
        pl.semaphore_signal(barrier, inc=1, device_id=(target_tm, target_tile), device_id_type=MESH)

    for k in range(1, n_tile):
        hail(block, wrapped(tile + k, n_tile))

    @pl.when(block != tm)
    def _():
        hail(block, tile)

    @pl.when(has_edge)
    def _():
        for k in range(1, n_tile):
            hail(edge_block, wrapped(tile + k, n_tile))

        @pl.when(edge_block != tm)
        def _():
            hail(edge_block, tile)

    hail(partner, tile)
    for k in range(1, groups):
        hail(tm, y_hi * groups + wrapped(spot + k, groups))
    for k in range(n_tm):
        source = (k % CORES) * CORES + y_hi, (k // CORES) * groups + spot

        @pl.when(jnp.logical_not(is_me(*source)))
        def _():
            hail(*source)

    r, c = lane_of((LANES, LANES), 0), lane_of((LANES, LANES), 1)
    same = jnp.logical_and(r // OUT + c // OUT == STRIP - 1, lax.rem(r, OUT) == lax.rem(c, OUT))
    flip = jnp.where(same, 1.0, 0.0).astype(BF16)
    row = lane_of((FRAMES, 1), 0)
    nothing = jnp.zeros((FRAMES, LANES), F32)
    grad_copy.wait()
    flipped, halos = [], []
    for t in range(n_tm):
        rows = grad_ref[:, t].astype(F32).reshape(ROWS * FRAMES, strips * LANES).astype(BF16)
        here = [
            jnp.dot(rows[:, s * LANES : (s + 1) * LANES], flip, preferred_element_type=F32)
            .reshape(ROWS, FRAMES, LANES)
            for s in range(strips)
        ]
        flipped.append(here)
        padded = [None, None] + here + [None, None]
        halos.append([strip_halo(padded[s], padded[s + 2]) for s in range(strips + 2)])
    later = []
    for t in range(n_tm):
        later.append([
            nothing if t + 1 == n_tm else later_halo(*halos[t + 1][s]) for s in range(strips + 2)
        ])
        for s in range(strips):
            here = flipped[t][s]
            tiles = [
                jnp.where(row < EARLY, here[0], turned(here[1], EARLY, 0)),
                jnp.where(row < EARLY, here[2], turned(here[3], EARLY, 0)),
                here[4], *halos[t][s + 1],
            ]
            for i, value in enumerate(tiles):
                msg[t, s, i] = value.astype(BF16)
        for side, s in ((0, strips + 1), (1, 0)):
            for i, value in enumerate([*halos[t][s], later[t][s]]):
                emsg[side, t, i] = value.astype(BF16)

    self_main = (block == tm).astype(jnp.int32)
    to_right, to_left = tm < n_tm - 1, tm > 0
    right_tile, left_tile = (tm + 1) * strips, tm * strips - 1
    self_edge = (
        jnp.logical_and(to_right, tile == right_tile).astype(jnp.int32)
        + jnp.logical_and(to_left, tile == left_tile).astype(jnp.int32)
    )
    edges_out = n_tm * (to_right.astype(jnp.int32) + to_left.astype(jnp.int32))
    self_owner = (core == y_hi).astype(jnp.int32)
    exchange_out = messages - self_main + edges_out - self_edge
    pl.semaphore_wait(barrier, exchange_out + 1 + groups - 1 + n_tm - self_owner)

    def send(source, target, send_sem, recv_sem, target_tm, target_tile):
        own = is_me(target_tm, target_tile)

        @pl.when(jnp.logical_not(own))
        def _():
            pltpu.make_async_remote_copy(
                src_ref=source, dst_ref=target, send_sem=send_sem, recv_sem=recv_sem,
                device_id=(target_tm, target_tile), device_id_type=MESH,
            ).start()

        @pl.when(own)
        def _():
            pltpu.make_async_copy(source, target, recv_sem).start()

    def send_edges(t, _):
        @pl.when(to_right)
        def _():
            send(emsg.at[0, t], edge.at[tile], send_edge, recv_edge, t, right_tile)

        @pl.when(to_left)
        def _():
            send(emsg.at[1, t], edge.at[tile], send_edge, recv_edge, t, left_tile)

        return 0

    def send_all(source, target, send_sem, recv_sem):
        for k in range(messages):
            t, s = wrapped(tm + k // strips, n_tm), wrapped(place_in_block + k % strips, strips)
            if k == 0:
                send(source.at[t, s], target.at[tile], send_sem, recv_sem, t, tm * strips + s)
            else:
                pltpu.make_async_remote_copy(
                    src_ref=source.at[t, s], dst_ref=target.at[tile], send_sem=send_sem, recv_sem=recv_sem,
                    device_id=(t, tm * strips + s), device_id_type=MESH,
                ).start()

    lax.fori_loop(0, n_tm, send_edges, 0)
    send_all(msg, recv, send_main, recv_main)

    for t in range(n_tm):
        for s in range(strips):
            here, rest = flipped[t][s], later[t][s + 1]
            if t + 1 < n_tm:
                nxt = flipped[t + 1][s]
                late = jnp.where(row < 6, turned(nxt[2], 4, 0), turned(nxt[3], 6, 0))
                late = jnp.where(row < 2, nxt[0], jnp.where(row < 4, turned(nxt[1], 2, 0), late))
                rest = jnp.where(row < 2, nxt[4], rest)
            else:
                late = nothing
            tiles = [
                jnp.where(row < EARLY, turned(here[0], EARLY, 0), here[1]),
                jnp.where(row < EARLY, turned(here[2], EARLY, 0), here[3]),
                late, rest,
            ]
            for i, value in enumerate(tiles):
                msg_2[t, s, i] = value.astype(BF16)

    kernel_copy.wait()
    weights[...] = jnp.zeros(weights.shape, BF16)
    for kt in range(3):
        taps = kernel_ref[9 * kt * OUT : 9 * (kt + 1) * OUT, :]
        taps = (0.5 * taps.astype(F32)).astype(BF16)
        weights[kt * LANES : (kt + 1) * LANES, :] = taps[:LANES]
        weights[3 * LANES + kt * OUT : 3 * LANES + (kt + 1) * OUT, :] = taps[LANES:]

    step = 8

    def silu_frame(t, _):
        fetch(t).wait()

        def silu_rows(r, _):
            half_x = 0.5 * out_ref[t, pl.ds(r * step, step)].astype(F32).reshape(step * width, cin)
            u = jnp.tanh(half_x)
            more = 1.0 + u
            value = half_x * more
            rows = aligned(r, step * width)
            act[t, rows, :] = value.astype(BF16)
            slope[t, rows, :] = more + value * (1.0 - u)
            return 0

        lax.fori_loop(0, height // step, silu_rows, 0, unroll=4)
        return 0

    lax.fori_loop(0, EARLY, silu_frame, 0)
    send_all(msg_2, recv_2, send_2, recv_main_2)
    lax.fori_loop(EARLY, frames, silu_frame, 0)

    @pl.when(jnp.logical_not(has_edge))
    def _():
        edge[...] = jnp.zeros(edge.shape, BF16)

    @pl.when(has_edge)
    def _():
        pltpu.make_async_copy(edge, edge, recv_edge).wait()

    pltpu.make_async_copy(recv, recv, recv_main).wait()

    def unpack(b, _):
        tiles = [recv[b, i].astype(F32) for i in range(FIRST)]
        beside = tiles[3] + edge[b, 0].astype(F32)
        beside_4 = tiles[4] + edge[b, 1].astype(F32)
        for i in range(ROWS):
            at = b * ROWS + i
            field[at, 0:FRAMES] = turned(tiles[i // 2], EARLY * (i % 2), 0)
            halo[at, 0:FRAMES] = turned(beside if i < 4 else beside_4, -OUT - 2 * OUT * i, 1)
        return 0

    def unpack_2(b, _):
        tiles = [recv_2[b, i].astype(F32) for i in range(SECOND)]
        late = tiles[3] + edge[b, 2].astype(F32)
        for i in range(ROWS):
            at = b * ROWS + i
            if i < 4:
                field[at, EARLY:FRAMES] = turned(tiles[i // 2], EARLY * (1 - i % 2), 0)[EARLY:]
            field[at, FRAMES:] = turned(tiles[2], -2 * i, 0) if i < 4 else late
            halo[at, FRAMES:] = turned(turned(late, -2 if i < 4 else -4, 0), -OUT - 2 * OUT * i, 1)
        return 0

    lax.fori_loop(0, n_tile, unpack, 0, unroll=4)

    lane3, col3 = lane_of((1, width, LANES), 2), lane_of((1, width, LANES), 1)
    outside = jnp.logical_or(
        jnp.logical_and(col3 == 0, lane3 < OUT),
        jnp.logical_and(col3 == width - 1, lane3 >= LANES - OUT),
    )
    edge_rows = jnp.zeros((width, LANES), F32)
    group = 16
    for t in range(WINDOW):
        vee[t, 0:width, :] = edge_rows
        vee[t, (height + 1) * width : (height + 2) * width, :] = edge_rows

    lane2 = lane_of((1, LANES), 1)

    def tap(t, g, shift_rows, shift):
        at = pl.ds(pl.multiple_of((g * group + shift_rows) * width, width), group * width)
        return turned(vee[t % WINDOW, at, :].astype(BF16), shift, 1)

    acc[...] = jnp.zeros(acc.shape, F32)

    def add_frame(t):
        left = jnp.concatenate([cols_t[t * LANES : (t + 3) * LANES, :], last_t[t]], axis=0)
        acc[...] += jnp.dot(left, act[t], preferred_element_type=F32)

    for t in range(wide):
        if t == EARLY:
            pltpu.make_async_copy(recv_2, recv_2, recv_main_2).wait()
            lax.fori_loop(0, n_tile, unpack_2, 0, unroll=4)

        def spread(g, _, t=t):
            rows = pl.ds(g * group, group)
            main = jnp.broadcast_to(field[rows, t : t + 1, :], (group, width, LANES))
            side = jnp.broadcast_to(halo[rows, t : t + 1, :], (group, width, LANES))
            at = pl.ds(pl.multiple_of((g * group + 1) * width, width), group * width)
            values = jnp.where(outside, side, main).reshape(group * width, LANES)
            vee[t % WINDOW, at, :] = pltpu.roll(values, 0, 1, stride=OUT, stride_axis=0)
            return 0

        def fill(g, _, t=t):
            rows = aligned(g, group * width)
            s0, s1, s2 = tap(t, g, 2, 2 * OUT), tap(t, g, 1, 5 * OUT), tap(t, g, 0, 0)
            cols[t, rows, :] = jnp.where(lane2 < 3 * OUT, s0, jnp.where(lane2 < 6 * OUT, s1, s2))
            return 0

        def fill_last(g, _, t=t):
            rows = aligned(g, group * width)
            taps = [tap(t - 2 + kt, g, 0, kt * OUT) for kt in range(3)]
            value = jnp.where(lane2 < 3 * OUT, taps[2], jnp.zeros_like(taps[2]))
            last[t - 2, rows, :] = jnp.where(lane2 < OUT, taps[0], jnp.where(lane2 < 2 * OUT, taps[1], value))
            return 0

        lax.fori_loop(0, height // group, spread, 0, unroll=True)
        lax.fori_loop(0, height // group, fill, 0, unroll=True)
        cols_t[t * LANES : (t + 1) * LANES, :] = jnp.transpose(cols[t])
        if t >= 2:
            lax.fori_loop(0, height // group, fill_last, 0, unroll=True)
            last_t[t - 2] = jnp.transpose(last[t - 2])[0 : 3 * OUT]
        if t >= 3:
            add_frame(t - 3)
    add_frame(frames - 1)

    pieces_of_total = []
    for kt in range(3):
        pieces_of_total.append(acc[kt * LANES : (kt + 1) * LANES, :])
        pieces_of_total.append(acc[3 * LANES + kt * OUT : 3 * LANES + (kt + 1) * OUT, :])
    pieces_of_total.append(jnp.zeros((part.shape[1] - 27 * OUT, cin), F32))
    part[...] = jnp.transpose(jnp.concatenate(pieces_of_total, axis=0))

    chunk = 40

    def grad_frame(t, _):
        def grad_rows(r, _):
            rows = aligned(r, chunk * width)
            left = jnp.concatenate([cols[t + kt, rows, :] for kt in range(3)] + [last[t, rows, :]], axis=1)
            grad = jnp.dot(left, weights[...], preferred_element_type=F32) * slope[t, rows, :]
            out_ref[t, pl.ds(r * chunk, chunk)] = grad.reshape(chunk, width, cin).astype(BF16)
            return 0

        lax.fori_loop(0, height // chunk, grad_rows, 0, unroll=True)
        return 0

    def drain(source, sem):
        pltpu.make_async_copy(source, source, sem).wait()

    def drain_messages(source, sem):
        if n_tm > 1:
            drain(source.at[pl.ds(0, n_tm - 1)], sem)
        if strips > 1:
            drain(source.at[0, pl.ds(0, strips - 1)], sem)

        @pl.when(block != tm)
        def _():
            drain(source.at[0, 0], sem)

    drain_messages(msg, send_main)
    drain_messages(msg_2, send_2)

    def drain_edge(k, _):
        drain(emsg.at[0, 0], send_edge)
        return 0

    lax.fori_loop(0, edges_out - self_edge, drain_edge, 0)

    rows = mine.shape[0]
    share = rows // groups
    swap = pltpu.make_async_remote_copy(
        src_ref=part.at[aligned(1 - core, rows)], dst_ref=mine,
        send_sem=swap_send, recv_sem=swap_recv,
        device_id=(partner, tile), device_id_type=MESH,
    )
    swap.start()
    lax.fori_loop(0, SPLIT[0], grad_frame, 0)
    swap.wait()
    mine[...] += part[aligned(core, rows), :]

    mine_half[...] = mine[...].astype(BF16)

    for k in range(1, groups):
        g = wrapped(spot + k, groups)
        pltpu.make_async_remote_copy(
            src_ref=mine_half.at[aligned(g, share)], dst_ref=pieces.at[spot],
            send_sem=piece_send, recv_sem=piece_recv,
            device_id=(tm, y_hi * groups + g), device_id_type=MESH,
        ).start()
    pieces[spot] = mine_half[aligned(spot, share), :]
    lax.fori_loop(SPLIT[0], SPLIT[1], grad_frame, 0)
    others = pieces.at[pl.ds(0, groups - 1)]
    pltpu.make_async_copy(others, others, piece_recv).wait()
    sums[...] = jnp.sum(pieces[...].astype(F32), axis=0)

    for k in range(n_tm):
        send(sums, quads.at[level], row_send, row_recv, k, owner_tile)
    lax.fori_loop(SPLIT[1], frames, grad_frame, 0)
    pltpu.make_async_copy(quads, quads, row_recv).wait()

    drain(others, piece_send)
    drain(quads.at[pl.ds(0, n_tm - 1)], row_send)

    @pl.when(core != y_hi)
    def _():
        drain(sums, row_send)

    result = quads[0]
    for k in range(1, n_tm):
        result = result + quads[k]
    kgrad_ref[...] = (result * scale)[:, : kgrad_ref.shape[1]]


SPLIT = (1, 7)


def write_out(grad_ref, kgrad_ref, grad_out, kgrad_out, sem):
    frames, height = grad_ref.shape[:2]
    copies = [pltpu.make_async_copy(kgrad_ref, kgrad_out, sem.at[2 * frames])]
    for i in range(2 * frames):
        place = (i // 2, pl.ds((i % 2) * (height // 2), height // 2))
        copies.append(pltpu.make_async_copy(grad_ref.at[place], grad_out.at[place], sem.at[i]))
    for copy in copies:
        copy.start()
    for copy in copies:
        copy.wait()


def on_device(n_tm, n_tile, scale, latent_grad, section_input, kernel):
    frames, height, width, cin = section_input.shape
    taps = kernel.shape[1]
    strips = n_tile // n_tm
    banded = jnp.transpose(latent_grad, (1, 0, 2)).reshape(ROWS, n_tm, FRAMES, strips * LANES)
    wide, count = frames + 2, height * width
    rows, share, padded = cin // CORES, cin // n_tile, 4 * LANES
    vmem = pl.BlockSpec(memory_space=pltpu.VMEM)
    results = pl.pallas_call(
        functools.partial(whole, n_tm, n_tile, scale),
        out_shape=(
            pltpu.VMEM((frames, height, width, cin), BF16),
            pltpu.VMEM((share, taps), F32),
        ),
        in_specs=[pl.BlockSpec(memory_space=pl.ANY)] * 3,
        out_specs=(vmem, vmem),
        scratch_shapes=[
            pltpu.VMEM((ROWS, n_tm, FRAMES, strips * LANES), BF16),
            pltpu.VMEM((taps, cin), BF16),
            pltpu.VMEM((n_tm, strips, FIRST, FRAMES, LANES), BF16),
            pltpu.VMEM((n_tm, strips, SECOND, FRAMES, LANES), BF16),
            pltpu.VMEM((2, n_tm, 3, FRAMES, LANES), BF16),
            pltpu.VMEM((n_tile, FIRST, FRAMES, LANES), BF16),
            pltpu.VMEM((n_tile, SECOND, FRAMES, LANES), BF16),
            pltpu.VMEM((n_tile, 3, FRAMES, LANES), BF16),
            pltpu.VMEM((frames, count, cin), BF16),
            pltpu.VMEM((frames, count, cin), F32),
            pltpu.VMEM((height, 2 * FRAMES, LANES), F32),
            pltpu.VMEM((height, 2 * FRAMES, LANES), F32),
            pltpu.VMEM((WINDOW, (height + 2) * width, LANES), F32),
            pltpu.VMEM((wide, count, LANES), BF16),
            pltpu.VMEM((wide * LANES, count), BF16),
            pltpu.VMEM((frames, count, LANES), BF16),
            pltpu.VMEM((frames, 3 * OUT, count), BF16),
            pltpu.VMEM((padded, cin), BF16),
            pltpu.VMEM((27 * OUT, cin), F32),
            pltpu.VMEM((cin, padded), F32),
            pltpu.VMEM((rows, padded), F32),
            pltpu.VMEM((rows, padded), BF16),
            pltpu.VMEM((n_tile // CORES, share, padded), BF16),
            pltpu.VMEM((share, padded), F32),
            pltpu.VMEM((n_tm, share, padded), F32),
            pltpu.SemaphoreType.DMA((frames,)),
            pltpu.SemaphoreType.DMA((16,)),
        ],
        compiler_params=pltpu.CompilerParams(
            collective_id=0, has_side_effects=True, vmem_limit_bytes=VMEM_LIMIT
        ),
    )(banded, section_input, jnp.transpose(kernel))
    return pl.pallas_call(
        write_out,
        out_shape=(
            jax.ShapeDtypeStruct((frames, height, width, cin), BF16),
            jax.ShapeDtypeStruct((share, taps), F32),
        ),
        in_specs=[vmem, vmem],
        out_specs=[pl.BlockSpec(memory_space=pl.ANY)] * 2,
        scratch_shapes=[pltpu.SemaphoreType.DMA((2 * frames + 1,))],
    )(*results)


VMEM_LIMIT = 53 << 20


def solution(mesh):
    n_tm, n_tile = mesh.shape["tm"], mesh.shape["tile"]
    positions = n_tm * FRAMES * n_tile * ROWS * n_tile * STRIP
    return jax.shard_map(
        functools.partial(on_device, n_tm, n_tile, 1.0 / math.sqrt(positions)),
        mesh=mesh,
        in_specs=(P(None, "tile", "tm"), P("tm", None, "tile", None), P()),
        out_specs=(P("tm", None, "tile", None), P("tile", None)),
        check_vma=False,
    )
```

```python
import functools
import math

import jax
import jax.numpy as jnp
from jax import lax
from jax.experimental import pallas as pl
from jax.experimental.pallas import tpu as pltpu
from jax.sharding import PartitionSpec as P

MESH = pl.DeviceIdType.MESH
F32, BF16 = jnp.float32, jnp.bfloat16
LANES = 128
OUT = 16
STRIP = 8
FRAMES = 8
ROWS = 5
FIRST = 4
SECOND = 3
EARLY = 4
CORES = 2
WINDOW = 3


def lane_of(shape, axis):
    return lax.broadcasted_iota(jnp.int32, shape, axis)


def aligned(index, size):
    return pl.ds(pl.multiple_of(index * size, size), size)


def turned(value, shift, axis):
    shift %= value.shape[axis]
    return pltpu.roll(value, shift, axis) if shift else value


def wrapped(index, size):
    return jnp.where(index >= size, index - size, index)


def strip_halo(left, right):
    lane = lane_of((1, LANES), 1)
    rows = []
    for i in range(ROWS):
        value = jnp.zeros((FRAMES, LANES), F32)
        if right is not None:
            value = jnp.where(lane >= LANES - OUT, right[i], value)
        if left is not None:
            value = jnp.where(lane < OUT, left[i], value)
        rows.append(turned(value, OUT + 2 * OUT * i, 1))
    return rows[0] + rows[1] + rows[2] + rows[3], rows[4]


def joined(upper, lower, turn_upper=False, turn_lower=False):
    upper = turned(upper, EARLY, 0) if turn_upper else upper
    lower = turned(lower, EARLY, 0) if turn_lower else lower
    return jnp.where(lane_of((FRAMES, 1), 0) < EARLY, upper, lower)


def whole(
    n_tm, n_tile, scale, grad_hbm, x_ref, kernel_hbm, out_ref, kgrad_ref,
    grad_ref, kernel_ref, msg, msg_2, emsg, recv, recv_2, edge, lead, ahead, act, slope, field, halo, vee, cols, cols_t, last, last_t,
    weights, acc, part, mine, mine_half, pieces, sums, quads, in_sem, sems,
):
    frames, height, width, cin = out_ref.shape
    wide, count = frames + 2, height * width
    tm, tile = lax.axis_index("tm"), lax.axis_index("tile")
    strips = n_tile // n_tm
    block = tile // strips
    place_in_block = lax.rem(tile, strips)
    from_left = jnp.logical_and(place_in_block == 0, block > 0)
    from_right = jnp.logical_and(place_in_block == strips - 1, block < n_tm - 1)
    has_edge = jnp.logical_or(from_left, from_right)
    edge_block = jnp.where(place_in_block == 0, block - 1, block + 1)
    messages = n_tm * strips
    send_main, send_edge, recv_main, recv_edge = (sems.at[i] for i in range(4))
    swap_send, swap_recv, piece_send, piece_recv = (sems.at[i] for i in range(4, 8))
    send_2, recv_main_2 = sems.at[10], sems.at[11]
    row_send, row_recv = sems.at[12], sems.at[13]
    lead_send, lead_recv = sems.at[14], sems.at[15]
    core, y_lo = lax.rem(tm, CORES), tm // CORES
    groups = n_tile // CORES
    y_hi, spot = tile // groups, lax.rem(tile, groups)
    partner = tm + 1 - 2 * core
    level = y_hi * CORES + y_lo
    owner_tile = core * groups + spot

    def is_me(target_tm, target_tile):
        return jnp.logical_and(target_tm == tm, target_tile == tile)

    grad_copy = pltpu.make_async_copy(grad_hbm, grad_ref, sems.at[8])
    kernel_copy = pltpu.make_async_copy(kernel_hbm, kernel_ref, sems.at[9])
    grad_copy.start()
    kernel_copy.start()

    def fetch(t):
        return pltpu.make_async_copy(x_ref.at[t], out_ref.at[t], in_sem.at[t])

    for t in range(frames):
        fetch(t).start()

    barrier = pltpu.get_barrier_semaphore()

    def hail(target_tm, target_tile):
        pl.semaphore_signal(barrier, inc=1, device_id=(target_tm, target_tile), device_id_type=MESH)

    for k in range(1, n_tile):
        hail(block, wrapped(tile + k, n_tile))

    @pl.when(block != tm)
    def _():
        hail(block, tile)

    @pl.when(has_edge)
    def _():
        for k in range(1, n_tile):
            hail(edge_block, wrapped(tile + k, n_tile))

        @pl.when(edge_block != tm)
        def _():
            hail(edge_block, tile)

    @pl.when(tm < n_tm - 1)
    def _():
        hail(tm + 1, tile)

    hail(partner, tile)
    for k in range(1, groups):
        hail(tm, y_hi * groups + wrapped(spot + k, groups))
    for k in range(n_tm):
        source = (k % CORES) * CORES + y_hi, (k // CORES) * groups + spot

        @pl.when(jnp.logical_not(is_me(*source)))
        def _():
            hail(*source)

    r, c = lane_of((LANES, LANES), 0), lane_of((LANES, LANES), 1)
    same = jnp.logical_and(r // OUT + c // OUT == STRIP - 1, lax.rem(r, OUT) == lax.rem(c, OUT))
    flip = jnp.where(same, 1.0, 0.0).astype(BF16)
    row = lane_of((FRAMES, 1), 0)
    nothing = jnp.zeros((FRAMES, LANES), F32)
    grad_copy.wait()
    flipped, halos = [], []
    for t in range(n_tm):
        rows = grad_ref[:, t].astype(F32).reshape(ROWS * FRAMES, strips * LANES).astype(BF16)
        here = [
            jnp.dot(rows[:, s * LANES : (s + 1) * LANES], flip, preferred_element_type=F32)
            .reshape(ROWS, FRAMES, LANES)
            for s in range(strips)
        ]
        flipped.append(here)
        padded = [None, None] + here + [None, None]
        halos.append([strip_halo(padded[s], padded[s + 2]) for s in range(strips + 2)])
    for t in range(n_tm):
        for s in range(strips):
            here, (first, second) = flipped[t][s], halos[t][s + 1]
            tiles = [
                joined(here[0], here[1], False, True), joined(here[2], here[3], False, True),
                joined(here[4], first, False, True), joined(second, here[4]),
            ]
            for i, value in enumerate(tiles):
                msg[t, s, i] = value.astype(BF16)
        for side, s in ((0, strips + 1), (1, 0)):
            for i, value in enumerate(halos[t][s]):
                emsg[side, t, i] = value.astype(BF16)

    self_main = (block == tm).astype(jnp.int32)
    to_right, to_left = tm < n_tm - 1, tm > 0
    right_tile, left_tile = (tm + 1) * strips, tm * strips - 1
    self_edge = (
        jnp.logical_and(to_right, tile == right_tile).astype(jnp.int32)
        + jnp.logical_and(to_left, tile == left_tile).astype(jnp.int32)
    )
    edges_out = n_tm * (to_right.astype(jnp.int32) + to_left.astype(jnp.int32))
    self_owner = (core == y_hi).astype(jnp.int32)
    exchange_out = messages - self_main + edges_out - self_edge
    pl.semaphore_wait(barrier, exchange_out + 1 + groups - 1 + n_tm - self_owner + to_left.astype(jnp.int32))

    def send(source, target, send_sem, recv_sem, target_tm, target_tile):
        own = is_me(target_tm, target_tile)

        @pl.when(jnp.logical_not(own))
        def _():
            pltpu.make_async_remote_copy(
                src_ref=source, dst_ref=target, send_sem=send_sem, recv_sem=recv_sem,
                device_id=(target_tm, target_tile), device_id_type=MESH,
            ).start()

        @pl.when(own)
        def _():
            pltpu.make_async_copy(source, target, recv_sem).start()

    def send_edges(t, _):
        @pl.when(to_right)
        def _():
            send(emsg.at[0, t], edge.at[tile], send_edge, recv_edge, t, right_tile)

        @pl.when(to_left)
        def _():
            send(emsg.at[1, t], edge.at[tile], send_edge, recv_edge, t, left_tile)

        return 0

    def send_all(source, target, send_sem, recv_sem):
        for k in range(messages):
            t, s = wrapped(tm + k // strips, n_tm), wrapped(place_in_block + k % strips, strips)
            if k == 0:
                send(source.at[t, s], target.at[tile], send_sem, recv_sem, t, tm * strips + s)
            else:
                pltpu.make_async_remote_copy(
                    src_ref=source.at[t, s], dst_ref=target.at[tile], send_sem=send_sem, recv_sem=recv_sem,
                    device_id=(t, tm * strips + s), device_id_type=MESH,
                ).start()

    lax.fori_loop(0, n_tm, send_edges, 0)
    send_all(msg, recv, send_main, recv_main)

    for t in range(n_tm):
        for s in range(strips):
            here, (first, second) = flipped[t][s], halos[t][s + 1]
            tiles = [
                joined(here[0], here[1], True), joined(here[2], here[3], True), joined(first, second, True),
            ]
            for i, value in enumerate(tiles):
                msg_2[t, s, i] = value.astype(BF16)

    kernel_copy.wait()
    weights[...] = jnp.zeros(weights.shape, BF16)
    for kt in range(3):
        taps = kernel_ref[9 * kt * OUT : 9 * (kt + 1) * OUT, :]
        taps = (0.5 * taps.astype(F32)).astype(BF16)
        weights[kt * LANES : (kt + 1) * LANES, :] = taps[:LANES]
        weights[3 * LANES + kt * OUT : 3 * LANES + (kt + 1) * OUT, :] = taps[LANES:]

    step = 8

    def silu_frame(t, _):
        fetch(t).wait()

        def silu_rows(r, _):
            half_x = 0.5 * out_ref[t, pl.ds(r * step, step)].astype(F32).reshape(step * width, cin)
            u = jnp.tanh(half_x)
            more = 1.0 + u
            value = half_x * more
            rows = aligned(r, step * width)
            act[t, rows, :] = value.astype(BF16)
            slope[t, rows, :] = more + value * (1.0 - u)
            return 0

        lax.fori_loop(0, height // step, silu_rows, 0, unroll=4)
        return 0

    lax.fori_loop(0, EARLY, silu_frame, 0)
    send_all(msg_2, recv_2, send_2, recv_main_2)
    lax.fori_loop(EARLY, frames, silu_frame, 0)

    @pl.when(jnp.logical_not(has_edge))
    def _():
        edge[...] = jnp.zeros(edge.shape, BF16)

    @pl.when(has_edge)
    def _():
        pltpu.make_async_copy(edge, edge, recv_edge).wait()

    pltpu.make_async_copy(recv, recv, recv_main).wait()

    def beside(value, i):
        return turned(value, -OUT - 2 * OUT * i, 1)

    def unpack(b, _):
        tiles = [recv[b, i].astype(F32) for i in range(FIRST)]
        sides = turned(tiles[2], EARLY, 0) + edge[b, 0].astype(F32)
        for i in range(ROWS - 1):
            field[b * ROWS + i, 0:FRAMES] = turned(tiles[i // 2], EARLY * (i % 2), 0)
            halo[b * ROWS + i, 0:FRAMES] = beside(sides, i)
        field[b * ROWS + 4, 0:FRAMES] = joined(tiles[2], tiles[3])
        halo[b * ROWS + 4, 0:FRAMES] = beside(tiles[3] + edge[b, 1].astype(F32), 4)
        return 0

    def unpack_2(b, _):
        tiles = [recv_2[b, i].astype(F32) for i in range(SECOND)]
        sides = turned(tiles[2], EARLY, 0) + edge[b, 0].astype(F32)
        for i in range(ROWS - 1):
            field[b * ROWS + i, EARLY:FRAMES] = turned(tiles[i // 2], EARLY * (1 - i % 2), 0)[EARLY:]
            halo[b * ROWS + i, EARLY:FRAMES] = beside(sides, i)[EARLY:]
        halo[b * ROWS + 4, EARLY:FRAMES] = beside(tiles[2] + edge[b, 1].astype(F32), 4)[EARLY:]
        return 0

    lax.fori_loop(0, n_tile, unpack, 0, unroll=4)

    def pack_lead(k, _):
        both = [
            jnp.where(row < 2, field[2 * k + i, 0:FRAMES], turned(halo[2 * k + i, 0:FRAMES], 2, 0)) for i in range(2)
        ]
        lead[k] = joined(both[0], both[1], False, True).astype(BF16)
        return 0

    def unpack_ahead(k, _):
        tiles = ahead[k].astype(F32)
        for i in range(2):
            field[2 * k + i, FRAMES:] = turned(tiles, -4 * i, 0)
            halo[2 * k + i, FRAMES:] = turned(tiles, -4 * i - 2, 0)
        return 0

    lead_copy = pltpu.make_async_remote_copy(
        src_ref=lead, dst_ref=ahead, send_sem=lead_send, recv_sem=lead_recv,
        device_id=(jnp.maximum(tm - 1, 0), tile), device_id_type=MESH,
    )

    @pl.when(to_left)
    def _():
        lax.fori_loop(0, height // 2, pack_lead, 0, unroll=8)
        lead_copy.start()

    lane3, col3 = lane_of((1, width, LANES), 2), lane_of((1, width, LANES), 1)
    outside = jnp.logical_or(
        jnp.logical_and(col3 == 0, lane3 < OUT),
        jnp.logical_and(col3 == width - 1, lane3 >= LANES - OUT),
    )
    edge_rows = jnp.zeros((width, LANES), F32)
    group = 16
    for t in range(WINDOW):
        vee[t, 0:width, :] = edge_rows
        vee[t, (height + 1) * width : (height + 2) * width, :] = edge_rows

    lane2 = lane_of((1, LANES), 1)

    def tap(t, g, shift_rows, shift):
        at = pl.ds(pl.multiple_of((g * group + shift_rows) * width, width), group * width)
        return turned(vee[t % WINDOW, at, :].astype(BF16), shift, 1)

    acc[...] = jnp.zeros(acc.shape, F32)

    def add_frame(t):
        left = jnp.concatenate([cols_t[t * LANES : (t + 3) * LANES, :], last_t[t]], axis=0)
        acc[...] += jnp.dot(left, act[t], preferred_element_type=F32)

    for t in range(wide):
        if t == EARLY:
            pltpu.make_async_copy(recv_2, recv_2, recv_main_2).wait()
            lax.fori_loop(0, n_tile, unpack_2, 0, unroll=4)
        if t == FRAMES:
            @pl.when(to_right)
            def _():
                pltpu.make_async_copy(ahead, ahead, lead_recv).wait()

            @pl.when(jnp.logical_not(to_right))
            def _():
                ahead[...] = jnp.zeros(ahead.shape, BF16)

            lax.fori_loop(0, height // 2, unpack_ahead, 0, unroll=8)

        def spread(g, _, t=t):
            rows = pl.ds(g * group, group)
            main = jnp.broadcast_to(field[rows, t : t + 1, :], (group, width, LANES))
            side = jnp.broadcast_to(halo[rows, t : t + 1, :], (group, width, LANES))
            at = pl.ds(pl.multiple_of((g * group + 1) * width, width), group * width)
            values = jnp.where(outside, side, main).reshape(group * width, LANES)
            vee[t % WINDOW, at, :] = pltpu.roll(values, 0, 1, stride=OUT, stride_axis=0)
            return 0

        def fill(g, _, t=t):
            rows = aligned(g, group * width)
            s0, s1, s2 = tap(t, g, 2, 2 * OUT), tap(t, g, 1, 5 * OUT), tap(t, g, 0, 0)
            cols[t, rows, :] = jnp.where(lane2 < 3 * OUT, s0, jnp.where(lane2 < 6 * OUT, s1, s2))
            return 0

        def fill_last(g, _, t=t):
            rows = aligned(g, group * width)
            taps = [tap(t - 2 + kt, g, 0, kt * OUT) for kt in range(3)]
            value = jnp.where(lane2 < 3 * OUT, taps[2], jnp.zeros_like(taps[2]))
            last[t - 2, rows, :] = jnp.where(lane2 < OUT, taps[0], jnp.where(lane2 < 2 * OUT, taps[1], value))
            return 0

        lax.fori_loop(0, height // group, spread, 0, unroll=True)
        lax.fori_loop(0, height // group, fill, 0, unroll=True)
        cols_t[t * LANES : (t + 1) * LANES, :] = jnp.transpose(cols[t])
        if t >= 2:
            lax.fori_loop(0, height // group, fill_last, 0, unroll=True)
            last_t[t - 2] = jnp.transpose(last[t - 2])[0 : 3 * OUT]
        if t >= 3:
            add_frame(t - 3)
    add_frame(frames - 1)

    pieces_of_total = []
    for kt in range(3):
        pieces_of_total.append(acc[kt * LANES : (kt + 1) * LANES, :])
        pieces_of_total.append(acc[3 * LANES + kt * OUT : 3 * LANES + (kt + 1) * OUT, :])
    pieces_of_total.append(jnp.zeros((part.shape[1] - 27 * OUT, cin), F32))
    part[...] = jnp.transpose(jnp.concatenate(pieces_of_total, axis=0))

    chunk = 40

    def grad_frame(t, _):
        def grad_rows(r, _):
            rows = aligned(r, chunk * width)
            left = jnp.concatenate([cols[t + kt, rows, :] for kt in range(3)] + [last[t, rows, :]], axis=1)
            grad = jnp.dot(left, weights[...], preferred_element_type=F32) * slope[t, rows, :]
            out_ref[t, pl.ds(r * chunk, chunk)] = grad.reshape(chunk, width, cin).astype(BF16)
            return 0

        lax.fori_loop(0, height // chunk, grad_rows, 0, unroll=True)
        return 0

    def drain(source, sem):
        pltpu.make_async_copy(source, source, sem).wait()

    def drain_messages(source, sem):
        if n_tm > 1:
            drain(source.at[pl.ds(0, n_tm - 1)], sem)
        if strips > 1:
            drain(source.at[0, pl.ds(0, strips - 1)], sem)

        @pl.when(block != tm)
        def _():
            drain(source.at[0, 0], sem)

    drain_messages(msg, send_main)
    drain_messages(msg_2, send_2)

    def drain_edge(k, _):
        drain(emsg.at[0, 0], send_edge)
        return 0

    lax.fori_loop(0, edges_out - self_edge, drain_edge, 0)

    @pl.when(to_left)
    def _():
        drain(lead, lead_send)

    rows = mine.shape[0]
    share = rows // groups
    swap = pltpu.make_async_remote_copy(
        src_ref=part.at[aligned(1 - core, rows)], dst_ref=mine,
        send_sem=swap_send, recv_sem=swap_recv,
        device_id=(partner, tile), device_id_type=MESH,
    )
    swap.start()
    lax.fori_loop(0, SPLIT[0], grad_frame, 0)
    swap.wait()
    mine[...] += part[aligned(core, rows), :]

    mine_half[...] = mine[...].astype(BF16)

    for k in range(1, groups):
        g = wrapped(spot + k, groups)
        pltpu.make_async_remote_copy(
            src_ref=mine_half.at[aligned(g, share)], dst_ref=pieces.at[spot],
            send_sem=piece_send, recv_sem=piece_recv,
            device_id=(tm, y_hi * groups + g), device_id_type=MESH,
        ).start()
    pieces[spot] = mine_half[aligned(spot, share), :]
    lax.fori_loop(SPLIT[0], SPLIT[1], grad_frame, 0)
    others = pieces.at[pl.ds(0, groups - 1)]
    pltpu.make_async_copy(others, others, piece_recv).wait()
    sums[...] = jnp.sum(pieces[...].astype(F32), axis=0)

    for k in range(n_tm):
        send(sums, quads.at[level], row_send, row_recv, k, owner_tile)
    lax.fori_loop(SPLIT[1], frames, grad_frame, 0)
    pltpu.make_async_copy(quads, quads, row_recv).wait()

    drain(others, piece_send)
    drain(quads.at[pl.ds(0, n_tm - 1)], row_send)

    @pl.when(core != y_hi)
    def _():
        drain(sums, row_send)

    result = quads[0]
    for k in range(1, n_tm):
        result = result + quads[k]
    kgrad_ref[...] = (result * scale)[:, : kgrad_ref.shape[1]]


SPLIT = (1, 6)


def on_device(n_tm, n_tile, scale, latent_grad, section_input, kernel):
    frames, height, width, cin = section_input.shape
    taps = kernel.shape[1]
    strips = n_tile // n_tm
    banded = jnp.transpose(latent_grad, (1, 0, 2)).reshape(ROWS, n_tm, FRAMES, strips * LANES)
    wide, count = frames + 2, height * width
    rows, share, padded = cin // CORES, cin // n_tile, 4 * LANES
    vmem = pl.BlockSpec(memory_space=pltpu.VMEM)
    return pl.pallas_call(
        functools.partial(whole, n_tm, n_tile, scale),
        out_shape=(
            pltpu.VMEM((frames, height, width, cin), BF16),
            pltpu.VMEM((share, taps), F32),
        ),
        in_specs=[pl.BlockSpec(memory_space=pl.ANY)] * 3,
        out_specs=(vmem, vmem),
        scratch_shapes=[
            pltpu.VMEM((ROWS, n_tm, FRAMES, strips * LANES), BF16),
            pltpu.VMEM((taps, cin), BF16),
            pltpu.VMEM((n_tm, strips, FIRST, FRAMES, LANES), BF16),
            pltpu.VMEM((n_tm, strips, SECOND, FRAMES, LANES), BF16),
            pltpu.VMEM((2, n_tm, 2, FRAMES, LANES), BF16),
            pltpu.VMEM((n_tile, FIRST, FRAMES, LANES), BF16),
            pltpu.VMEM((n_tile, SECOND, FRAMES, LANES), BF16),
            pltpu.VMEM((n_tile, 2, FRAMES, LANES), BF16),
            pltpu.VMEM((height // 2, FRAMES, LANES), BF16),
            pltpu.VMEM((height // 2, FRAMES, LANES), BF16),
            pltpu.VMEM((frames, count, cin), BF16),
            pltpu.VMEM((frames, count, cin), F32),
            pltpu.VMEM((height, 2 * FRAMES, LANES), F32),
            pltpu.VMEM((height, 2 * FRAMES, LANES), F32),
            pltpu.VMEM((WINDOW, (height + 2) * width, LANES), F32),
            pltpu.VMEM((wide, count, LANES), BF16),
            pltpu.VMEM((wide * LANES, count), BF16),
            pltpu.VMEM((frames, count, LANES), BF16),
            pltpu.VMEM((frames, 3 * OUT, count), BF16),
            pltpu.VMEM((padded, cin), BF16),
            pltpu.VMEM((27 * OUT, cin), F32),
            pltpu.VMEM((cin, padded), F32),
            pltpu.VMEM((rows, padded), F32),
            pltpu.VMEM((rows, padded), BF16),
            pltpu.VMEM((n_tile // CORES, share, padded), BF16),
            pltpu.VMEM((share, padded), F32),
            pltpu.VMEM((n_tm, share, padded), F32),
            pltpu.SemaphoreType.DMA((frames,)),
            pltpu.SemaphoreType.DMA((16,)),
        ],
        compiler_params=pltpu.CompilerParams(
            collective_id=0, has_side_effects=True, vmem_limit_bytes=VMEM_LIMIT
        ),
    )(banded, section_input, jnp.transpose(kernel))


VMEM_LIMIT = 53 << 20


def solution(mesh):
    n_tm, n_tile = mesh.shape["tm"], mesh.shape["tile"]
    positions = n_tm * FRAMES * n_tile * ROWS * n_tile * STRIP
    return jax.shard_map(
        functools.partial(on_device, n_tm, n_tile, 1.0 / math.sqrt(positions)),
        mesh=mesh,
        in_specs=(P(None, "tile", "tm"), P("tm", None, "tile", None), P()),
        out_specs=(P("tm", None, "tile", None), P("tile", None)),
        check_vma=False,
    )
```

```python
import functools
import math

import jax
import jax.numpy as jnp
from jax import lax
from jax.experimental import pallas as pl
from jax.experimental.pallas import tpu as pltpu
from jax.sharding import PartitionSpec as P

MESH = pl.DeviceIdType.MESH
F32, BF16 = jnp.float32, jnp.bfloat16
LANES = 128
OUT = 16
STRIP = 8
FRAMES = 8
ROWS = 5
FIRST = 4
SECOND = 3
EARLY = 4
CORES = 2
KEPT = 4
WINDOW = 3


def lane_of(shape, axis):
    return lax.broadcasted_iota(jnp.int32, shape, axis)


def aligned(index, size):
    return pl.ds(pl.multiple_of(index * size, size), size)


def turned(value, shift, axis):
    shift %= value.shape[axis]
    return pltpu.roll(value, shift, axis) if shift else value


def wrapped(index, size):
    return jnp.where(index >= size, index - size, index)


def strip_halo(left, right):
    lane = lane_of((1, LANES), 1)
    rows = []
    for i in range(ROWS):
        value = jnp.zeros((FRAMES, LANES), F32)
        if right is not None:
            value = jnp.where(lane >= LANES - OUT, right[i], value)
        if left is not None:
            value = jnp.where(lane < OUT, left[i], value)
        rows.append(turned(value, OUT + 2 * OUT * i, 1))
    return rows[0] + rows[1] + rows[2] + rows[3], rows[4]


def joined(upper, lower, turn_upper=False, turn_lower=False):
    upper = turned(upper, EARLY, 0) if turn_upper else upper
    lower = turned(lower, EARLY, 0) if turn_lower else lower
    return jnp.where(lane_of((FRAMES, 1), 0) < EARLY, upper, lower)


def whole(
    n_tm, n_tile, scale, grad_hbm, x_ref, kernel_hbm, out_ref, kgrad_ref,
    grad_ref, kernel_ref, msg, msg_2, emsg, recv, recv_2, edge, lead, ahead, act, slope, field, halo, vee, cols, cols_t, last, last_t,
    weights, acc, half, mine, pieces, sums, quads, in_sem, sems,
):
    frames, height, width, cin = out_ref.shape
    wide, count = frames + 2, height * width
    tm, tile = lax.axis_index("tm"), lax.axis_index("tile")
    strips = n_tile // n_tm
    block = tile // strips
    place_in_block = lax.rem(tile, strips)
    from_left = jnp.logical_and(place_in_block == 0, block > 0)
    from_right = jnp.logical_and(place_in_block == strips - 1, block < n_tm - 1)
    has_edge = jnp.logical_or(from_left, from_right)
    edge_block = jnp.where(place_in_block == 0, block - 1, block + 1)
    messages = n_tm * strips
    send_main, send_edge, recv_main, recv_edge = (sems.at[i] for i in range(4))
    send_2, recv_main_2 = sems.at[10], sems.at[11]
    lead_send, lead_recv = sems.at[12], sems.at[13]

    def half_sem(kind, p):
        return sems.at[14 + 2 * kind + p]

    core, y_lo = lax.rem(tm, CORES), tm // CORES
    groups = n_tile // CORES
    y_hi, spot = tile // groups, lax.rem(tile, groups)
    partner = tm + 1 - 2 * core
    level = y_hi * CORES + y_lo
    owner_tile = core * groups + spot

    def is_me(target_tm, target_tile):
        return jnp.logical_and(target_tm == tm, target_tile == tile)

    grad_copy = pltpu.make_async_copy(grad_hbm, grad_ref, sems.at[8])
    kernel_copy = pltpu.make_async_copy(kernel_hbm, kernel_ref, sems.at[9])
    grad_copy.start()
    kernel_copy.start()

    def fetch(t):
        return pltpu.make_async_copy(x_ref.at[t], out_ref.at[t], in_sem.at[t])

    for t in range(frames):
        fetch(t).start()

    barrier = pltpu.get_barrier_semaphore()

    def hail(target_tm, target_tile):
        pl.semaphore_signal(barrier, inc=1, device_id=(target_tm, target_tile), device_id_type=MESH)

    for k in range(1, n_tile):
        hail(block, wrapped(tile + k, n_tile))

    @pl.when(block != tm)
    def _():
        hail(block, tile)

    @pl.when(has_edge)
    def _():
        for k in range(1, n_tile):
            hail(edge_block, wrapped(tile + k, n_tile))

        @pl.when(edge_block != tm)
        def _():
            hail(edge_block, tile)

    @pl.when(tm < n_tm - 1)
    def _():
        hail(tm + 1, tile)

    hail(partner, tile)
    for k in range(1, groups):
        hail(tm, y_hi * groups + wrapped(spot + k, groups))
    for k in range(n_tm):
        source = (k % CORES) * CORES + y_hi, (k // CORES) * groups + spot

        @pl.when(jnp.logical_not(is_me(*source)))
        def _():
            hail(*source)

    r, c = lane_of((LANES, LANES), 0), lane_of((LANES, LANES), 1)
    same = jnp.logical_and(r // OUT + c // OUT == STRIP - 1, lax.rem(r, OUT) == lax.rem(c, OUT))
    flip = jnp.where(same, 1.0, 0.0).astype(BF16)
    row = lane_of((FRAMES, 1), 0)
    nothing = jnp.zeros((FRAMES, LANES), F32)
    grad_copy.wait()
    flipped, halos = [], []
    for t in range(n_tm):
        rows = grad_ref[:, t].astype(F32).reshape(ROWS * FRAMES, strips * LANES).astype(BF16)
        here = [
            jnp.dot(rows[:, s * LANES : (s + 1) * LANES], flip, preferred_element_type=F32)
            .reshape(ROWS, FRAMES, LANES)
            for s in range(strips)
        ]
        flipped.append(here)
        padded = [None, None] + here + [None, None]
        halos.append([strip_halo(padded[s], padded[s + 2]) for s in range(strips + 2)])
    for t in range(n_tm):
        for s in range(strips):
            here, (first, second) = flipped[t][s], halos[t][s + 1]
            tiles = [
                joined(here[0], here[1], False, True), joined(here[2], here[3], False, True),
                joined(here[4], first, False, True), joined(second, here[4]),
            ]
            for i, value in enumerate(tiles):
                msg[t, s, i] = value.astype(BF16)
        for side, s in ((0, strips + 1), (1, 0)):
            for i, value in enumerate(halos[t][s]):
                emsg[side, t, i] = value.astype(BF16)

    self_main = (block == tm).astype(jnp.int32)
    to_right, to_left = tm < n_tm - 1, tm > 0
    right_tile, left_tile = (tm + 1) * strips, tm * strips - 1
    self_edge = (
        jnp.logical_and(to_right, tile == right_tile).astype(jnp.int32)
        + jnp.logical_and(to_left, tile == left_tile).astype(jnp.int32)
    )
    edges_out = n_tm * (to_right.astype(jnp.int32) + to_left.astype(jnp.int32))
    self_owner = (core == y_hi).astype(jnp.int32)
    exchange_out = messages - self_main + edges_out - self_edge
    pl.semaphore_wait(barrier, exchange_out + 1 + groups - 1 + n_tm - self_owner + to_left.astype(jnp.int32))

    def send(source, target, send_sem, recv_sem, target_tm, target_tile):
        own = is_me(target_tm, target_tile)

        @pl.when(jnp.logical_not(own))
        def _():
            pltpu.make_async_remote_copy(
                src_ref=source, dst_ref=target, send_sem=send_sem, recv_sem=recv_sem,
                device_id=(target_tm, target_tile), device_id_type=MESH,
            ).start()

        @pl.when(own)
        def _():
            pltpu.make_async_copy(source, target, recv_sem).start()

    def send_edges(t, _):
        @pl.when(to_right)
        def _():
            send(emsg.at[0, t], edge.at[tile], send_edge, recv_edge, t, right_tile)

        @pl.when(to_left)
        def _():
            send(emsg.at[1, t], edge.at[tile], send_edge, recv_edge, t, left_tile)

        return 0

    def send_all(source, target, send_sem, recv_sem):
        for k in range(messages):
            t, s = wrapped(tm + k // strips, n_tm), wrapped(place_in_block + k % strips, strips)
            if k == 0:
                send(source.at[t, s], target.at[tile], send_sem, recv_sem, t, tm * strips + s)
            else:
                pltpu.make_async_remote_copy(
                    src_ref=source.at[t, s], dst_ref=target.at[tile], send_sem=send_sem, recv_sem=recv_sem,
                    device_id=(t, tm * strips + s), device_id_type=MESH,
                ).start()

    lax.fori_loop(0, n_tm, send_edges, 0)
    send_all(msg, recv, send_main, recv_main)

    for t in range(n_tm):
        for s in range(strips):
            here, (first, second) = flipped[t][s], halos[t][s + 1]
            tiles = [
                joined(here[0], here[1], True), joined(here[2], here[3], True), joined(first, second, True),
            ]
            for i, value in enumerate(tiles):
                msg_2[t, s, i] = value.astype(BF16)

    kernel_copy.wait()
    weights[...] = jnp.zeros(weights.shape, BF16)
    for kt in range(3):
        taps = kernel_ref[9 * kt * OUT : 9 * (kt + 1) * OUT, :]
        taps = (0.5 * taps.astype(F32)).astype(BF16)
        weights[kt * LANES : (kt + 1) * LANES, :] = taps[:LANES]
        weights[3 * LANES + kt * OUT : 3 * LANES + (kt + 1) * OUT, :] = taps[LANES:]

    step = 8

    def silu(x):
        half_x = 0.5 * x.astype(F32).reshape(x.shape[0] * width, cin)
        u = jnp.tanh(half_x)
        more = 1.0 + u
        value = half_x * more
        return value, lambda: more + value * (1.0 - u)

    def silu_frame(t, kept):
        fetch(t).wait()

        def silu_rows(r, _):
            value, slope_of = silu(out_ref[t, pl.ds(r * step, step)])
            rows = aligned(r, step * width)
            act[t, rows, :] = value.astype(BF16)
            if kept:
                slope[t, rows, :] = slope_of()
            return 0

        lax.fori_loop(0, height // step, silu_rows, 0, unroll=4)

    def silu_frames(first, end, kept):
        def one(t, _):
            silu_frame(t, kept)
            return 0

        lax.fori_loop(first, end, one, 0)

    silu_frames(0, KEPT, True)
    send_all(msg_2, recv_2, send_2, recv_main_2)
    silu_frames(KEPT, frames, False)

    @pl.when(jnp.logical_not(has_edge))
    def _():
        edge[...] = jnp.zeros(edge.shape, BF16)

    @pl.when(has_edge)
    def _():
        pltpu.make_async_copy(edge, edge, recv_edge).wait()

    pltpu.make_async_copy(recv, recv, recv_main).wait()

    def beside(value, i):
        return turned(value, -OUT - 2 * OUT * i, 1)

    def unpack(b, _):
        tiles = [recv[b, i].astype(F32) for i in range(FIRST)]
        sides = turned(tiles[2], EARLY, 0) + edge[b, 0].astype(F32)
        for i in range(ROWS - 1):
            field[b * ROWS + i, 0:FRAMES] = turned(tiles[i // 2], EARLY * (i % 2), 0)
            halo[b * ROWS + i, 0:FRAMES] = beside(sides, i)
        field[b * ROWS + 4, 0:FRAMES] = joined(tiles[2], tiles[3])
        halo[b * ROWS + 4, 0:FRAMES] = beside(tiles[3] + edge[b, 1].astype(F32), 4)
        return 0

    def unpack_2(b, _):
        tiles = [recv_2[b, i].astype(F32) for i in range(SECOND)]
        sides = turned(tiles[2], EARLY, 0) + edge[b, 0].astype(F32)
        for i in range(ROWS - 1):
            field[b * ROWS + i, EARLY:FRAMES] = turned(tiles[i // 2], EARLY * (1 - i % 2), 0)[EARLY:]
            halo[b * ROWS + i, EARLY:FRAMES] = beside(sides, i)[EARLY:]
        halo[b * ROWS + 4, EARLY:FRAMES] = beside(tiles[2] + edge[b, 1].astype(F32), 4)[EARLY:]
        return 0

    lax.fori_loop(0, n_tile, unpack, 0, unroll=4)

    def pack_lead(k, _):
        both = [
            jnp.where(row < 2, field[2 * k + i, 0:FRAMES], turned(halo[2 * k + i, 0:FRAMES], 2, 0)) for i in range(2)
        ]
        lead[k] = joined(both[0], both[1], False, True).astype(BF16)
        return 0

    def unpack_ahead(k, _):
        tiles = ahead[k].astype(F32)
        for i in range(2):
            field[2 * k + i, FRAMES:] = turned(tiles, -4 * i, 0)
            halo[2 * k + i, FRAMES:] = turned(tiles, -4 * i - 2, 0)
        return 0

    lead_copy = pltpu.make_async_remote_copy(
        src_ref=lead, dst_ref=ahead, send_sem=lead_send, recv_sem=lead_recv,
        device_id=(jnp.maximum(tm - 1, 0), tile), device_id_type=MESH,
    )

    @pl.when(to_left)
    def _():
        lax.fori_loop(0, height // 2, pack_lead, 0, unroll=8)
        lead_copy.start()

    lane3, col3 = lane_of((1, width, LANES), 2), lane_of((1, width, LANES), 1)
    outside = jnp.logical_or(
        jnp.logical_and(col3 == 0, lane3 < OUT),
        jnp.logical_and(col3 == width - 1, lane3 >= LANES - OUT),
    )
    edge_rows = jnp.zeros((width, LANES), F32)
    group = 16
    for t in range(WINDOW):
        vee[t, 0:width, :] = edge_rows
        vee[t, (height + 1) * width : (height + 2) * width, :] = edge_rows

    lane2 = lane_of((1, LANES), 1)

    def tap(t, g, shift_rows, shift):
        at = pl.ds(pl.multiple_of((g * group + shift_rows) * width, width), group * width)
        return turned(vee[t % WINDOW, at, :].astype(BF16), shift, 1)

    acc[...] = jnp.zeros(acc.shape, F32)
    rest = LANES + 3 * OUT
    half[1, rest:, :] = jnp.zeros((half.shape[1] - rest, half.shape[2]), F32)

    def add_first(t):
        grad = jnp.dot(cols_t[t * LANES : (t + 2) * LANES, :], act[t], preferred_element_type=F32)
        for h in range(CORES):
            acc[0, h] += grad[:, h * (cin // CORES) : (h + 1) * (cin // CORES)]

    def add_second(t, _):
        left = jnp.concatenate([cols_t[aligned(t + 2, LANES), :], last_t[t]], axis=0)
        grad = jnp.dot(left, act[t], preferred_element_type=F32)
        for h in range(CORES):
            acc[1, h, 0:rest] += grad[:, h * (cin // CORES) : (h + 1) * (cin // CORES)]
        return 0

    for t in range(wide):
        if t == EARLY:
            pltpu.make_async_copy(recv_2, recv_2, recv_main_2).wait()
            lax.fori_loop(0, n_tile, unpack_2, 0, unroll=4)
        if t == FRAMES:
            @pl.when(to_right)
            def _():
                pltpu.make_async_copy(ahead, ahead, lead_recv).wait()

            @pl.when(jnp.logical_not(to_right))
            def _():
                ahead[...] = jnp.zeros(ahead.shape, BF16)

            lax.fori_loop(0, height // 2, unpack_ahead, 0, unroll=8)

        def spread(g, _, t=t):
            rows = pl.ds(g * group, group)
            main = jnp.broadcast_to(field[rows, t : t + 1, :], (group, width, LANES))
            side = jnp.broadcast_to(halo[rows, t : t + 1, :], (group, width, LANES))
            at = pl.ds(pl.multiple_of((g * group + 1) * width, width), group * width)
            values = jnp.where(outside, side, main).reshape(group * width, LANES)
            vee[t % WINDOW, at, :] = pltpu.roll(values, 0, 1, stride=OUT, stride_axis=0)
            return 0

        def fill(g, _, t=t):
            rows = aligned(g, group * width)
            s0, s1, s2 = tap(t, g, 2, 2 * OUT), tap(t, g, 1, 5 * OUT), tap(t, g, 0, 0)
            cols[t, rows, :] = jnp.where(lane2 < 3 * OUT, s0, jnp.where(lane2 < 6 * OUT, s1, s2))
            return 0

        def fill_last(g, _, t=t):
            rows = aligned(g, group * width)
            taps = [tap(t - 2 + kt, g, 0, kt * OUT) for kt in range(3)]
            value = jnp.where(lane2 < 3 * OUT, taps[2], jnp.zeros_like(taps[2]))
            last[t - 2, rows, :] = jnp.where(lane2 < OUT, taps[0], jnp.where(lane2 < 2 * OUT, taps[1], value))
            return 0

        lax.fori_loop(0, height // group, spread, 0, unroll=True)
        lax.fori_loop(0, height // group, fill, 0, unroll=True)
        cols_t[t * LANES : (t + 1) * LANES, :] = jnp.transpose(cols[t])
        if t >= 2:
            lax.fori_loop(0, height // group, fill_last, 0, unroll=True)
            last_t[t - 2] = jnp.transpose(last[t - 2])[0 : 3 * OUT]
        if t >= 2:
            add_first(t - 2)

    chunk = 40

    def grad_frame(t, kept):
        def grad_rows(r, _):
            rows = aligned(r, chunk * width)
            left = jnp.concatenate([cols[t + kt, rows, :] for kt in range(3)] + [last[t, rows, :]], axis=1)
            grad = jnp.dot(left, weights[...], preferred_element_type=F32)
            grad = grad * (slope[t, rows, :] if kept else silu(out_ref[t, pl.ds(r * chunk, chunk)])[1]())
            out_ref[t, pl.ds(r * chunk, chunk)] = grad.reshape(chunk, width, cin).astype(BF16)
            return 0

        lax.fori_loop(0, height // chunk, grad_rows, 0, unroll=True)

    def grad_frames(first, end):
        for kept, a, b in ((True, first, min(end, KEPT)), (False, max(first, KEPT), end)):
            def one(t, _, kept=kept):
                grad_frame(t, kept)
                return 0

            if a < b:
                lax.fori_loop(a, b, one, 0)

    def drain(source, sem):
        pltpu.make_async_copy(source, source, sem).wait()

    def drain_messages(source, sem):
        if n_tm > 1:
            drain(source.at[pl.ds(0, n_tm - 1)], sem)
        if strips > 1:
            drain(source.at[0, pl.ds(0, strips - 1)], sem)

        @pl.when(block != tm)
        def _():
            drain(source.at[0, 0], sem)

    drain_messages(msg, send_main)
    drain_messages(msg_2, send_2)

    def drain_edge(k, _):
        drain(emsg.at[0, 0], send_edge)
        return 0

    lax.fori_loop(0, edges_out - self_edge, drain_edge, 0)

    @pl.when(to_left)
    def _():
        drain(lead, lead_send)

    share = mine.shape[1] // groups
    used = (acc.shape[2], rest)

    def swap(p):
        return pltpu.make_async_remote_copy(
            src_ref=acc.at[p, 1 - core, pl.ds(0, used[p])], dst_ref=half.at[p, pl.ds(0, used[p])],
            send_sem=half_sem(0, p), recv_sem=half_sem(1, p),
            device_id=(partner, tile), device_id_type=MESH,
        )

    def send_pieces(p):
        swap(p).wait()
        mine[p] = jnp.transpose(acc[p, core] + half[p]).astype(BF16)
        for k in range(1, groups):
            g = wrapped(spot + k, groups)
            pltpu.make_async_remote_copy(
                src_ref=mine.at[p, aligned(g, share)], dst_ref=pieces.at[p, spot],
                send_sem=half_sem(2, p), recv_sem=half_sem(3, p),
                device_id=(tm, y_hi * groups + g), device_id_type=MESH,
            ).start()
        pieces[p, spot] = mine[p, aligned(spot, share), :]

    def send_sums(p):
        drain(pieces.at[p, pl.ds(0, groups - 1)], half_sem(3, p))
        sums[p] = jnp.sum(pieces[p].astype(F32), axis=0)
        for k in range(n_tm):
            send(sums.at[p], quads.at[p, level], half_sem(4, p), half_sem(5, p), k, owner_tile)

    swap(0).start()
    lax.fori_loop(0, frames, add_second, 0)
    swap(1).start()
    send_pieces(0)
    grad_frames(0, SPLIT[0])
    send_pieces(1)
    grad_frames(SPLIT[0], SPLIT[1])
    send_sums(0)
    grad_frames(SPLIT[1], SPLIT[2])
    send_sums(1)
    grad_frames(SPLIT[2], frames)

    results = []
    for p in range(2):
        drain(quads.at[p], half_sem(5, p))
        drain(pieces.at[p, pl.ds(0, groups - 1)], half_sem(2, p))
        drain(quads.at[p, pl.ds(0, n_tm - 1)], half_sem(4, p))
        result = quads[p, 0]
        for k in range(1, n_tm):
            result = result + quads[p, k]
        results.append(result * scale)

    @pl.when(core != y_hi)
    def _():
        for p in range(2):
            drain(sums.at[p], half_sem(4, p))

    blocks = [results[0][:, :LANES], results[0][:, LANES:], results[1][:, :LANES]]
    for kt in range(3):
        at = 9 * kt * OUT
        kgrad_ref[:, at : at + LANES] = blocks[kt]
        kgrad_ref[:, at + LANES : at + 9 * OUT] = results[1][:, LANES + kt * OUT : LANES + (kt + 1) * OUT]


SPLIT = (1, 4, 5)


def on_device(n_tm, n_tile, scale, latent_grad, section_input, kernel):
    frames, height, width, cin = section_input.shape
    taps = kernel.shape[1]
    strips = n_tile // n_tm
    banded = jnp.transpose(latent_grad, (1, 0, 2)).reshape(ROWS, n_tm, FRAMES, strips * LANES)
    wide, count = frames + 2, height * width
    rows, share, padded = cin // CORES, cin // n_tile, 4 * LANES
    vmem = pl.BlockSpec(memory_space=pltpu.VMEM)
    return pl.pallas_call(
        functools.partial(whole, n_tm, n_tile, scale),
        out_shape=(
            pltpu.VMEM((frames, height, width, cin), BF16),
            pltpu.VMEM((share, taps), F32),
        ),
        in_specs=[pl.BlockSpec(memory_space=pl.ANY)] * 3,
        out_specs=(vmem, vmem),
        scratch_shapes=[
            pltpu.VMEM((ROWS, n_tm, FRAMES, strips * LANES), BF16),
            pltpu.VMEM((taps, cin), BF16),
            pltpu.VMEM((n_tm, strips, FIRST, FRAMES, LANES), BF16),
            pltpu.VMEM((n_tm, strips, SECOND, FRAMES, LANES), BF16),
            pltpu.VMEM((2, n_tm, 2, FRAMES, LANES), BF16),
            pltpu.VMEM((n_tile, FIRST, FRAMES, LANES), BF16),
            pltpu.VMEM((n_tile, SECOND, FRAMES, LANES), BF16),
            pltpu.VMEM((n_tile, 2, FRAMES, LANES), BF16),
            pltpu.VMEM((height // 2, FRAMES, LANES), BF16),
            pltpu.VMEM((height // 2, FRAMES, LANES), BF16),
            pltpu.VMEM((frames, count, cin), BF16),
            pltpu.VMEM((KEPT, count, cin), F32),
            pltpu.VMEM((height, 2 * FRAMES, LANES), F32),
            pltpu.VMEM((height, 2 * FRAMES, LANES), F32),
            pltpu.VMEM((WINDOW, (height + 2) * width, LANES), F32),
            pltpu.VMEM((wide, count, LANES), BF16),
            pltpu.VMEM((wide * LANES, count), BF16),
            pltpu.VMEM((frames, count, LANES), BF16),
            pltpu.VMEM((frames, 3 * OUT, count), BF16),
            pltpu.VMEM((padded, cin), BF16),
            pltpu.VMEM((2, CORES, 2 * LANES, rows), F32),
            pltpu.VMEM((2, 2 * LANES, rows), F32),
            pltpu.VMEM((2, rows, 2 * LANES), BF16),
            pltpu.VMEM((2, n_tile // CORES, share, 2 * LANES), BF16),
            pltpu.VMEM((2, share, 2 * LANES), F32),
            pltpu.VMEM((2, n_tm, share, 2 * LANES), F32),
            pltpu.SemaphoreType.DMA((frames,)),
            pltpu.SemaphoreType.DMA((26,)),
        ],
        compiler_params=pltpu.CompilerParams(
            collective_id=0, has_side_effects=True, vmem_limit_bytes=VMEM_LIMIT
        ),
    )(banded, section_input, jnp.transpose(kernel))


VMEM_LIMIT = 53 << 20


def solution(mesh):
    n_tm, n_tile = mesh.shape["tm"], mesh.shape["tile"]
    positions = n_tm * FRAMES * n_tile * ROWS * n_tile * STRIP
    return jax.shard_map(
        functools.partial(on_device, n_tm, n_tile, 1.0 / math.sqrt(positions)),
        mesh=mesh,
        in_specs=(P(None, "tile", "tm"), P("tm", None, "tile", None), P()),
        out_specs=(P("tm", None, "tile", None), P("tile", None)),
        check_vma=False,
    )
```

```python
import functools
import math

import jax
import jax.numpy as jnp
from jax import lax
from jax.experimental import pallas as pl
from jax.experimental.pallas import tpu as pltpu
from jax.sharding import PartitionSpec as P

MESH = pl.DeviceIdType.MESH
F32, BF16 = jnp.float32, jnp.bfloat16
LANES = 128
OUT = 16
STRIP = 8
FRAMES = 8
ROWS = 5
FIRST = 4
SECOND = 3
EARLY = 4
CORES = 2
WINDOW = 3


def lane_of(shape, axis):
    return lax.broadcasted_iota(jnp.int32, shape, axis)


def aligned(index, size):
    return pl.ds(pl.multiple_of(index * size, size), size)


def turned(value, shift, axis):
    shift %= value.shape[axis]
    return pltpu.roll(value, shift, axis) if shift else value


def wrapped(index, size):
    return jnp.where(index >= size, index - size, index)


def strip_halo(left, right):
    lane = lane_of((1, LANES), 1)
    rows = []
    for i in range(ROWS):
        value = jnp.zeros((FRAMES, LANES), F32)
        if right is not None:
            value = jnp.where(lane >= LANES - OUT, right[i], value)
        if left is not None:
            value = jnp.where(lane < OUT, left[i], value)
        rows.append(turned(value, OUT + 2 * OUT * i, 1))
    return rows[0] + rows[1] + rows[2] + rows[3], rows[4]


def joined(upper, lower, turn_upper=False, turn_lower=False):
    upper = turned(upper, EARLY, 0) if turn_upper else upper
    lower = turned(lower, EARLY, 0) if turn_lower else lower
    return jnp.where(lane_of((FRAMES, 1), 0) < EARLY, upper, lower)


def whole(
    n_tm, n_tile, scale, grad_hbm, x_ref, kernel_hbm, out_ref, kgrad_ref,
    grad_ref, kernel_ref, msg, msg_2, emsg, recv, recv_2, edge, lead, ahead, act, slope, field, halo, vee, cols, cols_t, last, last_t,
    weights, acc, half, mine, pieces, sums, quads, in_sem, sems,
):
    frames, height, width, cin = out_ref.shape
    wide, count = frames + 2, height * width
    tm, tile = lax.axis_index("tm"), lax.axis_index("tile")
    strips = n_tile // n_tm
    block = tile // strips
    place_in_block = lax.rem(tile, strips)
    from_left = jnp.logical_and(place_in_block == 0, block > 0)
    from_right = jnp.logical_and(place_in_block == strips - 1, block < n_tm - 1)
    has_edge = jnp.logical_or(from_left, from_right)
    edge_block = jnp.where(place_in_block == 0, block - 1, block + 1)
    messages = n_tm * strips
    send_main, send_edge, recv_main, recv_edge = (sems.at[i] for i in range(4))
    send_2, recv_main_2 = sems.at[10], sems.at[11]
    lead_send, lead_recv = sems.at[12], sems.at[13]

    def half_sem(kind, p):
        return sems.at[14 + 2 * kind + p]

    core, y_lo = lax.rem(tm, CORES), tm // CORES
    groups = n_tile // CORES
    y_hi, spot = tile // groups, lax.rem(tile, groups)
    partner = tm + 1 - 2 * core
    level = y_hi * CORES + y_lo
    owner_tile = core * groups + spot

    def is_me(target_tm, target_tile):
        return jnp.logical_and(target_tm == tm, target_tile == tile)

    grad_copy = pltpu.make_async_copy(grad_hbm, grad_ref, sems.at[8])
    kernel_copy = pltpu.make_async_copy(kernel_hbm, kernel_ref, sems.at[9])
    grad_copy.start()
    kernel_copy.start()

    def fetch(t):
        return pltpu.make_async_copy(x_ref.at[t], out_ref.at[t], in_sem.at[t])

    for t in range(frames):
        fetch(t).start()

    barrier = pltpu.get_barrier_semaphore()

    def hail(target_tm, target_tile):
        pl.semaphore_signal(barrier, inc=1, device_id=(target_tm, target_tile), device_id_type=MESH)

    for k in range(1, n_tile):
        hail(block, wrapped(tile + k, n_tile))

    @pl.when(block != tm)
    def _():
        hail(block, tile)

    @pl.when(has_edge)
    def _():
        for k in range(1, n_tile):
            hail(edge_block, wrapped(tile + k, n_tile))

        @pl.when(edge_block != tm)
        def _():
            hail(edge_block, tile)

    @pl.when(tm < n_tm - 1)
    def _():
        hail(tm + 1, tile)

    hail(partner, tile)
    for k in range(1, groups):
        hail(tm, y_hi * groups + wrapped(spot + k, groups))
    for k in range(n_tm):
        source = (k % CORES) * CORES + y_hi, (k // CORES) * groups + spot

        @pl.when(jnp.logical_not(is_me(*source)))
        def _():
            hail(*source)

    r, c = lane_of((LANES, LANES), 0), lane_of((LANES, LANES), 1)
    same = jnp.logical_and(r // OUT + c // OUT == STRIP - 1, lax.rem(r, OUT) == lax.rem(c, OUT))
    flip = jnp.where(same, 1.0, 0.0).astype(BF16)
    row = lane_of((FRAMES, 1), 0)
    nothing = jnp.zeros((FRAMES, LANES), F32)
    grad_copy.wait()
    flipped, halos = [], []
    for t in range(n_tm):
        rows = grad_ref[:, t].astype(F32).reshape(ROWS * FRAMES, strips * LANES).astype(BF16)
        here = [
            jnp.dot(rows[:, s * LANES : (s + 1) * LANES], flip, preferred_element_type=F32)
            .reshape(ROWS, FRAMES, LANES)
            for s in range(strips)
        ]
        flipped.append(here)
        padded = [None, None] + here + [None, None]
        halos.append([strip_halo(padded[s], padded[s + 2]) for s in range(strips + 2)])
    for t in range(n_tm):
        for s in range(strips):
            here, (first, second) = flipped[t][s], halos[t][s + 1]
            tiles = [
                joined(here[0], here[1], False, True), joined(here[2], here[3], False, True),
                joined(here[4], first, False, True), joined(second, here[4]),
            ]
            for i, value in enumerate(tiles):
                msg[t, s, i] = value.astype(BF16)
        for side, s in ((0, strips + 1), (1, 0)):
            for i, value in enumerate(halos[t][s]):
                emsg[side, t, i] = value.astype(BF16)

    self_main = (block == tm).astype(jnp.int32)
    to_right, to_left = tm < n_tm - 1, tm > 0
    right_tile, left_tile = (tm + 1) * strips, tm * strips - 1
    self_edge = (
        jnp.logical_and(to_right, tile == right_tile).astype(jnp.int32)
        + jnp.logical_and(to_left, tile == left_tile).astype(jnp.int32)
    )
    edges_out = n_tm * (to_right.astype(jnp.int32) + to_left.astype(jnp.int32))
    self_owner = (core == y_hi).astype(jnp.int32)
    exchange_out = messages - self_main + edges_out - self_edge
    pl.semaphore_wait(barrier, exchange_out + 1 + groups - 1 + n_tm - self_owner + to_left.astype(jnp.int32))

    def send(source, target, send_sem, recv_sem, target_tm, target_tile):
        own = is_me(target_tm, target_tile)

        @pl.when(jnp.logical_not(own))
        def _():
            pltpu.make_async_remote_copy(
                src_ref=source, dst_ref=target, send_sem=send_sem, recv_sem=recv_sem,
                device_id=(target_tm, target_tile), device_id_type=MESH,
            ).start()

        @pl.when(own)
        def _():
            pltpu.make_async_copy(source, target, recv_sem).start()

    def send_edges(t, _):
        @pl.when(to_right)
        def _():
            send(emsg.at[0, t], edge.at[tile], send_edge, recv_edge, t, right_tile)

        @pl.when(to_left)
        def _():
            send(emsg.at[1, t], edge.at[tile], send_edge, recv_edge, t, left_tile)

        return 0

    def send_away(source, target, send_sem, recv_sem, k):
        t = wrapped(tm + lax.div(k, strips), n_tm)
        s = wrapped(place_in_block + lax.rem(k, strips), strips)
        pltpu.make_async_remote_copy(
            src_ref=source.at[t, s], dst_ref=target.at[tile], send_sem=send_sem, recv_sem=recv_sem,
            device_id=(t, tm * strips + s), device_id_type=MESH,
        ).start()

    def send_first(source, target, send_sem, recv_sem):
        send(source.at[tm, place_in_block], target.at[tile], send_sem, recv_sem, tm, tm * strips + place_in_block)

    lax.fori_loop(0, n_tm, send_edges, 0)
    send_first(msg, recv, send_main, recv_main)
    for k in range(1, messages):
        send_away(msg, recv, send_main, recv_main, jnp.int32(k))

    for t in range(n_tm):
        for s in range(strips):
            here, (first, second) = flipped[t][s], halos[t][s + 1]
            tiles = [
                joined(here[0], here[1], True), joined(here[2], here[3], True), joined(first, second, True),
            ]
            for i, value in enumerate(tiles):
                msg_2[t, s, i] = value.astype(BF16)

    kernel_copy.wait()
    weights[...] = jnp.zeros(weights.shape, BF16)
    for kt in range(3):
        taps = kernel_ref[9 * kt * OUT : 9 * (kt + 1) * OUT, :]
        taps = (0.5 * taps.astype(F32)).astype(BF16)
        weights[kt * LANES : (kt + 1) * LANES, :] = taps[:LANES]
        weights[3 * LANES + kt * OUT : 3 * LANES + (kt + 1) * OUT, :] = taps[LANES:]

    step = 8

    def silu(x):
        half_x = 0.5 * x.astype(F32).reshape(x.shape[0] * width, cin)
        u = jnp.tanh(half_x)
        more = 1.0 + u
        value = half_x * more
        return value, more + value * (1.0 - u)

    def silu_rows(t, r):
        value, slope_here = silu(out_ref[t, pl.ds(r * step, step)])
        rows = aligned(r, step * width)
        act[t, rows, :] = value.astype(BF16)
        slope[t, rows, :] = slope_here

    steps = height // step
    bunch = 4 if steps % 4 == 0 else 1

    def silu_frames(first, end, sends):
        def one(t, _):
            fetch(t).wait()

            def some(i, _):
                for k in range(sends):
                    send_away(msg_2, recv_2, send_2, recv_main_2, 1 + sends * ((t - first) * (steps // bunch) + i) + k)
                for k in range(bunch):
                    silu_rows(t, i * bunch + k)
                return 0

            lax.fori_loop(0, steps // bunch, some, 0)
            return 0

        lax.fori_loop(first, end, one, 0)

    sending = (messages - 1) // (2 * (steps // bunch))
    send_first(msg_2, recv_2, send_2, recv_main_2)
    silu_frames(0, sending, 2)
    for k in range(1 + 2 * sending * (steps // bunch), messages):
        send_away(msg_2, recv_2, send_2, recv_main_2, jnp.int32(k))
    silu_frames(sending, frames, 0)

    @pl.when(jnp.logical_not(has_edge))
    def _():
        edge[...] = jnp.zeros(edge.shape, BF16)

    @pl.when(has_edge)
    def _():
        pltpu.make_async_copy(edge, edge, recv_edge).wait()

    pltpu.make_async_copy(recv, recv, recv_main).wait()

    def beside(value, i):
        return turned(value, -OUT - 2 * OUT * i, 1)

    def unpack(b, _):
        tiles = [recv[b, i].astype(F32) for i in range(FIRST)]
        sides = turned(tiles[2], EARLY, 0) + edge[b, 0].astype(F32)
        for i in range(ROWS - 1):
            field[b * ROWS + i, 0:FRAMES] = turned(tiles[i // 2], EARLY * (i % 2), 0)
            halo[b * ROWS + i, 0:FRAMES] = beside(sides, i)
        field[b * ROWS + 4, 0:FRAMES] = joined(tiles[2], tiles[3])
        halo[b * ROWS + 4, 0:FRAMES] = beside(tiles[3] + edge[b, 1].astype(F32), 4)
        return 0

    def unpack_2(b, _):
        tiles = [recv_2[b, i].astype(F32) for i in range(SECOND)]
        sides = turned(tiles[2], EARLY, 0) + edge[b, 0].astype(F32)
        for i in range(ROWS - 1):
            field[b * ROWS + i, EARLY:FRAMES] = turned(tiles[i // 2], EARLY * (1 - i % 2), 0)[EARLY:]
            halo[b * ROWS + i, EARLY:FRAMES] = beside(sides, i)[EARLY:]
        halo[b * ROWS + 4, EARLY:FRAMES] = beside(tiles[2] + edge[b, 1].astype(F32), 4)[EARLY:]
        return 0

    lax.fori_loop(0, n_tile, unpack, 0, unroll=4)

    def pack_lead(k, _):
        both = [
            jnp.where(row < 2, field[2 * k + i, 0:FRAMES], turned(halo[2 * k + i, 0:FRAMES], 2, 0)) for i in range(2)
        ]
        lead[k] = joined(both[0], both[1], False, True).astype(BF16)
        return 0

    def unpack_ahead(k, _):
        tiles = ahead[k].astype(F32)
        for i in range(2):
            field[2 * k + i, FRAMES:] = turned(tiles, -4 * i, 0)
            halo[2 * k + i, FRAMES:] = turned(tiles, -4 * i - 2, 0)
        return 0

    lead_copy = pltpu.make_async_remote_copy(
        src_ref=lead, dst_ref=ahead, send_sem=lead_send, recv_sem=lead_recv,
        device_id=(jnp.maximum(tm - 1, 0), tile), device_id_type=MESH,
    )

    @pl.when(to_left)
    def _():
        lax.fori_loop(0, height // 2, pack_lead, 0, unroll=8)
        lead_copy.start()

    lane3, col3 = lane_of((1, width, LANES), 2), lane_of((1, width, LANES), 1)
    outside = jnp.logical_or(
        jnp.logical_and(col3 == 0, lane3 < OUT),
        jnp.logical_and(col3 == width - 1, lane3 >= LANES - OUT),
    )
    edge_row = jnp.zeros((width, LANES), F32)
    group = 32

    lane2 = lane_of((1, LANES), 1)

    acc[...] = jnp.zeros(acc.shape, F32)
    rest = LANES + 3 * OUT
    half[1, rest:, :] = jnp.zeros((half.shape[1] - rest, half.shape[2]), F32)

    def add_first(t):
        grad = jnp.dot(cols_t[t * LANES : (t + 2) * LANES, :], act[t], preferred_element_type=F32)
        for h in range(CORES):
            acc[0, h] += grad[:, h * (cin // CORES) : (h + 1) * (cin // CORES)]

    def add_second(t, _):
        left = jnp.concatenate([cols_t[aligned(t + 2, LANES), :], last_t[t]], axis=0)
        grad = jnp.dot(left, act[t], preferred_element_type=F32)
        for h in range(CORES):
            acc[1, h, 0:rest] += grad[:, h * (cin // CORES) : (h + 1) * (cin // CORES)]
        return 0

    for t in range(wide):
        if t == EARLY:
            pltpu.make_async_copy(recv_2, recv_2, recv_main_2).wait()
            lax.fori_loop(0, n_tile, unpack_2, 0, unroll=4)
        if t == FRAMES:
            @pl.when(to_right)
            def _():
                pltpu.make_async_copy(ahead, ahead, lead_recv).wait()

            @pl.when(jnp.logical_not(to_right))
            def _():
                ahead[...] = jnp.zeros(ahead.shape, BF16)

            lax.fori_loop(0, height // 2, unpack_ahead, 0, unroll=8)

        for g in range(height // group):
            first, end = max(g * group - 1, 0), min((g + 1) * group + 1, height)
            main = jnp.broadcast_to(field[first:end, t : t + 1, :], (end - first, width, LANES))
            side = jnp.broadcast_to(halo[first:end, t : t + 1, :], (end - first, width, LANES))
            values = jnp.where(outside, side, main).reshape((end - first) * width, LANES)
            values = pltpu.roll(values, 0, 1, stride=OUT, stride_axis=0)
            if g == 0:
                values = jnp.concatenate([edge_row, values], axis=0)
            if end == height:
                values = jnp.concatenate([values, edge_row], axis=0)
            size = group * width
            rows = slice(g * size, (g + 1) * size)
            around = values.astype(BF16)
            inside = values[width : width + size].astype(BF16)
            ahead_turned = pltpu.roll(around, 2 * OUT, 1)
            before = around[:size]
            cols[t, rows, :] = jnp.where(
                lane2 < 3 * OUT, ahead_turned[2 * width :],
                jnp.where(lane2 < 6 * OUT, pltpu.roll(inside, 5 * OUT, 1), before),
            )
            vee[t % WINDOW, rows, :] = before
            if t >= 2:
                value = jnp.where(lane2 < 3 * OUT, ahead_turned[:size], jnp.zeros_like(before))
                value = jnp.where(lane2 < 2 * OUT, pltpu.roll(vee[(t - 1) % WINDOW, rows, :], OUT, 1), value)
                last[t - 2, rows, :] = jnp.where(lane2 < OUT, vee[(t - 2) % WINDOW, rows, :], value)
        cols_t[t * LANES : (t + 1) * LANES, :] = jnp.transpose(cols[t])
        if t >= 2:
            last_t[t - 2] = jnp.transpose(last[t - 2])[0 : 3 * OUT]
        if t >= 2:
            add_first(t - 2)

    chunk = 40

    def grad_frame(t, _):
        def grad_rows(r, _):
            rows = aligned(r, chunk * width)
            left = jnp.concatenate([cols[t + kt, rows, :] for kt in range(3)] + [last[t, rows, :]], axis=1)
            grad = jnp.dot(left, weights[...], preferred_element_type=F32)
            grad = grad * slope[t, rows, :]
            out_ref[t, pl.ds(r * chunk, chunk)] = grad.reshape(chunk, width, cin).astype(BF16)
            return 0

        lax.fori_loop(0, height // chunk, grad_rows, 0, unroll=True)
        return 0

    def grad_frames(first, end):
        lax.fori_loop(first, end, grad_frame, 0)

    def drain(source, sem):
        pltpu.make_async_copy(source, source, sem).wait()

    def drain_messages(source, sem):
        if n_tm > 1:
            drain(source.at[pl.ds(0, n_tm - 1)], sem)
        if strips > 1:
            drain(source.at[0, pl.ds(0, strips - 1)], sem)

        @pl.when(block != tm)
        def _():
            drain(source.at[0, 0], sem)

    drain_messages(msg, send_main)
    drain_messages(msg_2, send_2)

    def drain_edge(k, _):
        drain(emsg.at[0, 0], send_edge)
        return 0

    lax.fori_loop(0, edges_out - self_edge, drain_edge, 0)

    @pl.when(to_left)
    def _():
        drain(lead, lead_send)

    share = mine.shape[1] // groups
    used = (acc.shape[2], rest)

    def swap(p):
        return pltpu.make_async_remote_copy(
            src_ref=acc.at[p, 1 - core, pl.ds(0, used[p])], dst_ref=half.at[p, pl.ds(0, used[p])],
            send_sem=half_sem(0, p), recv_sem=half_sem(1, p),
            device_id=(partner, tile), device_id_type=MESH,
        )

    def send_pieces(p):
        swap(p).wait()
        mine[p] = jnp.transpose(acc[p, core] + half[p]).astype(BF16)
        for k in range(1, groups):
            g = wrapped(spot + k, groups)
            pltpu.make_async_remote_copy(
                src_ref=mine.at[p, aligned(g, share)], dst_ref=pieces.at[p, spot],
                send_sem=half_sem(2, p), recv_sem=half_sem(3, p),
                device_id=(tm, y_hi * groups + g), device_id_type=MESH,
            ).start()
        pieces[p, spot] = mine[p, aligned(spot, share), :]

    def send_sums(p):
        drain(pieces.at[p, pl.ds(0, groups - 1)], half_sem(3, p))
        sums[p] = jnp.sum(pieces[p].astype(F32), axis=0)
        for k in range(n_tm):
            send(sums.at[p], quads.at[p, level], half_sem(4, p), half_sem(5, p), k, owner_tile)

    swap(0).start()
    lax.fori_loop(0, frames, add_second, 0)
    swap(1).start()
    send_pieces(0)
    grad_frames(0, SPLIT[0])
    send_pieces(1)
    grad_frames(SPLIT[0], SPLIT[1])
    send_sums(0)
    grad_frames(SPLIT[1], SPLIT[2])
    send_sums(1)
    grad_frames(SPLIT[2], frames)

    results = []
    for p in range(2):
        drain(quads.at[p], half_sem(5, p))
        drain(pieces.at[p, pl.ds(0, groups - 1)], half_sem(2, p))
        drain(quads.at[p, pl.ds(0, n_tm - 1)], half_sem(4, p))
        result = quads[p, 0]
        for k in range(1, n_tm):
            result = result + quads[p, k]
        results.append(result * scale)

    @pl.when(core != y_hi)
    def _():
        for p in range(2):
            drain(sums.at[p], half_sem(4, p))

    blocks = [results[0][:, :LANES], results[0][:, LANES:], results[1][:, :LANES]]
    for kt in range(3):
        at = 9 * kt * OUT
        kgrad_ref[:, at : at + LANES] = blocks[kt]
        kgrad_ref[:, at + LANES : at + 9 * OUT] = results[1][:, LANES + kt * OUT : LANES + (kt + 1) * OUT]


SPLIT = (1, 4, 5)


def on_device(n_tm, n_tile, scale, latent_grad, section_input, kernel):
    frames, height, width, cin = section_input.shape
    taps = kernel.shape[1]
    strips = n_tile // n_tm
    banded = jnp.transpose(latent_grad, (1, 0, 2)).reshape(ROWS, n_tm, FRAMES, strips * LANES)
    wide, count = frames + 2, height * width
    rows, share, padded = cin // CORES, cin // n_tile, 4 * LANES
    vmem = pl.BlockSpec(memory_space=pltpu.VMEM)
    return pl.pallas_call(
        functools.partial(whole, n_tm, n_tile, scale),
        out_shape=(
            pltpu.VMEM((frames, height, width, cin), BF16),
            pltpu.VMEM((share, taps), F32),
        ),
        in_specs=[pl.BlockSpec(memory_space=pl.ANY)] * 3,
        out_specs=(vmem, vmem),
        scratch_shapes=[
            pltpu.VMEM((ROWS, n_tm, FRAMES, strips * LANES), BF16),
            pltpu.VMEM((taps, cin), BF16),
            pltpu.VMEM((n_tm, strips, FIRST, FRAMES, LANES), BF16),
            pltpu.VMEM((n_tm, strips, SECOND, FRAMES, LANES), BF16),
            pltpu.VMEM((2, n_tm, 2, FRAMES, LANES), BF16),
            pltpu.VMEM((n_tile, FIRST, FRAMES, LANES), BF16),
            pltpu.VMEM((n_tile, SECOND, FRAMES, LANES), BF16),
            pltpu.VMEM((n_tile, 2, FRAMES, LANES), BF16),
            pltpu.VMEM((height // 2, FRAMES, LANES), BF16),
            pltpu.VMEM((height // 2, FRAMES, LANES), BF16),
            pltpu.VMEM((frames, count, cin), BF16),
            pltpu.VMEM((frames, count, cin), F32),
            pltpu.VMEM((height, 2 * FRAMES, LANES), F32),
            pltpu.VMEM((height, 2 * FRAMES, LANES), F32),
            pltpu.VMEM((WINDOW, count, LANES), BF16),
            pltpu.VMEM((wide, count, LANES), BF16),
            pltpu.VMEM((wide * LANES, count), BF16),
            pltpu.VMEM((frames, count, LANES), BF16),
            pltpu.VMEM((frames, 3 * OUT, count), BF16),
            pltpu.VMEM((padded, cin), BF16),
            pltpu.VMEM((2, CORES, 2 * LANES, rows), F32),
            pltpu.VMEM((2, 2 * LANES, rows), F32),
            pltpu.VMEM((2, rows, 2 * LANES), BF16),
            pltpu.VMEM((2, n_tile // CORES, share, 2 * LANES), BF16),
            pltpu.VMEM((2, share, 2 * LANES), F32),
            pltpu.VMEM((2, n_tm, share, 2 * LANES), F32),
            pltpu.SemaphoreType.DMA((frames,)),
            pltpu.SemaphoreType.DMA((26,)),
        ],
        compiler_params=pltpu.CompilerParams(
            collective_id=0, has_side_effects=True, vmem_limit_bytes=VMEM_LIMIT
        ),
    )(banded, section_input, jnp.transpose(kernel))


VMEM_LIMIT = 53 << 20


def solution(mesh):
    n_tm, n_tile = mesh.shape["tm"], mesh.shape["tile"]
    positions = n_tm * FRAMES * n_tile * ROWS * n_tile * STRIP
    return jax.shard_map(
        functools.partial(on_device, n_tm, n_tile, 1.0 / math.sqrt(positions)),
        mesh=mesh,
        in_specs=(P(None, "tile", "tm"), P("tm", None, "tile", None), P()),
        out_specs=(P("tm", None, "tile", None), P("tile", None)),
        check_vma=False,
    )
```

```python
import functools
import math

import jax
import jax.numpy as jnp
from jax import lax
from jax.experimental import pallas as pl
from jax.experimental.pallas import tpu as pltpu
from jax.sharding import PartitionSpec as P

MESH = pl.DeviceIdType.MESH
F32, BF16 = jnp.float32, jnp.bfloat16
LANES = 128
OUT = 16
STRIP = 8
FRAMES = 8
ROWS = 5
FIRST = 4
SECOND = 3
EARLY = 4
CORES = 2
KEPT = 4
WINDOW = 3


def lane_of(shape, axis):
    return lax.broadcasted_iota(jnp.int32, shape, axis)


def aligned(index, size):
    return pl.ds(pl.multiple_of(index * size, size), size)


def turned(value, shift, axis):
    shift %= value.shape[axis]
    return pltpu.roll(value, shift, axis) if shift else value


def wrapped(index, size):
    return jnp.where(index >= size, index - size, index)


def strip_halo(left, right):
    lane = lane_of((1, LANES), 1)
    rows = []
    for i in range(ROWS):
        value = jnp.zeros((FRAMES, LANES), F32)
        if right is not None:
            value = jnp.where(lane >= LANES - OUT, right[i], value)
        if left is not None:
            value = jnp.where(lane < OUT, left[i], value)
        rows.append(turned(value, OUT + 2 * OUT * i, 1))
    return rows[0] + rows[1] + rows[2] + rows[3], rows[4]


def joined(upper, lower, turn_upper=False, turn_lower=False):
    upper = turned(upper, EARLY, 0) if turn_upper else upper
    lower = turned(lower, EARLY, 0) if turn_lower else lower
    return jnp.where(lane_of((FRAMES, 1), 0) < EARLY, upper, lower)


def whole(
    n_tm, n_tile, scale, grad_hbm, x_ref, kernel_hbm, out_ref, kgrad_ref,
    grad_ref, kernel_ref, msg, msg_2, emsg, recv, recv_2, edge, lead, ahead, act, slope, field, halo, vee, cols, cols_t, last, last_t,
    weights, acc, part, mine, mine_half, pieces, sums, quads, in_sem, sems,
):
    frames, height, width, cin = out_ref.shape
    wide, count = frames + 2, height * width
    tm, tile = lax.axis_index("tm"), lax.axis_index("tile")
    strips = n_tile // n_tm
    block = tile // strips
    place_in_block = lax.rem(tile, strips)
    from_left = jnp.logical_and(place_in_block == 0, block > 0)
    from_right = jnp.logical_and(place_in_block == strips - 1, block < n_tm - 1)
    has_edge = jnp.logical_or(from_left, from_right)
    edge_block = jnp.where(place_in_block == 0, block - 1, block + 1)
    messages = n_tm * strips
    send_main, send_edge, recv_main, recv_edge = (sems.at[i] for i in range(4))
    swap_send, swap_recv, piece_send, piece_recv = (sems.at[i] for i in range(4, 8))
    send_2, recv_main_2 = sems.at[10], sems.at[11]
    row_send, row_recv = sems.at[12], sems.at[13]
    lead_send, lead_recv = sems.at[14], sems.at[15]
    core, y_lo = lax.rem(tm, CORES), tm // CORES
    groups = n_tile // CORES
    y_hi, spot = tile // groups, lax.rem(tile, groups)
    partner = tm + 1 - 2 * core
    level = y_hi * CORES + y_lo
    owner_tile = core * groups + spot

    def is_me(target_tm, target_tile):
        return jnp.logical_and(target_tm == tm, target_tile == tile)

    grad_copy = pltpu.make_async_copy(grad_hbm, grad_ref, sems.at[8])
    kernel_copy = pltpu.make_async_copy(kernel_hbm, kernel_ref, sems.at[9])
    grad_copy.start()
    kernel_copy.start()

    def fetch(t):
        return pltpu.make_async_copy(x_ref.at[t], out_ref.at[t], in_sem.at[t])

    for t in range(frames):
        fetch(t).start()

    barrier = pltpu.get_barrier_semaphore()

    def hail(target_tm, target_tile):
        pl.semaphore_signal(barrier, inc=1, device_id=(target_tm, target_tile), device_id_type=MESH)

    for k in range(1, n_tile):
        hail(block, wrapped(tile + k, n_tile))

    @pl.when(block != tm)
    def _():
        hail(block, tile)

    @pl.when(has_edge)
    def _():
        for k in range(1, n_tile):
            hail(edge_block, wrapped(tile + k, n_tile))

        @pl.when(edge_block != tm)
        def _():
            hail(edge_block, tile)

    @pl.when(tm < n_tm - 1)
    def _():
        hail(tm + 1, tile)

    hail(partner, tile)
    for k in range(1, groups):
        hail(tm, y_hi * groups + wrapped(spot + k, groups))
    for k in range(n_tm):
        source = (k % CORES) * CORES + y_hi, (k // CORES) * groups + spot

        @pl.when(jnp.logical_not(is_me(*source)))
        def _():
            hail(*source)

    r, c = lane_of((LANES, LANES), 0), lane_of((LANES, LANES), 1)
    same = jnp.logical_and(r // OUT + c // OUT == STRIP - 1, lax.rem(r, OUT) == lax.rem(c, OUT))
    flip = jnp.where(same, 1.0, 0.0).astype(BF16)
    row = lane_of((FRAMES, 1), 0)
    nothing = jnp.zeros((FRAMES, LANES), F32)
    grad_copy.wait()
    flipped, halos = [], []
    for t in range(n_tm):
        rows = grad_ref[:, t].astype(F32).reshape(ROWS * FRAMES, strips * LANES).astype(BF16)
        here = [
            jnp.dot(rows[:, s * LANES : (s + 1) * LANES], flip, preferred_element_type=F32)
            .reshape(ROWS, FRAMES, LANES)
            for s in range(strips)
        ]
        flipped.append(here)
        padded = [None, None] + here + [None, None]
        halos.append([strip_halo(padded[s], padded[s + 2]) for s in range(strips + 2)])
    for t in range(n_tm):
        for s in range(strips):
            here, (first, second) = flipped[t][s], halos[t][s + 1]
            tiles = [
                joined(here[0], here[1], False, True), joined(here[2], here[3], False, True),
                joined(here[4], first, False, True), joined(second, here[4]),
            ]
            for i, value in enumerate(tiles):
                msg[t, s, i] = value.astype(BF16)
        for side, s in ((0, strips + 1), (1, 0)):
            for i, value in enumerate(halos[t][s]):
                emsg[side, t, i] = value.astype(BF16)

    self_main = (block == tm).astype(jnp.int32)
    to_right, to_left = tm < n_tm - 1, tm > 0
    right_tile, left_tile = (tm + 1) * strips, tm * strips - 1
    self_edge = (
        jnp.logical_and(to_right, tile == right_tile).astype(jnp.int32)
        + jnp.logical_and(to_left, tile == left_tile).astype(jnp.int32)
    )
    edges_out = n_tm * (to_right.astype(jnp.int32) + to_left.astype(jnp.int32))
    self_owner = (core == y_hi).astype(jnp.int32)
    exchange_out = messages - self_main + edges_out - self_edge
    pl.semaphore_wait(barrier, exchange_out + 1 + groups - 1 + n_tm - self_owner + to_left.astype(jnp.int32))

    def send(source, target, send_sem, recv_sem, target_tm, target_tile):
        own = is_me(target_tm, target_tile)

        @pl.when(jnp.logical_not(own))
        def _():
            pltpu.make_async_remote_copy(
                src_ref=source, dst_ref=target, send_sem=send_sem, recv_sem=recv_sem,
                device_id=(target_tm, target_tile), device_id_type=MESH,
            ).start()

        @pl.when(own)
        def _():
            pltpu.make_async_copy(source, target, recv_sem).start()

    def send_edges(t, _):
        @pl.when(to_right)
        def _():
            send(emsg.at[0, t], edge.at[tile], send_edge, recv_edge, t, right_tile)

        @pl.when(to_left)
        def _():
            send(emsg.at[1, t], edge.at[tile], send_edge, recv_edge, t, left_tile)

        return 0

    def send_all(source, target, send_sem, recv_sem):
        for k in range(messages):
            t, s = wrapped(tm + k // strips, n_tm), wrapped(place_in_block + k % strips, strips)
            if k == 0:
                send(source.at[t, s], target.at[tile], send_sem, recv_sem, t, tm * strips + s)
            else:
                pltpu.make_async_remote_copy(
                    src_ref=source.at[t, s], dst_ref=target.at[tile], send_sem=send_sem, recv_sem=recv_sem,
                    device_id=(t, tm * strips + s), device_id_type=MESH,
                ).start()

    lax.fori_loop(0, n_tm, send_edges, 0)
    send_all(msg, recv, send_main, recv_main)

    for t in range(n_tm):
        for s in range(strips):
            here, (first, second) = flipped[t][s], halos[t][s + 1]
            tiles = [
                joined(here[0], here[1], True), joined(here[2], here[3], True), joined(first, second, True),
            ]
            for i, value in enumerate(tiles):
                msg_2[t, s, i] = value.astype(BF16)

    kernel_copy.wait()
    weights[...] = jnp.zeros(weights.shape, BF16)
    for kt in range(3):
        taps = kernel_ref[9 * kt * OUT : 9 * (kt + 1) * OUT, :]
        taps = (0.5 * taps.astype(F32)).astype(BF16)
        weights[kt * LANES : (kt + 1) * LANES, :] = taps[:LANES]
        weights[3 * LANES + kt * OUT : 3 * LANES + (kt + 1) * OUT, :] = taps[LANES:]

    step = 8

    def silu(x):
        half_x = 0.5 * x.astype(F32).reshape(x.shape[0] * width, cin)
        u = jnp.tanh(half_x)
        more = 1.0 + u
        value = half_x * more
        return value, lambda: more + value * (1.0 - u)

    def silu_frames(first, end, kept):
        def one(t, _):
            fetch(t).wait()

            def silu_rows(r, _):
                value, slope_of = silu(out_ref[t, pl.ds(r * step, step)])
                rows = aligned(r, step * width)
                act[t, rows, :] = value.astype(BF16)
                if kept:
                    slope[t, rows, :] = slope_of()
                return 0

            lax.fori_loop(0, height // step, silu_rows, 0, unroll=4)
            return 0

        lax.fori_loop(first, end, one, 0)

    silu_frames(0, KEPT, True)
    send_all(msg_2, recv_2, send_2, recv_main_2)
    silu_frames(KEPT, frames, False)

    @pl.when(jnp.logical_not(has_edge))
    def _():
        edge[...] = jnp.zeros(edge.shape, BF16)

    @pl.when(has_edge)
    def _():
        pltpu.make_async_copy(edge, edge, recv_edge).wait()

    pltpu.make_async_copy(recv, recv, recv_main).wait()

    def beside(value, i):
        return turned(value, -OUT - 2 * OUT * i, 1)

    def unpack(b, _):
        tiles = [recv[b, i].astype(F32) for i in range(FIRST)]
        sides = turned(tiles[2], EARLY, 0) + edge[b, 0].astype(F32)
        for i in range(ROWS - 1):
            field[b * ROWS + i, 0:FRAMES] = turned(tiles[i // 2], EARLY * (i % 2), 0)
            halo[b * ROWS + i, 0:FRAMES] = beside(sides, i)
        field[b * ROWS + 4, 0:FRAMES] = joined(tiles[2], tiles[3])
        halo[b * ROWS + 4, 0:FRAMES] = beside(tiles[3] + edge[b, 1].astype(F32), 4)
        return 0

    def unpack_2(b, _):
        tiles = [recv_2[b, i].astype(F32) for i in range(SECOND)]
        sides = turned(tiles[2], EARLY, 0) + edge[b, 0].astype(F32)
        for i in range(ROWS - 1):
            field[b * ROWS + i, EARLY:FRAMES] = turned(tiles[i // 2], EARLY * (1 - i % 2), 0)[EARLY:]
            halo[b * ROWS + i, EARLY:FRAMES] = beside(sides, i)[EARLY:]
        halo[b * ROWS + 4, EARLY:FRAMES] = beside(tiles[2] + edge[b, 1].astype(F32), 4)[EARLY:]
        return 0

    lax.fori_loop(0, n_tile, unpack, 0, unroll=4)

    def pack_lead(k, _):
        both = [
            jnp.where(row < 2, field[2 * k + i, 0:FRAMES], turned(halo[2 * k + i, 0:FRAMES], 2, 0)) for i in range(2)
        ]
        lead[k] = joined(both[0], both[1], False, True).astype(BF16)
        return 0

    def unpack_ahead(k, _):
        tiles = ahead[k].astype(F32)
        for i in range(2):
            field[2 * k + i, FRAMES:] = turned(tiles, -4 * i, 0)
            halo[2 * k + i, FRAMES:] = turned(tiles, -4 * i - 2, 0)
        return 0

    lead_copy = pltpu.make_async_remote_copy(
        src_ref=lead, dst_ref=ahead, send_sem=lead_send, recv_sem=lead_recv,
        device_id=(jnp.maximum(tm - 1, 0), tile), device_id_type=MESH,
    )

    @pl.when(to_left)
    def _():
        lax.fori_loop(0, height // 2, pack_lead, 0, unroll=8)
        lead_copy.start()

    lane3, col3 = lane_of((1, width, LANES), 2), lane_of((1, width, LANES), 1)
    outside = jnp.logical_or(
        jnp.logical_and(col3 == 0, lane3 < OUT),
        jnp.logical_and(col3 == width - 1, lane3 >= LANES - OUT),
    )
    edge_rows = jnp.zeros((width, LANES), F32)
    group = 16
    for t in range(WINDOW):
        vee[t, 0:width, :] = edge_rows
        vee[t, (height + 1) * width : (height + 2) * width, :] = edge_rows

    lane2 = lane_of((1, LANES), 1)

    def tap(t, g, shift_rows, shift):
        at = pl.ds(pl.multiple_of((g * group + shift_rows) * width, width), group * width)
        return turned(vee[t % WINDOW, at, :].astype(BF16), shift, 1)

    acc[...] = jnp.zeros(acc.shape, F32)

    def add_frame(t):
        left = jnp.concatenate([cols_t[t * LANES : (t + 3) * LANES, :], last_t[t]], axis=0)
        acc[...] += jnp.dot(left, act[t], preferred_element_type=F32)

    for t in range(wide):
        if t == EARLY:
            pltpu.make_async_copy(recv_2, recv_2, recv_main_2).wait()
            lax.fori_loop(0, n_tile, unpack_2, 0, unroll=4)
        if t == FRAMES:
            @pl.when(to_right)
            def _():
                pltpu.make_async_copy(ahead, ahead, lead_recv).wait()

            @pl.when(jnp.logical_not(to_right))
            def _():
                ahead[...] = jnp.zeros(ahead.shape, BF16)

            lax.fori_loop(0, height // 2, unpack_ahead, 0, unroll=8)

        def spread(g, _, t=t):
            rows = pl.ds(g * group, group)
            main = jnp.broadcast_to(field[rows, t : t + 1, :], (group, width, LANES))
            side = jnp.broadcast_to(halo[rows, t : t + 1, :], (group, width, LANES))
            at = pl.ds(pl.multiple_of((g * group + 1) * width, width), group * width)
            values = jnp.where(outside, side, main).reshape(group * width, LANES)
            vee[t % WINDOW, at, :] = pltpu.roll(values, 0, 1, stride=OUT, stride_axis=0)
            return 0

        def fill(g, _, t=t):
            rows = aligned(g, group * width)
            s0, s1, s2 = tap(t, g, 2, 2 * OUT), tap(t, g, 1, 5 * OUT), tap(t, g, 0, 0)
            cols[t, rows, :] = jnp.where(lane2 < 3 * OUT, s0, jnp.where(lane2 < 6 * OUT, s1, s2))
            return 0

        def fill_last(g, _, t=t):
            rows = aligned(g, group * width)
            taps = [tap(t - 2 + kt, g, 0, kt * OUT) for kt in range(3)]
            value = jnp.where(lane2 < 3 * OUT, taps[2], jnp.zeros_like(taps[2]))
            last[t - 2, rows, :] = jnp.where(lane2 < OUT, taps[0], jnp.where(lane2 < 2 * OUT, taps[1], value))
            return 0

        lax.fori_loop(0, height // group, spread, 0, unroll=True)
        lax.fori_loop(0, height // group, fill, 0, unroll=True)
        cols_t[t * LANES : (t + 1) * LANES, :] = jnp.transpose(cols[t])
        if t >= 2:
            lax.fori_loop(0, height // group, fill_last, 0, unroll=True)
            last_t[t - 2] = jnp.transpose(last[t - 2])[0 : 3 * OUT]
        if t >= 3:
            add_frame(t - 3)
    add_frame(frames - 1)

    pieces_of_total = []
    for kt in range(3):
        pieces_of_total.append(acc[kt * LANES : (kt + 1) * LANES, :])
        pieces_of_total.append(acc[3 * LANES + kt * OUT : 3 * LANES + (kt + 1) * OUT, :])
    pieces_of_total.append(jnp.zeros((part.shape[1] - 27 * OUT, cin), F32))
    part[...] = jnp.transpose(jnp.concatenate(pieces_of_total, axis=0))

    chunk = 40

    def grad_frame(t, kept):
        def grad_rows(r, _):
            rows = aligned(r, chunk * width)
            left = jnp.concatenate([cols[t + kt, rows, :] for kt in range(3)] + [last[t, rows, :]], axis=1)
            grad = jnp.dot(left, weights[...], preferred_element_type=F32)
            grad = grad * (slope[t, rows, :] if kept else silu(out_ref[t, pl.ds(r * chunk, chunk)])[1]())
            out_ref[t, pl.ds(r * chunk, chunk)] = grad.reshape(chunk, width, cin).astype(BF16)
            return 0

        lax.fori_loop(0, height // chunk, grad_rows, 0, unroll=True)

    def grad_frames(first, end):
        for kept, a, b in ((True, first, min(end, KEPT)), (False, max(first, KEPT), end)):
            def one(t, _, kept=kept):
                grad_frame(t, kept)
                return 0

            if a < b:
                lax.fori_loop(a, b, one, 0)

    def drain(source, sem):
        pltpu.make_async_copy(source, source, sem).wait()

    def drain_messages(source, sem):
        if n_tm > 1:
            drain(source.at[pl.ds(0, n_tm - 1)], sem)
        if strips > 1:
            drain(source.at[0, pl.ds(0, strips - 1)], sem)

        @pl.when(block != tm)
        def _():
            drain(source.at[0, 0], sem)

    drain_messages(msg, send_main)
    drain_messages(msg_2, send_2)

    def drain_edge(k, _):
        drain(emsg.at[0, 0], send_edge)
        return 0

    lax.fori_loop(0, edges_out - self_edge, drain_edge, 0)

    @pl.when(to_left)
    def _():
        drain(lead, lead_send)

    rows = mine.shape[0]
    share = rows // groups
    swap = pltpu.make_async_remote_copy(
        src_ref=part.at[aligned(1 - core, rows)], dst_ref=mine,
        send_sem=swap_send, recv_sem=swap_recv,
        device_id=(partner, tile), device_id_type=MESH,
    )
    swap.start()
    grad_frames(0, SPLIT[0])
    swap.wait()
    mine[...] += part[aligned(core, rows), :]

    mine_half[...] = mine[...].astype(BF16)

    for k in range(1, groups):
        g = wrapped(spot + k, groups)
        pltpu.make_async_remote_copy(
            src_ref=mine_half.at[aligned(g, share)], dst_ref=pieces.at[spot],
            send_sem=piece_send, recv_sem=piece_recv,
            device_id=(tm, y_hi * groups + g), device_id_type=MESH,
        ).start()
    pieces[spot] = mine_half[aligned(spot, share), :]
    grad_frames(SPLIT[0], SPLIT[1])
    others = pieces.at[pl.ds(0, groups - 1)]
    pltpu.make_async_copy(others, others, piece_recv).wait()
    sums[...] = jnp.sum(pieces[...].astype(F32), axis=0)

    for k in range(n_tm):
        send(sums, quads.at[level], row_send, row_recv, k, owner_tile)
    grad_frames(SPLIT[1], frames)
    pltpu.make_async_copy(quads, quads, row_recv).wait()

    drain(others, piece_send)
    drain(quads.at[pl.ds(0, n_tm - 1)], row_send)

    @pl.when(core != y_hi)
    def _():
        drain(sums, row_send)

    result = quads[0]
    for k in range(1, n_tm):
        result = result + quads[k]
    kgrad_ref[...] = (result * scale)[:, : kgrad_ref.shape[1]]


SPLIT = (1, 6)


def on_device(n_tm, n_tile, scale, latent_grad, section_input, kernel):
    frames, height, width, cin = section_input.shape
    taps = kernel.shape[1]
    strips = n_tile // n_tm
    banded = jnp.transpose(latent_grad, (1, 0, 2)).reshape(ROWS, n_tm, FRAMES, strips * LANES)
    wide, count = frames + 2, height * width
    rows, share, padded = cin // CORES, cin // n_tile, 4 * LANES
    vmem = pl.BlockSpec(memory_space=pltpu.VMEM)
    return pl.pallas_call(
        functools.partial(whole, n_tm, n_tile, scale),
        out_shape=(
            pltpu.VMEM((frames, height, width, cin), BF16),
            pltpu.VMEM((share, taps), F32),
        ),
        in_specs=[pl.BlockSpec(memory_space=pl.ANY)] * 3,
        out_specs=(vmem, vmem),
        scratch_shapes=[
            pltpu.VMEM((ROWS, n_tm, FRAMES, strips * LANES), BF16),
            pltpu.VMEM((taps, cin), BF16),
            pltpu.VMEM((n_tm, strips, FIRST, FRAMES, LANES), BF16),
            pltpu.VMEM((n_tm, strips, SECOND, FRAMES, LANES), BF16),
            pltpu.VMEM((2, n_tm, 2, FRAMES, LANES), BF16),
            pltpu.VMEM((n_tile, FIRST, FRAMES, LANES), BF16),
            pltpu.VMEM((n_tile, SECOND, FRAMES, LANES), BF16),
            pltpu.VMEM((n_tile, 2, FRAMES, LANES), BF16),
            pltpu.VMEM((height // 2, FRAMES, LANES), BF16),
            pltpu.VMEM((height // 2, FRAMES, LANES), BF16),
            pltpu.VMEM((frames, count, cin), BF16),
            pltpu.VMEM((KEPT, count, cin), F32),
            pltpu.VMEM((height, 2 * FRAMES, LANES), F32),
            pltpu.VMEM((height, 2 * FRAMES, LANES), F32),
            pltpu.VMEM((WINDOW, (height + 2) * width, LANES), F32),
            pltpu.VMEM((wide, count, LANES), BF16),
            pltpu.VMEM((wide * LANES, count), BF16),
            pltpu.VMEM((frames, count, LANES), BF16),
            pltpu.VMEM((frames, 3 * OUT, count), BF16),
            pltpu.VMEM((padded, cin), BF16),
            pltpu.VMEM((27 * OUT, cin), F32),
            pltpu.VMEM((cin, padded), F32),
            pltpu.VMEM((rows, padded), F32),
            pltpu.VMEM((rows, padded), BF16),
            pltpu.VMEM((n_tile // CORES, share, padded), BF16),
            pltpu.VMEM((share, padded), F32),
            pltpu.VMEM((n_tm, share, padded), F32),
            pltpu.SemaphoreType.DMA((frames,)),
            pltpu.SemaphoreType.DMA((16,)),
        ],
        compiler_params=pltpu.CompilerParams(
            collective_id=0, has_side_effects=True, vmem_limit_bytes=VMEM_LIMIT
        ),
    )(banded, section_input, jnp.transpose(kernel))


VMEM_LIMIT = 53 << 20


def solution(mesh):
    n_tm, n_tile = mesh.shape["tm"], mesh.shape["tile"]
    positions = n_tm * FRAMES * n_tile * ROWS * n_tile * STRIP
    return jax.shard_map(
        functools.partial(on_device, n_tm, n_tile, 1.0 / math.sqrt(positions)),
        mesh=mesh,
        in_specs=(P(None, "tile", "tm"), P("tm", None, "tile", None), P()),
        out_specs=(P("tm", None, "tile", None), P("tile", None)),
        check_vma=False,
    )
```

```python
import functools
import math

import jax
import jax.numpy as jnp
from jax import lax
from jax.experimental import pallas as pl
from jax.experimental.pallas import tpu as pltpu
from jax.sharding import PartitionSpec as P

MESH = pl.DeviceIdType.MESH
F32, BF16 = jnp.float32, jnp.bfloat16
LANES = 128
OUT = 16
STRIP = 8
FRAMES = 8
ROWS = 5
FIRST = 4
SECOND = 3
EARLY = 4
CORES = 2
WINDOW = 3


def lane_of(shape, axis):
    return lax.broadcasted_iota(jnp.int32, shape, axis)


def aligned(index, size):
    return pl.ds(pl.multiple_of(index * size, size), size)


def turned(value, shift, axis):
    shift %= value.shape[axis]
    return pltpu.roll(value, shift, axis) if shift else value


def wrapped(index, size):
    return jnp.where(index >= size, index - size, index)


def strip_halo(left, right):
    lane = lane_of((1, LANES), 1)
    rows = []
    for i in range(ROWS):
        value = jnp.zeros((FRAMES, LANES), F32)
        if right is not None:
            value = jnp.where(lane >= LANES - OUT, right[i], value)
        if left is not None:
            value = jnp.where(lane < OUT, left[i], value)
        rows.append(turned(value, OUT + 2 * OUT * i, 1))
    return rows[0] + rows[1] + rows[2] + rows[3], rows[4]


def joined(upper, lower, turn_upper=False, turn_lower=False):
    upper = turned(upper, EARLY, 0) if turn_upper else upper
    lower = turned(lower, EARLY, 0) if turn_lower else lower
    return jnp.where(lane_of((FRAMES, 1), 0) < EARLY, upper, lower)


def whole(
    n_tm, n_tile, scale, grad_hbm, x_ref, kernel_hbm, out_ref, kgrad_ref,
    grad_ref, kernel_ref, msg, msg_2, emsg, recv, recv_2, edge, lead, ahead, act, slope, field, halo, vee, cols, cols_t, last, last_t,
    weights, acc, part, mine, mine_half, pieces, sums, quads, in_sem, sems,
):
    frames, height, width, cin = out_ref.shape
    wide, count = frames + 2, height * width
    tm, tile = lax.axis_index("tm"), lax.axis_index("tile")
    strips = n_tile // n_tm
    block = tile // strips
    place_in_block = lax.rem(tile, strips)
    from_left = jnp.logical_and(place_in_block == 0, block > 0)
    from_right = jnp.logical_and(place_in_block == strips - 1, block < n_tm - 1)
    has_edge = jnp.logical_or(from_left, from_right)
    edge_block = jnp.where(place_in_block == 0, block - 1, block + 1)
    messages = n_tm * strips
    send_main, send_edge, recv_main, recv_edge = (sems.at[i] for i in range(4))
    swap_send, swap_recv, piece_send, piece_recv = (sems.at[i] for i in range(4, 8))
    send_2, recv_main_2 = sems.at[10], sems.at[11]
    row_send, row_recv = sems.at[12], sems.at[13]
    lead_send, lead_recv = sems.at[14], sems.at[15]
    core, y_lo = lax.rem(tm, CORES), tm // CORES
    groups = n_tile // CORES
    y_hi, spot = tile // groups, lax.rem(tile, groups)
    partner = tm + 1 - 2 * core
    level = y_hi * CORES + y_lo
    owner_tile = core * groups + spot

    def is_me(target_tm, target_tile):
        return jnp.logical_and(target_tm == tm, target_tile == tile)

    grad_copy = pltpu.make_async_copy(grad_hbm, grad_ref, sems.at[8])
    kernel_copy = pltpu.make_async_copy(kernel_hbm, kernel_ref, sems.at[9])
    grad_copy.start()
    kernel_copy.start()

    def fetch(t):
        return pltpu.make_async_copy(x_ref.at[t], out_ref.at[t], in_sem.at[t])

    for t in range(frames):
        fetch(t).start()

    barrier = pltpu.get_barrier_semaphore()

    def hail(target_tm, target_tile):
        pl.semaphore_signal(barrier, inc=1, device_id=(target_tm, target_tile), device_id_type=MESH)

    for k in range(1, n_tile):
        hail(block, wrapped(tile + k, n_tile))

    @pl.when(block != tm)
    def _():
        hail(block, tile)

    @pl.when(has_edge)
    def _():
        for k in range(1, n_tile):
            hail(edge_block, wrapped(tile + k, n_tile))

        @pl.when(edge_block != tm)
        def _():
            hail(edge_block, tile)

    @pl.when(tm < n_tm - 1)
    def _():
        hail(tm + 1, tile)

    hail(partner, tile)
    for k in range(1, groups):
        hail(tm, y_hi * groups + wrapped(spot + k, groups))
    for k in range(n_tm):
        source = (k % CORES) * CORES + y_hi, (k // CORES) * groups + spot

        @pl.when(jnp.logical_not(is_me(*source)))
        def _():
            hail(*source)

    r, c = lane_of((LANES, LANES), 0), lane_of((LANES, LANES), 1)
    same = jnp.logical_and(r // OUT + c // OUT == STRIP - 1, lax.rem(r, OUT) == lax.rem(c, OUT))
    flip = jnp.where(same, 1.0, 0.0).astype(BF16)
    row = lane_of((FRAMES, 1), 0)
    nothing = jnp.zeros((FRAMES, LANES), F32)
    grad_copy.wait()
    rows = [grad_ref[:, t].astype(F32).reshape(ROWS * FRAMES, strips * LANES) for t in range(n_tm)]
    rows = jnp.concatenate(
        [rows[t][:, s * LANES : (s + 1) * LANES] for t in range(n_tm) for s in range(strips)], axis=0
    )
    rows = jnp.dot(rows.astype(BF16), flip, preferred_element_type=F32).reshape(n_tm, strips, ROWS, FRAMES, LANES)
    flipped, halos = [], []
    for t in range(n_tm):
        here = [rows[t, s] for s in range(strips)]
        flipped.append(here)
        padded = [None, None] + here + [None, None]
        halos.append([strip_halo(padded[s], padded[s + 2]) for s in range(strips + 2)])
    self_main = (block == tm).astype(jnp.int32)
    to_right, to_left = tm < n_tm - 1, tm > 0
    right_tile, left_tile = (tm + 1) * strips, tm * strips - 1
    self_edge = (
        jnp.logical_and(to_right, tile == right_tile).astype(jnp.int32)
        + jnp.logical_and(to_left, tile == left_tile).astype(jnp.int32)
    )
    edges_out = n_tm * (to_right.astype(jnp.int32) + to_left.astype(jnp.int32))
    self_owner = (core == y_hi).astype(jnp.int32)
    exchange_out = messages - self_main + edges_out - self_edge
    all_here = (exchange_out + 1 + groups - 1 + n_tm - self_owner + to_left.astype(jnp.int32))

    def send(source, target, send_sem, recv_sem, target_tm, target_tile):
        own = is_me(target_tm, target_tile)

        @pl.when(jnp.logical_not(own))
        def _():
            pltpu.make_async_remote_copy(
                src_ref=source, dst_ref=target, send_sem=send_sem, recv_sem=recv_sem,
                device_id=(target_tm, target_tile), device_id_type=MESH,
            ).start()

        @pl.when(own)
        def _():
            pltpu.make_async_copy(source, target, recv_sem).start()

    def send_block(source, target, send_sem, recv_sem, t):
        for k in range(strips):
            s = wrapped(place_in_block + k, strips)
            if k == 0:
                send(source.at[t, s], target.at[tile], send_sem, recv_sem, t, tm * strips + s)
            else:
                pltpu.make_async_remote_copy(
                    src_ref=source.at[t, s], dst_ref=target.at[tile], send_sem=send_sem, recv_sem=recv_sem,
                    device_id=(t, tm * strips + s), device_id_type=MESH,
                ).start()

    def make_block(t):
        for s in range(strips):
            here, (first, second) = flipped[t][s], halos[t][s + 1]
            tiles = [
                joined(here[0], here[1], False, True), joined(here[2], here[3], False, True),
                joined(here[4], first, False, True), joined(second, here[4]),
            ]
            for i, value in enumerate(tiles):
                msg[t, s, i] = value.astype(BF16)
        for side, s in ((0, strips + 1), (1, 0)):
            for i, value in enumerate(halos[t][s]):
                emsg[side, t, i] = value.astype(BF16)

    def leave_block(t):
        send_block(msg, recv, send_main, recv_main, t)

        @pl.when(to_right)
        def _():
            send(emsg.at[0, t], edge.at[tile], send_edge, recv_edge, t, right_tile)

        @pl.when(to_left)
        def _():
            send(emsg.at[1, t], edge.at[tile], send_edge, recv_edge, t, left_tile)

    ready = n_tm // 2
    for t in range(ready):
        make_block(t)
    pl.semaphore_wait(barrier, all_here)
    for t in range(n_tm):
        leave_block(t)
        if ready + t < n_tm:
            make_block(ready + t)

    for t in range(n_tm):
        for s in range(strips):
            here, (first, second) = flipped[t][s], halos[t][s + 1]
            tiles = [
                joined(here[0], here[1], True), joined(here[2], here[3], True), joined(first, second, True),
            ]
            for i, value in enumerate(tiles):
                msg_2[t, s, i] = value.astype(BF16)

    kernel_copy.wait()
    weights[...] = jnp.zeros(weights.shape, BF16)
    for kt in range(3):
        taps = kernel_ref[9 * kt * OUT : 9 * (kt + 1) * OUT, :]
        taps = (0.5 * taps.astype(F32)).astype(BF16)
        weights[kt * LANES : (kt + 1) * LANES, :] = taps[:LANES]
        weights[3 * LANES + kt * OUT : 3 * LANES + (kt + 1) * OUT, :] = taps[LANES:]

    step = 8

    def silu_frame(t, _):
        fetch(t).wait()

        def silu_rows(r, _):
            half_x = 0.5 * out_ref[t, pl.ds(r * step, step)].astype(F32).reshape(step * width, cin)
            u = jnp.tanh(half_x)
            more = 1.0 + u
            value = half_x * more
            rows = aligned(r, step * width)
            act[t, rows, :] = value.astype(BF16)
            slope[t, rows, :] = more + value * (1.0 - u)
            return 0

        lax.fori_loop(0, height // step, silu_rows, 0, unroll=4)
        return 0

    lax.fori_loop(0, EARLY, silu_frame, 0)
    for t in range(n_tm):
        send_block(msg_2, recv_2, send_2, recv_main_2, t)
    lax.fori_loop(EARLY, frames, silu_frame, 0)

    @pl.when(jnp.logical_not(has_edge))
    def _():
        edge[...] = jnp.zeros(edge.shape, BF16)

    @pl.when(has_edge)
    def _():
        pltpu.make_async_copy(edge, edge, recv_edge).wait()

    pltpu.make_async_copy(recv, recv, recv_main).wait()

    def beside(value, i):
        return turned(value, -OUT - 2 * OUT * i, 1)

    def unpack(b, _):
        tiles = [recv[b, i].astype(F32) for i in range(FIRST)]
        sides = turned(tiles[2], EARLY, 0) + edge[b, 0].astype(F32)
        for i in range(ROWS - 1):
            field[b * ROWS + i, 0:FRAMES] = turned(tiles[i // 2], EARLY * (i % 2), 0)
            halo[b * ROWS + i, 0:FRAMES] = beside(sides, i)
        field[b * ROWS + 4, 0:FRAMES] = joined(tiles[2], tiles[3])
        halo[b * ROWS + 4, 0:FRAMES] = beside(tiles[3] + edge[b, 1].astype(F32), 4)
        return 0

    def unpack_2(b, _):
        tiles = [recv_2[b, i].astype(F32) for i in range(SECOND)]
        sides = turned(tiles[2], EARLY, 0) + edge[b, 0].astype(F32)
        for i in range(ROWS - 1):
            field[b * ROWS + i, EARLY:FRAMES] = turned(tiles[i // 2], EARLY * (1 - i % 2), 0)[EARLY:]
            halo[b * ROWS + i, EARLY:FRAMES] = beside(sides, i)[EARLY:]
        halo[b * ROWS + 4, EARLY:FRAMES] = beside(tiles[2] + edge[b, 1].astype(F32), 4)[EARLY:]
        return 0

    lax.fori_loop(0, n_tile, unpack, 0, unroll=4)

    def pack_lead(k, _):
        both = [
            jnp.where(row < 2, field[2 * k + i, 0:FRAMES], turned(halo[2 * k + i, 0:FRAMES], 2, 0)) for i in range(2)
        ]
        lead[k] = joined(both[0], both[1], False, True).astype(BF16)
        return 0

    def unpack_ahead(k, _):
        tiles = ahead[k].astype(F32)
        for i in range(2):
            field[2 * k + i, FRAMES:] = turned(tiles, -4 * i, 0)
            halo[2 * k + i, FRAMES:] = turned(tiles, -4 * i - 2, 0)
        return 0

    lead_copy = pltpu.make_async_remote_copy(
        src_ref=lead, dst_ref=ahead, send_sem=lead_send, recv_sem=lead_recv,
        device_id=(jnp.maximum(tm - 1, 0), tile), device_id_type=MESH,
    )

    @pl.when(to_left)
    def _():
        lax.fori_loop(0, height // 2, pack_lead, 0, unroll=8)
        lead_copy.start()

    lane3, col3 = lane_of((1, width, LANES), 2), lane_of((1, width, LANES), 1)
    outside = jnp.logical_or(
        jnp.logical_and(col3 == 0, lane3 < OUT),
        jnp.logical_and(col3 == width - 1, lane3 >= LANES - OUT),
    )
    edge_rows = jnp.zeros((width, LANES), F32)
    group = 16
    for t in range(WINDOW):
        vee[t, 0:width, :] = edge_rows
        vee[t, (height + 1) * width : (height + 2) * width, :] = edge_rows

    lane2 = lane_of((1, LANES), 1)

    def tap(t, g, shift_rows, shift):
        at = pl.ds(pl.multiple_of((g * group + shift_rows) * width, width), group * width)
        return turned(vee[t % WINDOW, at, :].astype(BF16), shift, 1)

    acc[...] = jnp.zeros(acc.shape, F32)

    def add_frame(t):
        left = jnp.concatenate([cols_t[t * LANES : (t + 3) * LANES, :], last_t[t]], axis=0)
        acc[...] += jnp.dot(left, act[t], preferred_element_type=F32)

    for t in range(wide):
        if t == EARLY:
            pltpu.make_async_copy(recv_2, recv_2, recv_main_2).wait()
            lax.fori_loop(0, n_tile, unpack_2, 0, unroll=4)
        if t == FRAMES:
            @pl.when(to_right)
            def _():
                pltpu.make_async_copy(ahead, ahead, lead_recv).wait()

            @pl.when(jnp.logical_not(to_right))
            def _():
                ahead[...] = jnp.zeros(ahead.shape, BF16)

            lax.fori_loop(0, height // 2, unpack_ahead, 0, unroll=8)

        def spread(g, _, t=t):
            rows = pl.ds(g * group, group)
            main = jnp.broadcast_to(field[rows, t : t + 1, :], (group, width, LANES))
            side = jnp.broadcast_to(halo[rows, t : t + 1, :], (group, width, LANES))
            at = pl.ds(pl.multiple_of((g * group + 1) * width, width), group * width)
            values = jnp.where(outside, side, main).reshape(group * width, LANES)
            vee[t % WINDOW, at, :] = pltpu.roll(values, 0, 1, stride=OUT, stride_axis=0)
            return 0

        def fill(g, _, t=t):
            rows = aligned(g, group * width)
            s0, s1, s2 = tap(t, g, 2, 2 * OUT), tap(t, g, 1, 5 * OUT), tap(t, g, 0, 0)
            cols[t, rows, :] = jnp.where(lane2 < 3 * OUT, s0, jnp.where(lane2 < 6 * OUT, s1, s2))
            return 0

        def fill_last(g, _, t=t):
            rows = aligned(g, group * width)
            taps = [tap(t - 2 + kt, g, 0, kt * OUT) for kt in range(3)]
            value = jnp.where(lane2 < 3 * OUT, taps[2], jnp.zeros_like(taps[2]))
            last[t - 2, rows, :] = jnp.where(lane2 < OUT, taps[0], jnp.where(lane2 < 2 * OUT, taps[1], value))
            return 0

        lax.fori_loop(0, height // group, spread, 0, unroll=True)
        lax.fori_loop(0, height // group, fill, 0, unroll=True)
        cols_t[t * LANES : (t + 1) * LANES, :] = jnp.transpose(cols[t])
        if t >= 2:
            lax.fori_loop(0, height // group, fill_last, 0, unroll=True)
            last_t[t - 2] = jnp.transpose(last[t - 2])[0 : 3 * OUT]
        if t >= 3:
            add_frame(t - 3)
    add_frame(frames - 1)

    pieces_of_total = []
    for kt in range(3):
        pieces_of_total.append(acc[kt * LANES : (kt + 1) * LANES, :])
        pieces_of_total.append(acc[3 * LANES + kt * OUT : 3 * LANES + (kt + 1) * OUT, :])
    pieces_of_total.append(jnp.zeros((part.shape[1] - 27 * OUT, cin), F32))
    part[...] = jnp.transpose(jnp.concatenate(pieces_of_total, axis=0))

    chunk = 40

    def grad_frame(t, _):
        def grad_rows(r, _):
            rows = aligned(r, chunk * width)
            left = jnp.concatenate([cols[t + kt, rows, :] for kt in range(3)] + [last[t, rows, :]], axis=1)
            grad = jnp.dot(left, weights[...], preferred_element_type=F32) * slope[t, rows, :]
            out_ref[t, pl.ds(r * chunk, chunk)] = grad.reshape(chunk, width, cin).astype(BF16)
            return 0

        lax.fori_loop(0, height // chunk, grad_rows, 0, unroll=True)
        return 0

    def drain(source, sem):
        pltpu.make_async_copy(source, source, sem).wait()

    def drain_messages(source, sem):
        if n_tm > 1:
            drain(source.at[pl.ds(0, n_tm - 1)], sem)
        if strips > 1:
            drain(source.at[0, pl.ds(0, strips - 1)], sem)

        @pl.when(block != tm)
        def _():
            drain(source.at[0, 0], sem)

    drain_messages(msg, send_main)
    drain_messages(msg_2, send_2)

    def drain_edge(k, _):
        drain(emsg.at[0, 0], send_edge)
        return 0

    lax.fori_loop(0, edges_out - self_edge, drain_edge, 0)

    @pl.when(to_left)
    def _():
        drain(lead, lead_send)

    rows = mine.shape[0]
    share = rows // groups
    swap = pltpu.make_async_remote_copy(
        src_ref=part.at[aligned(1 - core, rows)], dst_ref=mine,
        send_sem=swap_send, recv_sem=swap_recv,
        device_id=(partner, tile), device_id_type=MESH,
    )
    swap.start()
    lax.fori_loop(0, SPLIT[0], grad_frame, 0)
    swap.wait()
    mine[...] += part[aligned(core, rows), :]

    mine_half[...] = mine[...].astype(BF16)

    for k in range(1, groups):
        g = wrapped(spot + k, groups)
        pltpu.make_async_remote_copy(
            src_ref=mine_half.at[aligned(g, share)], dst_ref=pieces.at[spot],
            send_sem=piece_send, recv_sem=piece_recv,
            device_id=(tm, y_hi * groups + g), device_id_type=MESH,
        ).start()
    pieces[spot] = mine_half[aligned(spot, share), :]
    lax.fori_loop(SPLIT[0], SPLIT[1], grad_frame, 0)
    others = pieces.at[pl.ds(0, groups - 1)]
    pltpu.make_async_copy(others, others, piece_recv).wait()
    sums[...] = jnp.sum(pieces[...].astype(F32), axis=0)

    for k in range(n_tm):
        send(sums, quads.at[level], row_send, row_recv, k, owner_tile)
    lax.fori_loop(SPLIT[1], frames, grad_frame, 0)
    pltpu.make_async_copy(quads, quads, row_recv).wait()

    drain(others, piece_send)
    drain(quads.at[pl.ds(0, n_tm - 1)], row_send)

    @pl.when(core != y_hi)
    def _():
        drain(sums, row_send)

    result = quads[0]
    for k in range(1, n_tm):
        result = result + quads[k]
    kgrad_ref[...] = (result * scale)[:, : kgrad_ref.shape[1]]


SPLIT = (1, 6)


def on_device(n_tm, n_tile, scale, latent_grad, section_input, kernel):
    frames, height, width, cin = section_input.shape
    taps = kernel.shape[1]
    strips = n_tile // n_tm
    banded = jnp.transpose(latent_grad, (1, 0, 2)).reshape(ROWS, n_tm, FRAMES, strips * LANES)
    wide, count = frames + 2, height * width
    rows, share, padded = cin // CORES, cin // n_tile, 4 * LANES
    vmem = pl.BlockSpec(memory_space=pltpu.VMEM)
    return pl.pallas_call(
        functools.partial(whole, n_tm, n_tile, scale),
        out_shape=(
            pltpu.VMEM((frames, height, width, cin), BF16),
            pltpu.VMEM((share, taps), F32),
        ),
        in_specs=[pl.BlockSpec(memory_space=pl.ANY)] * 3,
        out_specs=(vmem, vmem),
        scratch_shapes=[
            pltpu.VMEM((ROWS, n_tm, FRAMES, strips * LANES), BF16),
            pltpu.VMEM((taps, cin), BF16),
            pltpu.VMEM((n_tm, strips, FIRST, FRAMES, LANES), BF16),
            pltpu.VMEM((n_tm, strips, SECOND, FRAMES, LANES), BF16),
            pltpu.VMEM((2, n_tm, 2, FRAMES, LANES), BF16),
            pltpu.VMEM((n_tile, FIRST, FRAMES, LANES), BF16),
            pltpu.VMEM((n_tile, SECOND, FRAMES, LANES), BF16),
            pltpu.VMEM((n_tile, 2, FRAMES, LANES), BF16),
            pltpu.VMEM((height // 2, FRAMES, LANES), BF16),
            pltpu.VMEM((height // 2, FRAMES, LANES), BF16),
            pltpu.VMEM((frames, count, cin), BF16),
            pltpu.VMEM((frames, count, cin), F32),
            pltpu.VMEM((height, 2 * FRAMES, LANES), F32),
            pltpu.VMEM((height, 2 * FRAMES, LANES), F32),
            pltpu.VMEM((WINDOW, (height + 2) * width, LANES), F32),
            pltpu.VMEM((wide, count, LANES), BF16),
            pltpu.VMEM((wide * LANES, count), BF16),
            pltpu.VMEM((frames, count, LANES), BF16),
            pltpu.VMEM((frames, 3 * OUT, count), BF16),
            pltpu.VMEM((padded, cin), BF16),
            pltpu.VMEM((27 * OUT, cin), F32),
            pltpu.VMEM((cin, padded), F32),
            pltpu.VMEM((rows, padded), F32),
            pltpu.VMEM((rows, padded), BF16),
            pltpu.VMEM((n_tile // CORES, share, padded), BF16),
            pltpu.VMEM((share, padded), F32),
            pltpu.VMEM((n_tm, share, padded), F32),
            pltpu.SemaphoreType.DMA((frames,)),
            pltpu.SemaphoreType.DMA((16,)),
        ],
        compiler_params=pltpu.CompilerParams(
            collective_id=0, has_side_effects=True, vmem_limit_bytes=VMEM_LIMIT
        ),
    )(banded, section_input, jnp.transpose(kernel))


VMEM_LIMIT = 53 << 20


def solution(mesh):
    n_tm, n_tile = mesh.shape["tm"], mesh.shape["tile"]
    positions = n_tm * FRAMES * n_tile * ROWS * n_tile * STRIP
    return jax.shard_map(
        functools.partial(on_device, n_tm, n_tile, 1.0 / math.sqrt(positions)),
        mesh=mesh,
        in_specs=(P(None, "tile", "tm"), P("tm", None, "tile", None), P()),
        out_specs=(P("tm", None, "tile", None), P("tile", None)),
        check_vma=False,
    )
```

```python
import functools
import math

import jax
import jax.numpy as jnp
from jax import lax
from jax.experimental import pallas as pl
from jax.experimental.pallas import tpu as pltpu
from jax.sharding import PartitionSpec as P

MESH = pl.DeviceIdType.MESH
F32, BF16 = jnp.float32, jnp.bfloat16
LANES = 128
OUT = 16
STRIP = 8
FRAMES = 8
ROWS = 5
FIRST = 4
SECOND = 3
EARLY = 4
CORES = 2
WINDOW = 3


def lane_of(shape, axis):
    return lax.broadcasted_iota(jnp.int32, shape, axis)


def aligned(index, size):
    return pl.ds(pl.multiple_of(index * size, size), size)


def turned(value, shift, axis):
    shift %= value.shape[axis]
    return pltpu.roll(value, shift, axis) if shift else value


def wrapped(index, size):
    return jnp.where(index >= size, index - size, index)


def strip_halo(left, right):
    lane = lane_of((1, LANES), 1)
    rows = []
    for i in range(ROWS):
        value = jnp.zeros((FRAMES, LANES), F32)
        if right is not None:
            value = jnp.where(lane >= LANES - OUT, right[i], value)
        if left is not None:
            value = jnp.where(lane < OUT, left[i], value)
        rows.append(turned(value, OUT + 2 * OUT * i, 1))
    return rows[0] + rows[1] + rows[2] + rows[3], rows[4]


def joined(upper, lower, turn_upper=False, turn_lower=False):
    upper = turned(upper, EARLY, 0) if turn_upper else upper
    lower = turned(lower, EARLY, 0) if turn_lower else lower
    return jnp.where(lane_of((FRAMES, 1), 0) < EARLY, upper, lower)


def whole(
    n_tm, n_tile, scale, grad_hbm, x_ref, kernel_hbm, out_ref, kgrad_ref,
    grad_ref, kernel_ref, msg, msg_2, emsg, recv, recv_2, edge, lead, ahead, act, slope, field, halo, vee, cols, cols_t, last, last_t,
    weights, acc, half, mine_half, pieces, sums, quads, in_sem, sems,
):
    frames, height, width, cin = out_ref.shape
    wide, count = frames + 2, height * width
    tm, tile = lax.axis_index("tm"), lax.axis_index("tile")
    strips = n_tile // n_tm
    block = tile // strips
    place_in_block = lax.rem(tile, strips)
    from_left = jnp.logical_and(place_in_block == 0, block > 0)
    from_right = jnp.logical_and(place_in_block == strips - 1, block < n_tm - 1)
    has_edge = jnp.logical_or(from_left, from_right)
    edge_block = jnp.where(place_in_block == 0, block - 1, block + 1)
    messages = n_tm * strips
    send_main, send_edge, recv_main, recv_edge = (sems.at[i] for i in range(4))
    swap_send, swap_recv, piece_send, piece_recv = (sems.at[i] for i in range(4, 8))
    send_2, recv_main_2 = sems.at[10], sems.at[11]
    row_send, row_recv = sems.at[12], sems.at[13]
    lead_send, lead_recv = sems.at[14], sems.at[15]
    core, y_lo = lax.rem(tm, CORES), tm // CORES
    groups = n_tile // CORES
    y_hi, spot = tile // groups, lax.rem(tile, groups)
    partner = tm + 1 - 2 * core
    level = y_hi * CORES + y_lo
    owner_tile = core * groups + spot

    def is_me(target_tm, target_tile):
        return jnp.logical_and(target_tm == tm, target_tile == tile)

    grad_copy = pltpu.make_async_copy(grad_hbm, grad_ref, sems.at[8])
    kernel_copy = pltpu.make_async_copy(kernel_hbm, kernel_ref, sems.at[9])
    grad_copy.start()
    kernel_copy.start()

    def fetch(t):
        return pltpu.make_async_copy(x_ref.at[t], out_ref.at[t], in_sem.at[t])

    for t in range(frames):
        fetch(t).start()

    barrier = pltpu.get_barrier_semaphore()

    def hail(target_tm, target_tile):
        pl.semaphore_signal(barrier, inc=1, device_id=(target_tm, target_tile), device_id_type=MESH)

    for k in range(1, n_tile):
        hail(block, wrapped(tile + k, n_tile))

    @pl.when(block != tm)
    def _():
        hail(block, tile)

    @pl.when(has_edge)
    def _():
        for k in range(1, n_tile):
            hail(edge_block, wrapped(tile + k, n_tile))

        @pl.when(edge_block != tm)
        def _():
            hail(edge_block, tile)

    @pl.when(tm < n_tm - 1)
    def _():
        hail(tm + 1, tile)

    hail(partner, tile)
    for k in range(1, groups):
        hail(tm, y_hi * groups + wrapped(spot + k, groups))
    for k in range(n_tm):
        source = (k % CORES) * CORES + y_hi, (k // CORES) * groups + spot

        @pl.when(jnp.logical_not(is_me(*source)))
        def _():
            hail(*source)

    r, c = lane_of((LANES, LANES), 0), lane_of((LANES, LANES), 1)
    same = jnp.logical_and(r // OUT + c // OUT == STRIP - 1, lax.rem(r, OUT) == lax.rem(c, OUT))
    flip = jnp.where(same, 1.0, 0.0).astype(BF16)
    row = lane_of((FRAMES, 1), 0)
    nothing = jnp.zeros((FRAMES, LANES), F32)
    grad_copy.wait()
    rows = [grad_ref[:, t].astype(F32).reshape(ROWS * FRAMES, strips * LANES) for t in range(n_tm)]
    rows = jnp.concatenate(
        [rows[t][:, s * LANES : (s + 1) * LANES] for t in range(n_tm) for s in range(strips)], axis=0
    )
    rows = jnp.dot(rows.astype(BF16), flip, preferred_element_type=F32).reshape(n_tm, strips, ROWS, FRAMES, LANES)
    flipped, halos = [], []
    for t in range(n_tm):
        here = [rows[t, s] for s in range(strips)]
        flipped.append(here)
        padded = [None, None] + here + [None, None]
        halos.append([strip_halo(padded[s], padded[s + 2]) for s in range(strips + 2)])
    self_main = (block == tm).astype(jnp.int32)
    to_right, to_left = tm < n_tm - 1, tm > 0
    right_tile, left_tile = (tm + 1) * strips, tm * strips - 1
    self_edge = (
        jnp.logical_and(to_right, tile == right_tile).astype(jnp.int32)
        + jnp.logical_and(to_left, tile == left_tile).astype(jnp.int32)
    )
    edges_out = n_tm * (to_right.astype(jnp.int32) + to_left.astype(jnp.int32))
    self_owner = (core == y_hi).astype(jnp.int32)
    exchange_out = messages - self_main + edges_out - self_edge
    all_here = (exchange_out + 1 + groups - 1 + n_tm - self_owner + to_left.astype(jnp.int32))

    def send(source, target, send_sem, recv_sem, target_tm, target_tile):
        own = is_me(target_tm, target_tile)

        @pl.when(jnp.logical_not(own))
        def _():
            pltpu.make_async_remote_copy(
                src_ref=source, dst_ref=target, send_sem=send_sem, recv_sem=recv_sem,
                device_id=(target_tm, target_tile), device_id_type=MESH,
            ).start()

        @pl.when(own)
        def _():
            pltpu.make_async_copy(source, target, recv_sem).start()

    def send_block(source, target, send_sem, recv_sem, t):
        for k in range(strips):
            s = wrapped(place_in_block + k, strips)
            if k == 0:
                send(source.at[t, s], target.at[tile], send_sem, recv_sem, t, tm * strips + s)
            else:
                pltpu.make_async_remote_copy(
                    src_ref=source.at[t, s], dst_ref=target.at[tile], send_sem=send_sem, recv_sem=recv_sem,
                    device_id=(t, tm * strips + s), device_id_type=MESH,
                ).start()

    def make_block(t):
        for s in range(strips):
            here, (first, second) = flipped[t][s], halos[t][s + 1]
            tiles = [
                joined(here[0], here[1], False, True), joined(here[2], here[3], False, True),
                joined(here[4], first, False, True), joined(second, here[4]),
            ]
            for i, value in enumerate(tiles):
                msg[t, s, i] = value.astype(BF16)
        for side, s in ((0, strips + 1), (1, 0)):
            for i, value in enumerate(halos[t][s]):
                emsg[side, t, i] = value.astype(BF16)

    def leave_block(t):
        send_block(msg, recv, send_main, recv_main, t)

        @pl.when(to_right)
        def _():
            send(emsg.at[0, t], edge.at[tile], send_edge, recv_edge, t, right_tile)

        @pl.when(to_left)
        def _():
            send(emsg.at[1, t], edge.at[tile], send_edge, recv_edge, t, left_tile)

    ready = n_tm // 2
    for t in range(ready):
        make_block(t)
    pl.semaphore_wait(barrier, all_here)
    for t in range(n_tm):
        leave_block(t)
        if ready + t < n_tm:
            make_block(ready + t)

    for t in range(n_tm):
        for s in range(strips):
            here, (first, second) = flipped[t][s], halos[t][s + 1]
            tiles = [
                joined(here[0], here[1], True), joined(here[2], here[3], True), joined(first, second, True),
            ]
            for i, value in enumerate(tiles):
                msg_2[t, s, i] = value.astype(BF16)

    kernel_copy.wait()
    weights[...] = jnp.zeros(weights.shape, BF16)
    for kt in range(3):
        taps = kernel_ref[9 * kt * OUT : 9 * (kt + 1) * OUT, :]
        taps = (0.5 * taps.astype(F32)).astype(BF16)
        weights[kt * LANES : (kt + 1) * LANES, :] = taps[:LANES]
        weights[3 * LANES + kt * OUT : 3 * LANES + (kt + 1) * OUT, :] = taps[LANES:]

    step = 8

    def silu_frame(t, _):
        fetch(t).wait()

        def silu_rows(r, _):
            half_x = 0.5 * out_ref[t, pl.ds(r * step, step)].astype(F32).reshape(step * width, cin)
            u = jnp.tanh(half_x)
            more = 1.0 + u
            value = half_x * more
            rows = aligned(r, step * width)
            act[t, rows, :] = value.astype(BF16)
            slope[t, rows, :] = more + value * (1.0 - u)
            return 0

        lax.fori_loop(0, height // step, silu_rows, 0, unroll=4)
        return 0

    lax.fori_loop(0, EARLY, silu_frame, 0)
    for t in range(n_tm):
        send_block(msg_2, recv_2, send_2, recv_main_2, t)
    lax.fori_loop(EARLY, frames, silu_frame, 0)

    @pl.when(jnp.logical_not(has_edge))
    def _():
        edge[...] = jnp.zeros(edge.shape, BF16)

    @pl.when(has_edge)
    def _():
        pltpu.make_async_copy(edge, edge, recv_edge).wait()

    pltpu.make_async_copy(recv, recv, recv_main).wait()

    def beside(value, i):
        return turned(value, -OUT - 2 * OUT * i, 1)

    def unpack(b, _):
        tiles = [recv[b, i].astype(F32) for i in range(FIRST)]
        sides = turned(tiles[2], EARLY, 0) + edge[b, 0].astype(F32)
        for i in range(ROWS - 1):
            field[b * ROWS + i, 0:FRAMES] = turned(tiles[i // 2], EARLY * (i % 2), 0)
            halo[b * ROWS + i, 0:FRAMES] = beside(sides, i)
        field[b * ROWS + 4, 0:FRAMES] = joined(tiles[2], tiles[3])
        halo[b * ROWS + 4, 0:FRAMES] = beside(tiles[3] + edge[b, 1].astype(F32), 4)
        return 0

    def unpack_2(b, _):
        tiles = [recv_2[b, i].astype(F32) for i in range(SECOND)]
        sides = turned(tiles[2], EARLY, 0) + edge[b, 0].astype(F32)
        for i in range(ROWS - 1):
            field[b * ROWS + i, EARLY:FRAMES] = turned(tiles[i // 2], EARLY * (1 - i % 2), 0)[EARLY:]
            halo[b * ROWS + i, EARLY:FRAMES] = beside(sides, i)[EARLY:]
        halo[b * ROWS + 4, EARLY:FRAMES] = beside(tiles[2] + edge[b, 1].astype(F32), 4)[EARLY:]
        return 0

    lax.fori_loop(0, n_tile, unpack, 0, unroll=4)

    def pack_lead(k, _):
        both = [
            jnp.where(row < 2, field[2 * k + i, 0:FRAMES], turned(halo[2 * k + i, 0:FRAMES], 2, 0)) for i in range(2)
        ]
        lead[k] = joined(both[0], both[1], False, True).astype(BF16)
        return 0

    def unpack_ahead(k, _):
        tiles = ahead[k].astype(F32)
        for i in range(2):
            field[2 * k + i, FRAMES:] = turned(tiles, -4 * i, 0)
            halo[2 * k + i, FRAMES:] = turned(tiles, -4 * i - 2, 0)
        return 0

    lead_copy = pltpu.make_async_remote_copy(
        src_ref=lead, dst_ref=ahead, send_sem=lead_send, recv_sem=lead_recv,
        device_id=(jnp.maximum(tm - 1, 0), tile), device_id_type=MESH,
    )

    @pl.when(to_left)
    def _():
        lax.fori_loop(0, height // 2, pack_lead, 0, unroll=8)
        lead_copy.start()

    lane3, col3 = lane_of((1, width, LANES), 2), lane_of((1, width, LANES), 1)
    outside = jnp.logical_or(
        jnp.logical_and(col3 == 0, lane3 < OUT),
        jnp.logical_and(col3 == width - 1, lane3 >= LANES - OUT),
    )
    edge_rows = jnp.zeros((width, LANES), F32)
    group = 16
    for t in range(WINDOW):
        vee[t, 0:width, :] = edge_rows
        vee[t, (height + 1) * width : (height + 2) * width, :] = edge_rows

    lane2 = lane_of((1, LANES), 1)

    def tap(t, g, shift_rows, shift):
        at = pl.ds(pl.multiple_of((g * group + shift_rows) * width, width), group * width)
        return turned(vee[t % WINDOW, at, :].astype(BF16), shift, 1)

    acc[...] = jnp.zeros(acc.shape, F32)

    def add_frames(t):
        left = jnp.concatenate([
            jnp.concatenate([cols_t[i * LANES : (i + 3) * LANES, :], last_t[i]], axis=0) for i in (t, t + 1)
        ], axis=1)
        acc[...] += jnp.dot(left, act[t : t + 2].reshape(2 * count, cin), preferred_element_type=F32)

    for t in range(wide):
        if t >= 4 and t % 2 == 0:
            add_frames(t - 4)
        if t == EARLY:
            pltpu.make_async_copy(recv_2, recv_2, recv_main_2).wait()
            lax.fori_loop(0, n_tile, unpack_2, 0, unroll=4)
        if t == FRAMES:
            @pl.when(to_right)
            def _():
                pltpu.make_async_copy(ahead, ahead, lead_recv).wait()

            @pl.when(jnp.logical_not(to_right))
            def _():
                ahead[...] = jnp.zeros(ahead.shape, BF16)

            lax.fori_loop(0, height // 2, unpack_ahead, 0, unroll=8)

        def spread(g, _, t=t):
            rows = pl.ds(g * group, group)
            main = jnp.broadcast_to(field[rows, t : t + 1, :], (group, width, LANES))
            side = jnp.broadcast_to(halo[rows, t : t + 1, :], (group, width, LANES))
            at = pl.ds(pl.multiple_of((g * group + 1) * width, width), group * width)
            values = jnp.where(outside, side, main).reshape(group * width, LANES)
            vee[t % WINDOW, at, :] = pltpu.roll(values, 0, 1, stride=OUT, stride_axis=0)
            return 0

        def fill(g, _, t=t):
            rows = aligned(g, group * width)
            s0, s1, s2 = tap(t, g, 2, 2 * OUT), tap(t, g, 1, 5 * OUT), tap(t, g, 0, 0)
            cols[t, rows, :] = jnp.where(lane2 < 3 * OUT, s0, jnp.where(lane2 < 6 * OUT, s1, s2))
            return 0

        def fill_last(g, _, t=t):
            rows = aligned(g, group * width)
            taps = [tap(t - 2 + kt, g, 0, kt * OUT) for kt in range(3)]
            value = jnp.where(lane2 < 3 * OUT, taps[2], jnp.zeros_like(taps[2]))
            last[t - 2, rows, :] = jnp.where(lane2 < OUT, taps[0], jnp.where(lane2 < 2 * OUT, taps[1], value))
            return 0

        lax.fori_loop(0, height // group, spread, 0, unroll=True)
        lax.fori_loop(0, height // group, fill, 0, unroll=True)
        cols_t[t * LANES : (t + 1) * LANES, :] = jnp.transpose(cols[t])
        if t >= 2:
            lax.fori_loop(0, height // group, fill_last, 0, unroll=True)
            last_t[t - 2] = jnp.transpose(last[t - 2])[0 : 3 * OUT]
    add_frames(frames - 2)

    rows = half.shape[1]
    share = rows // groups
    swap = pltpu.make_async_remote_copy(
        src_ref=acc.at[:, aligned(1 - core, rows)], dst_ref=half,
        send_sem=swap_send, recv_sem=swap_recv,
        device_id=(partner, tile), device_id_type=MESH,
    )
    swap.start()

    chunk = 40

    def grad_frame(t, _):
        def grad_rows(r, _):
            rows = aligned(r, chunk * width)
            left = jnp.concatenate([cols[t + kt, rows, :] for kt in range(3)] + [last[t, rows, :]], axis=1)
            grad = jnp.dot(left, weights[...], preferred_element_type=F32) * slope[t, rows, :]
            out_ref[t, pl.ds(r * chunk, chunk)] = grad.reshape(chunk, width, cin).astype(BF16)
            return 0

        lax.fori_loop(0, height // chunk, grad_rows, 0, unroll=True)
        return 0

    def grad_frames(first, end):
        lax.fori_loop(first, end, grad_frame, 0)

    def drain(source, sem):
        pltpu.make_async_copy(source, source, sem).wait()

    def drain_messages(source, sem):
        if n_tm > 1:
            drain(source.at[pl.ds(0, n_tm - 1)], sem)
        if strips > 1:
            drain(source.at[0, pl.ds(0, strips - 1)], sem)

        @pl.when(block != tm)
        def _():
            drain(source.at[0, 0], sem)

    drain_messages(msg, send_main)
    drain_messages(msg_2, send_2)

    def drain_edge(k, _):
        drain(emsg.at[0, 0], send_edge)
        return 0

    lax.fori_loop(0, edges_out - self_edge, drain_edge, 0)

    @pl.when(to_left)
    def _():
        drain(lead, lead_send)

    grad_frames(0, SPLIT[0])
    swap.wait()
    own = acc[:, aligned(core, rows)] + half[...]
    ordered = []
    for kt in range(3):
        ordered.append(own[kt * LANES : (kt + 1) * LANES])
        ordered.append(own[3 * LANES + kt * OUT : 3 * LANES + (kt + 1) * OUT])
    ordered.append(jnp.zeros((mine_half.shape[1] - 27 * OUT, rows), F32))
    mine_half[...] = jnp.transpose(jnp.concatenate(ordered, axis=0)).astype(BF16)

    for k in range(1, groups):
        g = wrapped(spot + k, groups)
        pltpu.make_async_remote_copy(
            src_ref=mine_half.at[aligned(g, share)], dst_ref=pieces.at[spot],
            send_sem=piece_send, recv_sem=piece_recv,
            device_id=(tm, y_hi * groups + g), device_id_type=MESH,
        ).start()
    pieces[spot] = mine_half[aligned(spot, share), :]
    grad_frames(SPLIT[0], SPLIT[1])
    others = pieces.at[pl.ds(0, groups - 1)]
    pltpu.make_async_copy(others, others, piece_recv).wait()
    sums[...] = jnp.sum(pieces[...].astype(F32), axis=0)

    for k in range(n_tm):
        send(sums, quads.at[level], row_send, row_recv, k, owner_tile)
    grad_frames(SPLIT[1], frames)
    pltpu.make_async_copy(quads, quads, row_recv).wait()

    drain(others, piece_send)
    drain(quads.at[pl.ds(0, n_tm - 1)], row_send)

    @pl.when(core != y_hi)
    def _():
        drain(sums, row_send)

    result = quads[0]
    for k in range(1, n_tm):
        result = result + quads[k]
    kgrad_ref[...] = (result * scale)[:, : kgrad_ref.shape[1]]


SPLIT = (1, 6)


def on_device(n_tm, n_tile, scale, latent_grad, section_input, kernel):
    frames, height, width, cin = section_input.shape
    taps = kernel.shape[1]
    strips = n_tile // n_tm
    banded = jnp.transpose(latent_grad, (1, 0, 2)).reshape(ROWS, n_tm, FRAMES, strips * LANES)
    wide, count = frames + 2, height * width
    rows, share, padded = cin // CORES, cin // n_tile, 4 * LANES
    vmem = pl.BlockSpec(memory_space=pltpu.VMEM)
    return pl.pallas_call(
        functools.partial(whole, n_tm, n_tile, scale),
        out_shape=(
            pltpu.VMEM((frames, height, width, cin), BF16),
            pltpu.VMEM((share, taps), F32),
        ),
        in_specs=[pl.BlockSpec(memory_space=pl.ANY)] * 3,
        out_specs=(vmem, vmem),
        scratch_shapes=[
            pltpu.VMEM((ROWS, n_tm, FRAMES, strips * LANES), BF16),
            pltpu.VMEM((taps, cin), BF16),
            pltpu.VMEM((n_tm, strips, FIRST, FRAMES, LANES), BF16),
            pltpu.VMEM((n_tm, strips, SECOND, FRAMES, LANES), BF16),
            pltpu.VMEM((2, n_tm, 2, FRAMES, LANES), BF16),
            pltpu.VMEM((n_tile, FIRST, FRAMES, LANES), BF16),
            pltpu.VMEM((n_tile, SECOND, FRAMES, LANES), BF16),
            pltpu.VMEM((n_tile, 2, FRAMES, LANES), BF16),
            pltpu.VMEM((height // 2, FRAMES, LANES), BF16),
            pltpu.VMEM((height // 2, FRAMES, LANES), BF16),
            pltpu.VMEM((frames, count, cin), BF16),
            pltpu.VMEM((frames, count, cin), F32),
            pltpu.VMEM((height, 2 * FRAMES, LANES), F32),
            pltpu.VMEM((height, 2 * FRAMES, LANES), F32),
            pltpu.VMEM((WINDOW, (height + 2) * width, LANES), F32),
            pltpu.VMEM((wide, count, LANES), BF16),
            pltpu.VMEM((wide * LANES, count), BF16),
            pltpu.VMEM((frames, count, LANES), BF16),
            pltpu.VMEM((frames, 3 * OUT, count), BF16),
            pltpu.VMEM((padded, cin), BF16),
            pltpu.VMEM((27 * OUT, cin), F32),
            pltpu.VMEM((27 * OUT, rows), F32),
            pltpu.VMEM((rows, padded), BF16),
            pltpu.VMEM((n_tile // CORES, share, padded), BF16),
            pltpu.VMEM((share, padded), F32),
            pltpu.VMEM((n_tm, share, padded), F32),
            pltpu.SemaphoreType.DMA((frames,)),
            pltpu.SemaphoreType.DMA((16,)),
        ],
        compiler_params=pltpu.CompilerParams(
            collective_id=0, has_side_effects=True, vmem_limit_bytes=VMEM_LIMIT
        ),
    )(banded, section_input, jnp.transpose(kernel))


VMEM_LIMIT = 53 << 20


def solution(mesh):
    n_tm, n_tile = mesh.shape["tm"], mesh.shape["tile"]
    positions = n_tm * FRAMES * n_tile * ROWS * n_tile * STRIP
    return jax.shard_map(
        functools.partial(on_device, n_tm, n_tile, 1.0 / math.sqrt(positions)),
        mesh=mesh,
        in_specs=(P(None, "tile", "tm"), P("tm", None, "tile", None), P()),
        out_specs=(P("tm", None, "tile", None), P("tile", None)),
        check_vma=False,
    )
```

```python
import functools
import math

import jax
import jax.numpy as jnp
from jax import lax
from jax.experimental import pallas as pl
from jax.experimental.pallas import tpu as pltpu
from jax.sharding import PartitionSpec as P

MESH = pl.DeviceIdType.MESH
F32, BF16 = jnp.float32, jnp.bfloat16
LANES = 128
OUT = 16
STRIP = 8
FRAMES = 8
ROWS = 5
FIRST = 4
SECOND = 3
EARLY = 4
CORES = 2
WINDOW = 3


def lane_of(shape, axis):
    return lax.broadcasted_iota(jnp.int32, shape, axis)


def aligned(index, size):
    return pl.ds(pl.multiple_of(index * size, size), size)


def turned(value, shift, axis):
    shift %= value.shape[axis]
    return pltpu.roll(value, shift, axis) if shift else value


def wrapped(index, size):
    return jnp.where(index >= size, index - size, index)


def strip_halo(left, right):
    lane = lane_of((1, LANES), 1)
    rows = []
    for i in range(ROWS):
        value = jnp.zeros((FRAMES, LANES), F32)
        if right is not None:
            value = jnp.where(lane >= LANES - OUT, right[i], value)
        if left is not None:
            value = jnp.where(lane < OUT, left[i], value)
        rows.append(turned(value, OUT + 2 * OUT * i, 1))
    return rows[0] + rows[1] + rows[2] + rows[3], rows[4]


def joined(upper, lower, turn_upper=False, turn_lower=False):
    upper = turned(upper, EARLY, 0) if turn_upper else upper
    lower = turned(lower, EARLY, 0) if turn_lower else lower
    return jnp.where(lane_of((FRAMES, 1), 0) < EARLY, upper, lower)


def whole(
    n_tm, n_tile, scale, grad_hbm, x_ref, kernel_hbm, out_ref, kgrad_ref,
    grad_ref, kernel_ref, msg, msg_2, emsg, recv, recv_2, edge, lead, ahead, act, slope, field, halo, vee, cols, cols_t, last, last_t,
    weights, acc, part, mine, mine_half, pieces, sums, quads, in_sem, sems,
):
    frames, height, width, cin = out_ref.shape
    wide, count = frames + 2, height * width
    tm, tile = lax.axis_index("tm"), lax.axis_index("tile")
    strips = n_tile // n_tm
    block = tile // strips
    place_in_block = lax.rem(tile, strips)
    from_left = jnp.logical_and(place_in_block == 0, block > 0)
    from_right = jnp.logical_and(place_in_block == strips - 1, block < n_tm - 1)
    has_edge = jnp.logical_or(from_left, from_right)
    edge_block = jnp.where(place_in_block == 0, block - 1, block + 1)
    messages = n_tm * strips
    send_main, send_edge, recv_main, recv_edge = (sems.at[i] for i in range(4))
    swap_send, swap_recv, piece_send, piece_recv = (sems.at[i] for i in range(4, 8))
    send_2, recv_main_2 = sems.at[10], sems.at[11]
    row_send, row_recv = sems.at[12], sems.at[13]
    lead_send, lead_recv = sems.at[14], sems.at[15]
    core, y_lo = lax.rem(tm, CORES), tm // CORES
    groups = n_tile // CORES
    y_hi, spot = tile // groups, lax.rem(tile, groups)
    partner = tm + 1 - 2 * core
    level = y_hi * CORES + y_lo
    owner_tile = core * groups + spot

    def is_me(target_tm, target_tile):
        return jnp.logical_and(target_tm == tm, target_tile == tile)

    grad_copy = pltpu.make_async_copy(grad_hbm, grad_ref, sems.at[8])
    kernel_copy = pltpu.make_async_copy(kernel_hbm, kernel_ref, sems.at[9])
    grad_copy.start()
    kernel_copy.start()

    def fetch(t):
        return pltpu.make_async_copy(x_ref.at[t], out_ref.at[t], in_sem.at[t])

    for t in range(frames):
        fetch(t).start()

    barrier = pltpu.get_barrier_semaphore()

    def hail(target_tm, target_tile):
        pl.semaphore_signal(barrier, inc=1, device_id=(target_tm, target_tile), device_id_type=MESH)

    for k in range(1, n_tile):
        hail(block, wrapped(tile + k, n_tile))

    @pl.when(block != tm)
    def _():
        hail(block, tile)

    @pl.when(has_edge)
    def _():
        for k in range(1, n_tile):
            hail(edge_block, wrapped(tile + k, n_tile))

        @pl.when(edge_block != tm)
        def _():
            hail(edge_block, tile)

    @pl.when(tm < n_tm - 1)
    def _():
        hail(tm + 1, tile)

    hail(partner, tile)
    for k in range(1, groups):
        hail(tm, y_hi * groups + wrapped(spot + k, groups))
    for k in range(n_tm):
        source = (k % CORES) * CORES + y_hi, (k // CORES) * groups + spot

        @pl.when(jnp.logical_not(is_me(*source)))
        def _():
            hail(*source)

    r, c = lane_of((LANES, LANES), 0), lane_of((LANES, LANES), 1)
    same = jnp.logical_and(r // OUT + c // OUT == STRIP - 1, lax.rem(r, OUT) == lax.rem(c, OUT))
    flip = jnp.where(same, 1.0, 0.0).astype(BF16)
    row = lane_of((FRAMES, 1), 0)
    nothing = jnp.zeros((FRAMES, LANES), F32)
    grad_copy.wait()
    rows = [grad_ref[:, t].astype(F32).reshape(ROWS * FRAMES, strips * LANES) for t in range(n_tm)]
    rows = jnp.concatenate(
        [rows[t][:, s * LANES : (s + 1) * LANES] for t in range(n_tm) for s in range(strips)], axis=0
    )
    rows = jnp.dot(rows.astype(BF16), flip, preferred_element_type=F32).reshape(n_tm, strips, ROWS, FRAMES, LANES)
    flipped, halos = [], []
    for t in range(n_tm):
        here = [rows[t, s] for s in range(strips)]
        flipped.append(here)
        padded = [None, None] + here + [None, None]
        halos.append([strip_halo(padded[s], padded[s + 2]) for s in range(strips + 2)])
    self_main = (block == tm).astype(jnp.int32)
    to_right, to_left = tm < n_tm - 1, tm > 0
    right_tile, left_tile = (tm + 1) * strips, tm * strips - 1
    self_edge = (
        jnp.logical_and(to_right, tile == right_tile).astype(jnp.int32)
        + jnp.logical_and(to_left, tile == left_tile).astype(jnp.int32)
    )
    edges_out = n_tm * (to_right.astype(jnp.int32) + to_left.astype(jnp.int32))
    self_owner = (core == y_hi).astype(jnp.int32)
    exchange_out = messages - self_main + edges_out - self_edge
    all_here = (exchange_out + 1 + groups - 1 + n_tm - self_owner + to_left.astype(jnp.int32))

    def send(source, target, send_sem, recv_sem, target_tm, target_tile):
        own = is_me(target_tm, target_tile)

        @pl.when(jnp.logical_not(own))
        def _():
            pltpu.make_async_remote_copy(
                src_ref=source, dst_ref=target, send_sem=send_sem, recv_sem=recv_sem,
                device_id=(target_tm, target_tile), device_id_type=MESH,
            ).start()

        @pl.when(own)
        def _():
            pltpu.make_async_copy(source, target, recv_sem).start()

    def send_block(source, target, send_sem, recv_sem, t):
        for k in range(strips):
            s = wrapped(place_in_block + k, strips)
            if k == 0:
                send(source.at[t, s], target.at[tile], send_sem, recv_sem, t, tm * strips + s)
            else:
                pltpu.make_async_remote_copy(
                    src_ref=source.at[t, s], dst_ref=target.at[tile], send_sem=send_sem, recv_sem=recv_sem,
                    device_id=(t, tm * strips + s), device_id_type=MESH,
                ).start()

    def make_block(t):
        for s in range(strips):
            here, (first, second) = flipped[t][s], halos[t][s + 1]
            tiles = [
                joined(here[0], here[1], False, True), joined(here[2], here[3], False, True),
                joined(here[4], first, False, True), joined(second, here[4]),
            ]
            for i, value in enumerate(tiles):
                msg[t, s, i] = value.astype(BF16)
        for side, s in ((0, strips + 1), (1, 0)):
            for i, value in enumerate(halos[t][s]):
                emsg[side, t, i] = value.astype(BF16)

    def leave_block(t):
        send_block(msg, recv, send_main, recv_main, t)

        @pl.when(to_right)
        def _():
            send(emsg.at[0, t], edge.at[tile], send_edge, recv_edge, t, right_tile)

        @pl.when(to_left)
        def _():
            send(emsg.at[1, t], edge.at[tile], send_edge, recv_edge, t, left_tile)

    ready = n_tm // 2
    for t in range(ready):
        make_block(t)
    pl.semaphore_wait(barrier, all_here)
    for t in range(n_tm):
        leave_block(t)
        if ready + t < n_tm:
            make_block(ready + t)

    for t in range(n_tm):
        for s in range(strips):
            here, (first, second) = flipped[t][s], halos[t][s + 1]
            tiles = [
                joined(here[0], here[1], True), joined(here[2], here[3], True), joined(first, second, True),
            ]
            for i, value in enumerate(tiles):
                msg_2[t, s, i] = value.astype(BF16)

    kernel_copy.wait()
    weights[...] = jnp.zeros(weights.shape, BF16)
    for kt in range(3):
        taps = kernel_ref[9 * kt * OUT : 9 * (kt + 1) * OUT, :]
        taps = (0.5 * taps.astype(F32)).astype(BF16)
        weights[kt * LANES : (kt + 1) * LANES, :] = taps[:LANES]
        weights[3 * LANES + kt * OUT : 3 * LANES + (kt + 1) * OUT, :] = taps[LANES:]

    step = 8

    def silu_frame(t, _):
        fetch(t).wait()

        def silu_rows(r, _):
            half_x = 0.5 * out_ref[t, pl.ds(r * step, step)].astype(F32).reshape(step * width, cin)
            u = jnp.tanh(half_x)
            more = 1.0 + u
            value = half_x * more
            rows = aligned(r, step * width)
            act[t, rows, :] = value.astype(BF16)
            slope[t, rows, :] = more + value * (1.0 - u)
            return 0

        lax.fori_loop(0, height // step, silu_rows, 0, unroll=10)
        return 0

    lax.fori_loop(0, EARLY, silu_frame, 0)
    for t in range(n_tm):
        send_block(msg_2, recv_2, send_2, recv_main_2, t)
    lax.fori_loop(EARLY, frames, silu_frame, 0)

    @pl.when(jnp.logical_not(has_edge))
    def _():
        edge[...] = jnp.zeros(edge.shape, BF16)

    @pl.when(has_edge)
    def _():
        pltpu.make_async_copy(edge, edge, recv_edge).wait()

    pltpu.make_async_copy(recv, recv, recv_main).wait()

    def beside(value, i):
        return turned(value, -OUT - 2 * OUT * i, 1)

    def unpack(b, _):
        tiles = [recv[b, i].astype(F32) for i in range(FIRST)]
        sides = turned(tiles[2], EARLY, 0) + edge[b, 0].astype(F32)
        for i in range(ROWS - 1):
            field[b * ROWS + i, 0:FRAMES] = turned(tiles[i // 2], EARLY * (i % 2), 0)
            halo[b * ROWS + i, 0:FRAMES] = beside(sides, i)
        field[b * ROWS + 4, 0:FRAMES] = joined(tiles[2], tiles[3])
        halo[b * ROWS + 4, 0:FRAMES] = beside(tiles[3] + edge[b, 1].astype(F32), 4)
        return 0

    def unpack_2(b, _):
        tiles = [recv_2[b, i].astype(F32) for i in range(SECOND)]
        sides = turned(tiles[2], EARLY, 0) + edge[b, 0].astype(F32)
        for i in range(ROWS - 1):
            field[b * ROWS + i, EARLY:FRAMES] = turned(tiles[i // 2], EARLY * (1 - i % 2), 0)[EARLY:]
            halo[b * ROWS + i, EARLY:FRAMES] = beside(sides, i)[EARLY:]
        halo[b * ROWS + 4, EARLY:FRAMES] = beside(tiles[2] + edge[b, 1].astype(F32), 4)[EARLY:]
        return 0

    lax.fori_loop(0, n_tile, unpack, 0, unroll=8)

    def pack_lead(k, _):
        both = [
            jnp.where(row < 2, field[2 * k + i, 0:FRAMES], turned(halo[2 * k + i, 0:FRAMES], 2, 0)) for i in range(2)
        ]
        lead[k] = joined(both[0], both[1], False, True).astype(BF16)
        return 0

    def unpack_ahead(k, _):
        tiles = ahead[k].astype(F32)
        for i in range(2):
            field[2 * k + i, FRAMES:] = turned(tiles, -4 * i, 0)
            halo[2 * k + i, FRAMES:] = turned(tiles, -4 * i - 2, 0)
        return 0

    lead_copy = pltpu.make_async_remote_copy(
        src_ref=lead, dst_ref=ahead, send_sem=lead_send, recv_sem=lead_recv,
        device_id=(jnp.maximum(tm - 1, 0), tile), device_id_type=MESH,
    )

    @pl.when(to_left)
    def _():
        lax.fori_loop(0, height // 2, pack_lead, 0, unroll=8)
        lead_copy.start()

    lane3, col3 = lane_of((1, width, LANES), 2), lane_of((1, width, LANES), 1)
    outside = jnp.logical_or(
        jnp.logical_and(col3 == 0, lane3 < OUT),
        jnp.logical_and(col3 == width - 1, lane3 >= LANES - OUT),
    )
    edge_rows = jnp.zeros((width, LANES), F32)
    group = 16
    for t in range(WINDOW):
        vee[t, 0:width, :] = edge_rows
        vee[t, (height + 1) * width : (height + 2) * width, :] = edge_rows

    lane2 = lane_of((1, LANES), 1)

    def tap(t, g, shift_rows, shift):
        at = pl.ds(pl.multiple_of((g * group + shift_rows) * width, width), group * width)
        return turned(vee[t % WINDOW, at, :].astype(BF16), shift, 1)

    acc[...] = jnp.zeros(acc.shape, F32)

    def add_frame(t):
        left = jnp.concatenate([cols_t[t * LANES : (t + 3) * LANES, :], last_t[t]], axis=0)
        acc[...] += jnp.dot(left, act[t], preferred_element_type=F32)

    for t in range(wide):
        if t == EARLY:
            pltpu.make_async_copy(recv_2, recv_2, recv_main_2).wait()
            lax.fori_loop(0, n_tile, unpack_2, 0, unroll=8)
        if t == FRAMES:
            @pl.when(to_right)
            def _():
                pltpu.make_async_copy(ahead, ahead, lead_recv).wait()

            @pl.when(jnp.logical_not(to_right))
            def _():
                ahead[...] = jnp.zeros(ahead.shape, BF16)

            lax.fori_loop(0, height // 2, unpack_ahead, 0, unroll=8)

        def spread(g, _, t=t):
            rows = pl.ds(g * group, group)
            main = jnp.broadcast_to(field[rows, t : t + 1, :], (group, width, LANES))
            side = jnp.broadcast_to(halo[rows, t : t + 1, :], (group, width, LANES))
            at = pl.ds(pl.multiple_of((g * group + 1) * width, width), group * width)
            values = jnp.where(outside, side, main).reshape(group * width, LANES)
            vee[t % WINDOW, at, :] = pltpu.roll(values, 0, 1, stride=OUT, stride_axis=0)
            return 0

        def fill(g, _, t=t):
            rows = aligned(g, group * width)
            s0, s1, s2 = tap(t, g, 2, 2 * OUT), tap(t, g, 1, 5 * OUT), tap(t, g, 0, 0)
            cols[t, rows, :] = jnp.where(lane2 < 3 * OUT, s0, jnp.where(lane2 < 6 * OUT, s1, s2))
            return 0

        def fill_last(g, _, t=t):
            rows = aligned(g, group * width)
            taps = [tap(t - 2 + kt, g, 0, kt * OUT) for kt in range(3)]
            value = jnp.where(lane2 < 3 * OUT, taps[2], jnp.zeros_like(taps[2]))
            last[t - 2, rows, :] = jnp.where(lane2 < OUT, taps[0], jnp.where(lane2 < 2 * OUT, taps[1], value))
            return 0

        lax.fori_loop(0, height // group, spread, 0, unroll=True)
        lax.fori_loop(0, height // group, fill, 0, unroll=True)
        cols_t[t * LANES : (t + 1) * LANES, :] = jnp.transpose(cols[t])
        if t >= 2:
            lax.fori_loop(0, height // group, fill_last, 0, unroll=True)
            last_t[t - 2] = jnp.transpose(last[t - 2])[0 : 3 * OUT]
        if t >= 3:
            add_frame(t - 3)
    add_frame(frames - 1)

    pieces_of_total = []
    for kt in range(3):
        pieces_of_total.append(acc[kt * LANES : (kt + 1) * LANES, :])
        pieces_of_total.append(acc[3 * LANES + kt * OUT : 3 * LANES + (kt + 1) * OUT, :])
    pieces_of_total.append(jnp.zeros((part.shape[1] - 27 * OUT, cin), F32))
    part[...] = jnp.transpose(jnp.concatenate(pieces_of_total, axis=0))

    chunk = 40

    def grad_frame(t, _):
        def grad_rows(r, _):
            rows = aligned(r, chunk * width)
            left = jnp.concatenate([cols[t + kt, rows, :] for kt in range(3)] + [last[t, rows, :]], axis=1)
            grad = jnp.dot(left, weights[...], preferred_element_type=F32) * slope[t, rows, :]
            out_ref[t, pl.ds(r * chunk, chunk)] = grad.reshape(chunk, width, cin).astype(BF16)
            return 0

        lax.fori_loop(0, height // chunk, grad_rows, 0, unroll=True)
        return 0

    def drain(source, sem):
        pltpu.make_async_copy(source, source, sem).wait()

    def drain_messages(source, sem):
        if n_tm > 1:
            drain(source.at[pl.ds(0, n_tm - 1)], sem)
        if strips > 1:
            drain(source.at[0, pl.ds(0, strips - 1)], sem)

        @pl.when(block != tm)
        def _():
            drain(source.at[0, 0], sem)

    drain_messages(msg, send_main)
    drain_messages(msg_2, send_2)

    def drain_edge(k, _):
        drain(emsg.at[0, 0], send_edge)
        return 0

    lax.fori_loop(0, edges_out - self_edge, drain_edge, 0)

    @pl.when(to_left)
    def _():
        drain(lead, lead_send)

    rows = mine.shape[0]
    share = rows // groups
    swap = pltpu.make_async_remote_copy(
        src_ref=part.at[aligned(1 - core, rows)], dst_ref=mine,
        send_sem=swap_send, recv_sem=swap_recv,
        device_id=(partner, tile), device_id_type=MESH,
    )
    swap.start()
    lax.fori_loop(0, SPLIT[0], grad_frame, 0)
    swap.wait()
    mine[...] += part[aligned(core, rows), :]

    mine_half[...] = mine[...].astype(BF16)

    for k in range(1, groups):
        g = wrapped(spot + k, groups)
        pltpu.make_async_remote_copy(
            src_ref=mine_half.at[aligned(g, share)], dst_ref=pieces.at[spot],
            send_sem=piece_send, recv_sem=piece_recv,
            device_id=(tm, y_hi * groups + g), device_id_type=MESH,
        ).start()
    pieces[spot] = mine_half[aligned(spot, share), :]
    lax.fori_loop(SPLIT[0], SPLIT[1], grad_frame, 0)
    others = pieces.at[pl.ds(0, groups - 1)]
    pltpu.make_async_copy(others, others, piece_recv).wait()
    sums[...] = jnp.sum(pieces[...].astype(F32), axis=0)

    for k in range(n_tm):
        send(sums, quads.at[level], row_send, row_recv, k, owner_tile)
    lax.fori_loop(SPLIT[1], frames, grad_frame, 0)
    pltpu.make_async_copy(quads, quads, row_recv).wait()

    drain(others, piece_send)
    drain(quads.at[pl.ds(0, n_tm - 1)], row_send)

    @pl.when(core != y_hi)
    def _():
        drain(sums, row_send)

    result = quads[0]
    for k in range(1, n_tm):
        result = result + quads[k]
    kgrad_ref[...] = (result * scale)[:, : kgrad_ref.shape[1]]


SPLIT = (1, 6)


def on_device(n_tm, n_tile, scale, latent_grad, section_input, kernel):
    frames, height, width, cin = section_input.shape
    taps = kernel.shape[1]
    strips = n_tile // n_tm
    banded = jnp.transpose(latent_grad, (1, 0, 2)).reshape(ROWS, n_tm, FRAMES, strips * LANES)
    wide, count = frames + 2, height * width
    rows, share, padded = cin // CORES, cin // n_tile, 4 * LANES
    vmem = pl.BlockSpec(memory_space=pltpu.VMEM)
    return pl.pallas_call(
        functools.partial(whole, n_tm, n_tile, scale),
        out_shape=(
            pltpu.VMEM((frames, height, width, cin), BF16),
            pltpu.VMEM((share, taps), F32),
        ),
        in_specs=[pl.BlockSpec(memory_space=pl.ANY)] * 3,
        out_specs=(vmem, vmem),
        scratch_shapes=[
            pltpu.VMEM((ROWS, n_tm, FRAMES, strips * LANES), BF16),
            pltpu.VMEM((taps, cin), BF16),
            pltpu.VMEM((n_tm, strips, FIRST, FRAMES, LANES), BF16),
            pltpu.VMEM((n_tm, strips, SECOND, FRAMES, LANES), BF16),
            pltpu.VMEM((2, n_tm, 2, FRAMES, LANES), BF16),
            pltpu.VMEM((n_tile, FIRST, FRAMES, LANES), BF16),
            pltpu.VMEM((n_tile, SECOND, FRAMES, LANES), BF16),
            pltpu.VMEM((n_tile, 2, FRAMES, LANES), BF16),
            pltpu.VMEM((height // 2, FRAMES, LANES), BF16),
            pltpu.VMEM((height // 2, FRAMES, LANES), BF16),
            pltpu.VMEM((frames, count, cin), BF16),
            pltpu.VMEM((frames, count, cin), F32),
            pltpu.VMEM((height, 2 * FRAMES, LANES), F32),
            pltpu.VMEM((height, 2 * FRAMES, LANES), F32),
            pltpu.VMEM((WINDOW, (height + 2) * width, LANES), F32),
            pltpu.VMEM((wide, count, LANES), BF16),
            pltpu.VMEM((wide * LANES, count), BF16),
            pltpu.VMEM((frames, count, LANES), BF16),
            pltpu.VMEM((frames, 3 * OUT, count), BF16),
            pltpu.VMEM((padded, cin), BF16),
            pltpu.VMEM((27 * OUT, cin), F32),
            pltpu.VMEM((cin, padded), F32),
            pltpu.VMEM((rows, padded), F32),
            pltpu.VMEM((rows, padded), BF16),
            pltpu.VMEM((n_tile // CORES, share, padded), BF16),
            pltpu.VMEM((share, padded), F32),
            pltpu.VMEM((n_tm, share, padded), F32),
            pltpu.SemaphoreType.DMA((frames,)),
            pltpu.SemaphoreType.DMA((16,)),
        ],
        compiler_params=pltpu.CompilerParams(
            collective_id=0, has_side_effects=True, vmem_limit_bytes=VMEM_LIMIT
        ),
    )(banded, section_input, jnp.transpose(kernel))


VMEM_LIMIT = 53 << 20


def solution(mesh):
    n_tm, n_tile = mesh.shape["tm"], mesh.shape["tile"]
    positions = n_tm * FRAMES * n_tile * ROWS * n_tile * STRIP
    return jax.shard_map(
        functools.partial(on_device, n_tm, n_tile, 1.0 / math.sqrt(positions)),
        mesh=mesh,
        in_specs=(P(None, "tile", "tm"), P("tm", None, "tile", None), P()),
        out_specs=(P("tm", None, "tile", None), P("tile", None)),
        check_vma=False,
    )
```

```python
import functools
import math

import jax
import jax.numpy as jnp
from jax import lax
from jax.experimental import pallas as pl
from jax.experimental.pallas import tpu as pltpu
from jax.sharding import PartitionSpec as P

MESH = pl.DeviceIdType.MESH
F32, BF16 = jnp.float32, jnp.bfloat16
LANES = 128
OUT = 16
STRIP = 8
FRAMES = 8
ROWS = 5
FIRST = 4
SECOND = 3
EARLY = 4
CORES = 2
WINDOW = 3


def lane_of(shape, axis):
    return lax.broadcasted_iota(jnp.int32, shape, axis)


def aligned(index, size):
    return pl.ds(pl.multiple_of(index * size, size), size)


def turned(value, shift, axis):
    shift %= value.shape[axis]
    return pltpu.roll(value, shift, axis) if shift else value


def wrapped(index, size):
    return jnp.where(index >= size, index - size, index)


def strip_halo(left, right):
    lane = lane_of((1, LANES), 1)
    rows = []
    for i in range(ROWS):
        value = jnp.zeros((FRAMES, LANES), F32)
        if right is not None:
            value = jnp.where(lane >= LANES - OUT, right[i], value)
        if left is not None:
            value = jnp.where(lane < OUT, left[i], value)
        rows.append(turned(value, OUT + 2 * OUT * i, 1))
    return rows[0] + rows[1] + rows[2] + rows[3], rows[4]


def joined(upper, lower, turn_upper=False, turn_lower=False):
    upper = turned(upper, EARLY, 0) if turn_upper else upper
    lower = turned(lower, EARLY, 0) if turn_lower else lower
    return jnp.where(lane_of((FRAMES, 1), 0) < EARLY, upper, lower)


def whole(
    n_tm, n_tile, scale, grad_hbm, x_ref, kernel_hbm, out_ref, kgrad_ref,
    grad_ref, kernel_ref, msg, msg_2, emsg, recv, recv_2, edge, lead, ahead, act, slope, field, halo, vee, cols, cols_t, last, last_t,
    weights, acc, part, mine, mine_half, pieces, sums, quads, in_sem, sems,
):
    frames, height, width, cin = out_ref.shape
    wide, count = frames + 2, height * width
    tm, tile = lax.axis_index("tm"), lax.axis_index("tile")
    strips = n_tile // n_tm
    block = tile // strips
    place_in_block = lax.rem(tile, strips)
    from_left = jnp.logical_and(place_in_block == 0, block > 0)
    from_right = jnp.logical_and(place_in_block == strips - 1, block < n_tm - 1)
    has_edge = jnp.logical_or(from_left, from_right)
    edge_block = jnp.where(place_in_block == 0, block - 1, block + 1)
    messages = n_tm * strips
    send_main, send_edge, recv_main, recv_edge = (sems.at[i] for i in range(4))
    swap_send, swap_recv, piece_send, piece_recv = (sems.at[i] for i in range(4, 8))
    send_2, recv_main_2 = sems.at[10], sems.at[11]
    row_send, row_recv = sems.at[12], sems.at[13]
    lead_send, lead_recv = sems.at[14], sems.at[15]
    core, y_lo = lax.rem(tm, CORES), tm // CORES
    groups = n_tile // CORES
    y_hi, spot = tile // groups, lax.rem(tile, groups)
    partner = tm + 1 - 2 * core
    level = y_hi * CORES + y_lo
    owner_tile = core * groups + spot

    def is_me(target_tm, target_tile):
        return jnp.logical_and(target_tm == tm, target_tile == tile)

    grad_copy = pltpu.make_async_copy(grad_hbm, grad_ref, sems.at[8])
    kernel_copy = pltpu.make_async_copy(kernel_hbm, kernel_ref, sems.at[9])
    grad_copy.start()
    kernel_copy.start()

    def fetch(t):
        return pltpu.make_async_copy(x_ref.at[t], out_ref.at[t], in_sem.at[t])

    for t in range(frames):
        fetch(t).start()

    barrier = pltpu.get_barrier_semaphore()

    def hail(target_tm, target_tile):
        pl.semaphore_signal(barrier, inc=1, device_id=(target_tm, target_tile), device_id_type=MESH)

    for k in range(1, n_tile):
        hail(block, wrapped(tile + k, n_tile))

    @pl.when(block != tm)
    def _():
        hail(block, tile)

    @pl.when(has_edge)
    def _():
        for k in range(1, n_tile):
            hail(edge_block, wrapped(tile + k, n_tile))

        @pl.when(edge_block != tm)
        def _():
            hail(edge_block, tile)

    @pl.when(tm < n_tm - 1)
    def _():
        hail(tm + 1, tile)

    hail(partner, tile)
    for k in range(1, groups):
        hail(tm, y_hi * groups + wrapped(spot + k, groups))
    for k in range(n_tm):
        source = (k % CORES) * CORES + y_hi, (k // CORES) * groups + spot

        @pl.when(jnp.logical_not(is_me(*source)))
        def _():
            hail(*source)

    r, c = lane_of((LANES, LANES), 0), lane_of((LANES, LANES), 1)
    same = jnp.logical_and(r // OUT + c // OUT == STRIP - 1, lax.rem(r, OUT) == lax.rem(c, OUT))
    flip = jnp.where(same, 1.0, 0.0).astype(BF16)
    row = lane_of((FRAMES, 1), 0)
    nothing = jnp.zeros((FRAMES, LANES), F32)
    grad_copy.wait()
    rows = [grad_ref[:, t].astype(F32).reshape(ROWS * FRAMES, strips * LANES) for t in range(n_tm)]
    rows = jnp.concatenate(
        [rows[t][:, s * LANES : (s + 1) * LANES] for t in range(n_tm) for s in range(strips)], axis=0
    )
    rows = jnp.dot(rows.astype(BF16), flip, preferred_element_type=F32).reshape(n_tm, strips, ROWS, FRAMES, LANES)
    flipped, halos = [], []
    for t in range(n_tm):
        here = [rows[t, s] for s in range(strips)]
        flipped.append(here)
        padded = [None, None] + here + [None, None]
        halos.append([strip_halo(padded[s], padded[s + 2]) for s in range(strips + 2)])
    self_main = (block == tm).astype(jnp.int32)
    to_right, to_left = tm < n_tm - 1, tm > 0
    right_tile, left_tile = (tm + 1) * strips, tm * strips - 1
    self_edge = (
        jnp.logical_and(to_right, tile == right_tile).astype(jnp.int32)
        + jnp.logical_and(to_left, tile == left_tile).astype(jnp.int32)
    )
    edges_out = n_tm * (to_right.astype(jnp.int32) + to_left.astype(jnp.int32))
    self_owner = (core == y_hi).astype(jnp.int32)
    exchange_out = messages - self_main + edges_out - self_edge
    all_here = (exchange_out + 1 + groups - 1 + n_tm - self_owner + to_left.astype(jnp.int32))

    def send(source, target, send_sem, recv_sem, target_tm, target_tile):
        own = is_me(target_tm, target_tile)

        @pl.when(jnp.logical_not(own))
        def _():
            pltpu.make_async_remote_copy(
                src_ref=source, dst_ref=target, send_sem=send_sem, recv_sem=recv_sem,
                device_id=(target_tm, target_tile), device_id_type=MESH,
            ).start()

        @pl.when(own)
        def _():
            pltpu.make_async_copy(source, target, recv_sem).start()

    def send_block(source, target, send_sem, recv_sem, t):
        for k in range(strips):
            s = wrapped(place_in_block + k, strips)
            if k == 0:
                send(source.at[t, s], target.at[tile], send_sem, recv_sem, t, tm * strips + s)
            else:
                pltpu.make_async_remote_copy(
                    src_ref=source.at[t, s], dst_ref=target.at[tile], send_sem=send_sem, recv_sem=recv_sem,
                    device_id=(t, tm * strips + s), device_id_type=MESH,
                ).start()

    def make_block(t):
        for s in range(strips):
            here, (first, second) = flipped[t][s], halos[t][s + 1]
            tiles = [
                joined(here[0], here[1], False, True), joined(here[2], here[3], False, True),
                joined(here[4], first, False, True), joined(second, here[4]),
            ]
            for i, value in enumerate(tiles):
                msg[t, s, i] = value.astype(BF16)
        for side, s in ((0, strips + 1), (1, 0)):
            for i, value in enumerate(halos[t][s]):
                emsg[side, t, i] = value.astype(BF16)

    def leave_block(t):
        send_block(msg, recv, send_main, recv_main, t)

        @pl.when(to_right)
        def _():
            send(emsg.at[0, t], edge.at[tile], send_edge, recv_edge, t, right_tile)

        @pl.when(to_left)
        def _():
            send(emsg.at[1, t], edge.at[tile], send_edge, recv_edge, t, left_tile)

    ready = n_tm // 2
    for t in range(ready):
        make_block(t)
    pl.semaphore_wait(barrier, all_here)
    for t in range(n_tm):
        leave_block(t)
        if ready + t < n_tm:
            make_block(ready + t)

    for t in range(n_tm):
        for s in range(strips):
            here, (first, second) = flipped[t][s], halos[t][s + 1]
            tiles = [
                joined(here[0], here[1], True), joined(here[2], here[3], True), joined(first, second, True),
            ]
            for i, value in enumerate(tiles):
                msg_2[t, s, i] = value.astype(BF16)

    kernel_copy.wait()
    weights[...] = jnp.zeros(weights.shape, BF16)
    for kt in range(3):
        taps = kernel_ref[9 * kt * OUT : 9 * (kt + 1) * OUT, :]
        taps = (0.5 * taps.astype(F32)).astype(BF16)
        weights[kt * LANES : (kt + 1) * LANES, :] = taps[:LANES]
        weights[3 * LANES + kt * OUT : 3 * LANES + (kt + 1) * OUT, :] = taps[LANES:]

    step = 8

    def silu_frame(t, _):
        fetch(t).wait()

        def silu_rows(r, _):
            half_x = 0.5 * out_ref[t, pl.ds(r * step, step)].astype(F32).reshape(step * width, cin)
            u = jnp.tanh(half_x)
            more = 1.0 + u
            value = half_x * more
            rows = aligned(r, step * width)
            act[t, rows, :] = value.astype(BF16)
            slope[t, rows, :] = more + value * (1.0 - u)
            return 0

        lax.fori_loop(0, height // step, silu_rows, 0, unroll=10)
        return 0

    lax.fori_loop(0, EARLY, silu_frame, 0)
    for t in range(n_tm):
        send_block(msg_2, recv_2, send_2, recv_main_2, t)
    lax.fori_loop(EARLY, frames, silu_frame, 0)

    @pl.when(jnp.logical_not(has_edge))
    def _():
        edge[...] = jnp.zeros(edge.shape, BF16)

    @pl.when(has_edge)
    def _():
        pltpu.make_async_copy(edge, edge, recv_edge).wait()

    pltpu.make_async_copy(recv, recv, recv_main).wait()

    def beside(value, i):
        return turned(value, -OUT - 2 * OUT * i, 1)

    def unpack(b, _):
        tiles = [recv[b, i].astype(F32) for i in range(FIRST)]
        sides = turned(tiles[2], EARLY, 0) + edge[b, 0].astype(F32)
        for i in range(ROWS - 1):
            field[b * ROWS + i, 0:FRAMES] = turned(tiles[i // 2], EARLY * (i % 2), 0)
            halo[b * ROWS + i, 0:FRAMES] = beside(sides, i)
        field[b * ROWS + 4, 0:FRAMES] = joined(tiles[2], tiles[3])
        halo[b * ROWS + 4, 0:FRAMES] = beside(tiles[3] + edge[b, 1].astype(F32), 4)
        return 0

    def unpack_2(b, _):
        tiles = [recv_2[b, i].astype(F32) for i in range(SECOND)]
        sides = turned(tiles[2], EARLY, 0) + edge[b, 0].astype(F32)
        for i in range(ROWS - 1):
            field[b * ROWS + i, EARLY:FRAMES] = turned(tiles[i // 2], EARLY * (1 - i % 2), 0)[EARLY:]
            halo[b * ROWS + i, EARLY:FRAMES] = beside(sides, i)[EARLY:]
        halo[b * ROWS + 4, EARLY:FRAMES] = beside(tiles[2] + edge[b, 1].astype(F32), 4)[EARLY:]
        return 0

    lax.fori_loop(0, n_tile, unpack, 0, unroll=8)

    def pack_lead(k, _):
        both = [
            jnp.where(row < 2, field[2 * k + i, 0:FRAMES], turned(halo[2 * k + i, 0:FRAMES], 2, 0)) for i in range(2)
        ]
        lead[k] = joined(both[0], both[1], False, True).astype(BF16)
        return 0

    def unpack_ahead(k, _):
        tiles = ahead[k].astype(F32)
        for i in range(2):
            field[2 * k + i, FRAMES:] = turned(tiles, -4 * i, 0)
            halo[2 * k + i, FRAMES:] = turned(tiles, -4 * i - 2, 0)
        return 0

    lead_copy = pltpu.make_async_remote_copy(
        src_ref=lead, dst_ref=ahead, send_sem=lead_send, recv_sem=lead_recv,
        device_id=(jnp.maximum(tm - 1, 0), tile), device_id_type=MESH,
    )

    @pl.when(to_left)
    def _():
        lax.fori_loop(0, height // 2, pack_lead, 0, unroll=8)
        lead_copy.start()

    lane3, col3 = lane_of((1, width, LANES), 2), lane_of((1, width, LANES), 1)
    outside = jnp.logical_or(
        jnp.logical_and(col3 == 0, lane3 < OUT),
        jnp.logical_and(col3 == width - 1, lane3 >= LANES - OUT),
    )
    edge_rows = jnp.zeros((width, LANES), F32)
    group = 16
    for t in range(WINDOW):
        vee[t, 0:width, :] = edge_rows
        vee[t, (height + 1) * width : (height + 2) * width, :] = edge_rows

    lane2 = lane_of((1, LANES), 1)

    def tap(t, g, shift_rows, shift):
        at = pl.ds(pl.multiple_of((g * group + shift_rows) * width, width), group * width)
        return turned(vee[t % WINDOW, at, :].astype(BF16), shift, 1)

    acc[...] = jnp.zeros(acc.shape, F32)

    def add_frame(t):
        left = jnp.concatenate([cols_t[t * LANES : (t + 3) * LANES, :], last_t[t]], axis=0)
        for i in range(2):
            some = slice(i * (count // 2), (i + 1) * (count // 2))
            acc[...] += jnp.dot(left[:, some], act[t, some, :], preferred_element_type=F32)

    for t in range(wide):
        if t == EARLY:
            pltpu.make_async_copy(recv_2, recv_2, recv_main_2).wait()
            lax.fori_loop(0, n_tile, unpack_2, 0, unroll=8)
        if t == FRAMES:
            @pl.when(to_right)
            def _():
                pltpu.make_async_copy(ahead, ahead, lead_recv).wait()

            @pl.when(jnp.logical_not(to_right))
            def _():
                ahead[...] = jnp.zeros(ahead.shape, BF16)

            lax.fori_loop(0, height // 2, unpack_ahead, 0, unroll=8)

        def spread(g, _, t=t):
            rows = pl.ds(g * group, group)
            main = jnp.broadcast_to(field[rows, t : t + 1, :], (group, width, LANES))
            side = jnp.broadcast_to(halo[rows, t : t + 1, :], (group, width, LANES))
            at = pl.ds(pl.multiple_of((g * group + 1) * width, width), group * width)
            values = jnp.where(outside, side, main).reshape(group * width, LANES)
            vee[t % WINDOW, at, :] = pltpu.roll(values, 0, 1, stride=OUT, stride_axis=0)
            return 0

        def fill(g, _, t=t):
            rows = aligned(g, group * width)
            s0, s1, s2 = tap(t, g, 2, 2 * OUT), tap(t, g, 1, 5 * OUT), tap(t, g, 0, 0)
            cols[t, rows, :] = jnp.where(lane2 < 3 * OUT, s0, jnp.where(lane2 < 6 * OUT, s1, s2))
            return 0

        def fill_last(g, _, t=t):
            rows = aligned(g, group * width)
            taps = [tap(t - 2 + kt, g, 0, kt * OUT) for kt in range(3)]
            value = jnp.where(lane2 < 3 * OUT, taps[2], jnp.zeros_like(taps[2]))
            last[t - 2, rows, :] = jnp.where(lane2 < OUT, taps[0], jnp.where(lane2 < 2 * OUT, taps[1], value))
            return 0

        lax.fori_loop(0, height // group, spread, 0, unroll=True)
        lax.fori_loop(0, height // group, fill, 0, unroll=True)
        cols_t[t * LANES : (t + 1) * LANES, :] = jnp.transpose(cols[t])
        if t >= 2:
            lax.fori_loop(0, height // group, fill_last, 0, unroll=True)
            last_t[t - 2] = jnp.transpose(last[t - 2])[0 : 3 * OUT]
        if t >= 3:
            add_frame(t - 3)
    add_frame(frames - 1)

    pieces_of_total = []
    for kt in range(3):
        pieces_of_total.append(acc[kt * LANES : (kt + 1) * LANES, :])
        pieces_of_total.append(acc[3 * LANES + kt * OUT : 3 * LANES + (kt + 1) * OUT, :])
    pieces_of_total.append(jnp.zeros((part.shape[1] - 27 * OUT, cin), F32))
    part[...] = jnp.transpose(jnp.concatenate(pieces_of_total, axis=0))

    chunk = 40

    def grad_frame(t, _):
        def grad_rows(r, _):
            rows = aligned(r, chunk * width)
            left = jnp.concatenate([cols[t + kt, rows, :] for kt in range(3)] + [last[t, rows, :]], axis=1)
            grad = jnp.dot(left, weights[...], preferred_element_type=F32) * slope[t, rows, :]
            out_ref[t, pl.ds(r * chunk, chunk)] = grad.reshape(chunk, width, cin).astype(BF16)
            return 0

        lax.fori_loop(0, height // chunk, grad_rows, 0, unroll=True)
        return 0

    def drain(source, sem):
        pltpu.make_async_copy(source, source, sem).wait()

    def drain_messages(source, sem):
        if n_tm > 1:
            drain(source.at[pl.ds(0, n_tm - 1)], sem)
        if strips > 1:
            drain(source.at[0, pl.ds(0, strips - 1)], sem)

        @pl.when(block != tm)
        def _():
            drain(source.at[0, 0], sem)

    drain_messages(msg, send_main)
    drain_messages(msg_2, send_2)

    def drain_edge(k, _):
        drain(emsg.at[0, 0], send_edge)
        return 0

    lax.fori_loop(0, edges_out - self_edge, drain_edge, 0)

    @pl.when(to_left)
    def _():
        drain(lead, lead_send)

    rows = mine.shape[0]
    share = rows // groups
    swap = pltpu.make_async_remote_copy(
        src_ref=part.at[aligned(1 - core, rows)], dst_ref=mine,
        send_sem=swap_send, recv_sem=swap_recv,
        device_id=(partner, tile), device_id_type=MESH,
    )
    swap.start()
    lax.fori_loop(0, SPLIT[0], grad_frame, 0)
    swap.wait()
    mine[...] += part[aligned(core, rows), :]

    mine_half[...] = mine[...].astype(BF16)

    for k in range(1, groups):
        g = wrapped(spot + k, groups)
        pltpu.make_async_remote_copy(
            src_ref=mine_half.at[aligned(g, share)], dst_ref=pieces.at[spot],
            send_sem=piece_send, recv_sem=piece_recv,
            device_id=(tm, y_hi * groups + g), device_id_type=MESH,
        ).start()
    pieces[spot] = mine_half[aligned(spot, share), :]
    lax.fori_loop(SPLIT[0], SPLIT[1], grad_frame, 0)
    others = pieces.at[pl.ds(0, groups - 1)]
    pltpu.make_async_copy(others, others, piece_recv).wait()
    sums[...] = jnp.sum(pieces[...].astype(F32), axis=0)

    for k in range(n_tm):
        send(sums, quads.at[level], row_send, row_recv, k, owner_tile)
    lax.fori_loop(SPLIT[1], frames, grad_frame, 0)
    pltpu.make_async_copy(quads, quads, row_recv).wait()

    drain(others, piece_send)
    drain(quads.at[pl.ds(0, n_tm - 1)], row_send)

    @pl.when(core != y_hi)
    def _():
        drain(sums, row_send)

    result = quads[0]
    for k in range(1, n_tm):
        result = result + quads[k]
    kgrad_ref[...] = (result * scale)[:, : kgrad_ref.shape[1]]


SPLIT = (1, 6)


def on_device(n_tm, n_tile, scale, latent_grad, section_input, kernel):
    frames, height, width, cin = section_input.shape
    taps = kernel.shape[1]
    strips = n_tile // n_tm
    banded = jnp.transpose(latent_grad, (1, 0, 2)).reshape(ROWS, n_tm, FRAMES, strips * LANES)
    wide, count = frames + 2, height * width
    rows, share, padded = cin // CORES, cin // n_tile, 4 * LANES
    vmem = pl.BlockSpec(memory_space=pltpu.VMEM)
    return pl.pallas_call(
        functools.partial(whole, n_tm, n_tile, scale),
        out_shape=(
            pltpu.VMEM((frames, height, width, cin), BF16),
            pltpu.VMEM((share, taps), F32),
        ),
        in_specs=[pl.BlockSpec(memory_space=pl.ANY)] * 3,
        out_specs=(vmem, vmem),
        scratch_shapes=[
            pltpu.VMEM((ROWS, n_tm, FRAMES, strips * LANES), BF16),
            pltpu.VMEM((taps, cin), BF16),
            pltpu.VMEM((n_tm, strips, FIRST, FRAMES, LANES), BF16),
            pltpu.VMEM((n_tm, strips, SECOND, FRAMES, LANES), BF16),
            pltpu.VMEM((2, n_tm, 2, FRAMES, LANES), BF16),
            pltpu.VMEM((n_tile, FIRST, FRAMES, LANES), BF16),
            pltpu.VMEM((n_tile, SECOND, FRAMES, LANES), BF16),
            pltpu.VMEM((n_tile, 2, FRAMES, LANES), BF16),
            pltpu.VMEM((height // 2, FRAMES, LANES), BF16),
            pltpu.VMEM((height // 2, FRAMES, LANES), BF16),
            pltpu.VMEM((frames, count, cin), BF16),
            pltpu.VMEM((frames, count, cin), F32),
            pltpu.VMEM((height, 2 * FRAMES, LANES), F32),
            pltpu.VMEM((height, 2 * FRAMES, LANES), F32),
            pltpu.VMEM((WINDOW, (height + 2) * width, LANES), F32),
            pltpu.VMEM((wide, count, LANES), BF16),
            pltpu.VMEM((wide * LANES, count), BF16),
            pltpu.VMEM((frames, count, LANES), BF16),
            pltpu.VMEM((frames, 3 * OUT, count), BF16),
            pltpu.VMEM((padded, cin), BF16),
            pltpu.VMEM((27 * OUT, cin), F32),
            pltpu.VMEM((cin, padded), F32),
            pltpu.VMEM((rows, padded), F32),
            pltpu.VMEM((rows, padded), BF16),
            pltpu.VMEM((n_tile // CORES, share, padded), BF16),
            pltpu.VMEM((share, padded), F32),
            pltpu.VMEM((n_tm, share, padded), F32),
            pltpu.SemaphoreType.DMA((frames,)),
            pltpu.SemaphoreType.DMA((16,)),
        ],
        compiler_params=pltpu.CompilerParams(
            collective_id=0, has_side_effects=True, vmem_limit_bytes=VMEM_LIMIT
        ),
    )(banded, section_input, jnp.transpose(kernel))


VMEM_LIMIT = 53 << 20


def solution(mesh):
    n_tm, n_tile = mesh.shape["tm"], mesh.shape["tile"]
    positions = n_tm * FRAMES * n_tile * ROWS * n_tile * STRIP
    return jax.shard_map(
        functools.partial(on_device, n_tm, n_tile, 1.0 / math.sqrt(positions)),
        mesh=mesh,
        in_specs=(P(None, "tile", "tm"), P("tm", None, "tile", None), P()),
        out_specs=(P("tm", None, "tile", None), P("tile", None)),
        check_vma=False,
    )
```
